128 devices in a mesh: section: 2 (over core), dp: 64 (over y, x, z).
Axes of the slice: x: 4, y: 4, z: 4, core: 2. Of those that a mesh axis runs over, the one named last changes fastest.
Arguments:
- window_input: bfloat16 [2, 64, 64, 1536], P(None, 'dp'), may hold values from -6 to 6
- cotangent: bfloat16 [2, 64, 64, 1536], P(None, 'dp'), may hold values from -6 to 6
- lengths: int32 [2, 64], P(None, 'dp'), may hold values from 1 to 64, as said below
- widths: int32 [2], replicated, may hold values from 768 to 6144, as said below
- gain_first: bfloat16 [2, 1536], P('section', 'dp'), may hold values from 0.5 to 1.5
- shift_first: bfloat16 [2, 1536], P('section', 'dp'), may hold values from -4 to 4
- project_weight: bfloat16 [2, 1536, 4608], P('section', 'dp'), may hold values from -0.15625 to 0.15625
- project_bias: bfloat16 [2, 4608], P('section', 'dp'), may hold values from -6 to 6
- output_weight: bfloat16 [2, 1536, 1536], P('section', 'dp'), may hold values from -0.625 to 0.625
- output_bias: bfloat16 [2, 1536], P('section', 'dp'), may hold values from -6 to 6
- gain_second: bfloat16 [2, 1536], P('section', 'dp'), may hold values from 0.5 to 1.5
- shift_second: bfloat16 [2, 1536], P('section', 'dp'), may hold values from -4 to 4
- expand_weight: bfloat16 [2, 1536, 6144], P('section', 'dp'), may hold values from -0.15625 to 0.15625
- expand_bias: bfloat16 [2, 6144], P('section', 'dp'), may hold values from -6 to 6
- shrink_weight: bfloat16 [2, 6144, 1536], P('section', 'dp'), may hold values from -0.15625 to 0.15625
- shrink_bias: bfloat16 [2, 1536], P('section', 'dp'), may hold values from -4 to 4
Outputs:
- activations: bfloat16 [2, 2, 64, 64, 1536], P('section', None, 'dp')
- input_grads: bfloat16 [2, 2, 64, 64, 1536], P('section', None, 'dp')
- grad_gain_first: float32 [2, 1536], P('section', 'dp')
- grad_shift_first: float32 [2, 1536], P('section', 'dp')
- grad_project_weight: float32 [2, 1536, 4608], P('section', 'dp')
- grad_project_bias: float32 [2, 4608], P('section', 'dp')
- grad_output_weight: float32 [2, 1536, 1536], P('section', 'dp')
- grad_output_bias: float32 [2, 1536], P('section', 'dp')
- grad_gain_second: float32 [2, 1536], P('section', 'dp')
- grad_shift_second: float32 [2, 1536], P('section', 'dp')
- grad_expand_weight: float32 [2, 1536, 6144], P('section', 'dp')
- grad_expand_bias: float32 [2, 6144], P('section', 'dp')
- grad_shrink_weight: float32 [2, 6144, 1536], P('section', 'dp')
- grad_shrink_bias: float32 [2, 1536], P('section', 'dp')
The draws below stay inside these ranges and needn't reach their ends.
Inputs may be any that keep to these rules, and one draw needn't show every extreme that they name: `lengths`: in each micro-batch some sequence has all 64 tokens. `widths`: each is 6144, 3072, 1536 or 768; some micro-batch has 6144.
All inputs are finite; a program needn't handle non-finite values.
Results may differ from the reference program's by a relative error of at most 0.018.
Values may be sent and summed in bfloat16 or wider, within the bound.
A program may use at most 384 MiB of HBM per device.

```python
import jax
import jax.numpy as jnp
from jax import lax

HEADS = 12
HEAD_DIM = 128
FF = 6144
D = 1536
MICRO = 2
SEQ_LEN = 64
SEQS_ALL = 64


def draw_lengths(key, part):
    key = jax.random.fold_in(key, 11)
    key_one, key_two, key_three = jax.random.split(key, 3)
    factor_one = jax.random.randint(key_one, (MICRO, SEQS_ALL), 0, SEQ_LEN, dtype=jnp.int32)
    factor_two = jax.random.randint(key_two, (MICRO, SEQS_ALL), 0, SEQ_LEN, dtype=jnp.int32)
    drawn = SEQ_LEN - factor_one * factor_two // SEQ_LEN
    longest_at = jax.random.randint(key_three, (MICRO, 1), 0, SEQS_ALL, dtype=jnp.int32)
    column = jnp.arange(SEQS_ALL, dtype=jnp.int32)[None, :]
    return jnp.where(column == longest_at, SEQ_LEN, drawn).astype(jnp.int32)


def draw_widths(key, part):
    key = jax.random.fold_in(key, 23)
    key_level, key_full = jax.random.split(key)
    level = jax.random.randint(key_level, (MICRO,), 1, 4, dtype=jnp.int32)
    full_at = jax.random.randint(key_full, (), 0, MICRO, dtype=jnp.int32)
    level = jnp.where(jnp.arange(MICRO, dtype=jnp.int32) == full_at, 0, level)
    return (FF // jnp.left_shift(jnp.ones_like(level), level)).astype(jnp.int32)


def block_levels(key, extent, cuts, low, top_value):
    level = 1.0
    for axis_at, parts in cuts:
        draws = jax.random.uniform(jax.random.fold_in(jax.random.fold_in(key, 6), axis_at), (parts,), jnp.float32, low / len(cuts), top_value / len(cuts))
        level = level * jnp.repeat(jnp.exp(draws), extent[axis_at] // parts).reshape((-1,) + (1,) * (len(extent) - 1 - axis_at))
    return level


def normal_values(stream_key, extent, width, limit, shards=(), kind=jnp.bfloat16):
    entries = width * jax.random.normal(stream_key, extent, jnp.float32)
    if shards:
        entries = entries * block_levels(stream_key, extent, shards, -0.22, 0.18)
    return jnp.clip(entries, -limit, limit).astype(kind)


def setup_inputs(seed: int = 0) -> dict:
    splits = jax.random.split(jax.random.key(seed), 17)
    return {
        "window_input": normal_values(splits[0], (MICRO, SEQS_ALL, SEQ_LEN, D), 1.0, 6.0, ((1, 64),)),
        "cotangent": normal_values(splits[1], (MICRO, SEQS_ALL, SEQ_LEN, D), 1.0, 6.0, ((1, 64),)),
        "lengths": draw_lengths(jax.random.fold_in(splits[16], 71), 0),
        "widths": draw_widths(jax.random.fold_in(splits[16], 71), 0),
        "gain_first": jnp.clip(1.0 + 0.1 * jax.random.normal(splits[4], (2, D), jnp.float32), 0.5, 1.5).astype(jnp.bfloat16),
        "shift_first": normal_values(splits[5], (2, D), 0.3, 4.0, ((0, 2), (1, 64))),
        "project_weight": normal_values(splits[6], (2, D, 3 * D), D ** -0.5, 0.15625, ((0, 2), (1, 64))),
        "project_bias": normal_values(splits[7], (2, 3 * D), 0.5, 6.0, ((0, 2), (1, 64))),
        "output_weight": normal_values(splits[8], (2, D, D), (D // 16) ** -0.5, 0.625, ((0, 2), (1, 64))),
        "output_bias": normal_values(splits[9], (2, D), 0.5, 6.0, ((0, 2), (1, 64))),
        "gain_second": jnp.clip(1.0 + 0.1 * jax.random.normal(splits[10], (2, D), jnp.float32), 0.5, 1.5).astype(jnp.bfloat16),
        "shift_second": normal_values(splits[11], (2, D), 0.3, 4.0, ((0, 2), (1, 64))),
        "expand_weight": normal_values(splits[12], (2, D, FF), D ** -0.5, 0.15625, ((0, 2), (1, 64))),
        "expand_bias": normal_values(splits[13], (2, FF), 0.5, 6.0, ((0, 2), (1, 64))),
        "shrink_weight": normal_values(splits[14], (2, FF, D), (FF // 4) ** -0.5, 0.15625, ((0, 2), (1, 64))),
        "shrink_bias": normal_values(splits[15], (2, D), 0.3, 4.0, ((0, 2), (1, 64))),
    }


@jax.custom_vjp
def low(v):
    return lax.optimization_barrier(v.astype(jnp.bfloat16)).astype(jnp.float32)

@jax.custom_vjp
def low_back(v):
    return v

def low_keep(v):
    return (low(v), None)

def low_pass(kept, grad):
    return (grad,)

def back_keep(v):
    return (v, None)

def back_low(kept, grad):
    return (low(grad),)
low.defvjp(low_keep, low_pass)
low_back.defvjp(back_keep, back_low)
EPS = 1e-05
MASKED = -1000000000.0
HIGH = lax.Precision.HIGHEST

def norm_rows(values, norm_gain, norm_shift):
    row_mean = lax.optimization_barrier(jnp.mean(values, axis=-1, keepdims=True))
    centred = values - row_mean
    row_var = lax.optimization_barrier(jnp.mean(centred * centred, axis=-1, keepdims=True))
    return centred * lax.rsqrt(row_var + EPS) * norm_gain + norm_shift

def rotary_tables(seq_count, head_width):
    half_width = head_width // 2
    inverse_rates = 10000.0 ** (-jnp.arange(half_width, dtype=jnp.float32) / half_width)
    angles = jnp.arange(seq_count, dtype=jnp.float32)[:, None] * inverse_rates[None, :]
    return (jnp.cos(angles)[:, None, :], jnp.sin(angles)[:, None, :])

def rotate(vectors, cosine_table, sine_table):
    half_width = vectors.shape[-1] // 2
    front_half = vectors[..., :half_width]
    back_half = vectors[..., half_width:]
    return jnp.concatenate([front_half * cosine_table - back_half * sine_table, back_half * cosine_table + front_half * sine_table], axis=-1)

def one_layer(params, hidden, seq_length, prefix_width):
    gain_first, shift_first, project_weight, project_bias, output_weight, output_bias, gain_second, shift_second, expand_weight, expand_bias, shrink_weight, shrink_bias = params
    seq_count = hidden.shape[0]
    normed = low(norm_rows(hidden, gain_first, shift_first))
    joined = low_back(jnp.dot(normed, project_weight, precision=HIGH) + project_bias)
    joined = joined.reshape(seq_count, 3, HEADS, HEAD_DIM)
    cosine_table, sine_table = rotary_tables(seq_count, HEAD_DIM)
    queries = low(rotate(joined[:, 0], cosine_table, sine_table))
    keys_turned = low(rotate(joined[:, 1], cosine_table, sine_table))
    values = low(joined[:, 2])
    scores = jnp.einsum('qhd,khd->hqk', queries, keys_turned, precision=HIGH) * HEAD_DIM ** (-0.5)
    scores = low_back(scores)
    positions = jnp.arange(seq_count)
    visible = (positions[None, :] <= positions[:, None]) & (positions[None, :] < seq_length)
    scores = jnp.where(visible[None], scores, MASKED)
    row_top = lax.optimization_barrier(jnp.max(scores, axis=-1, keepdims=True))
    exp_terms = jnp.exp(scores - row_top)
    attention = exp_terms / lax.optimization_barrier(jnp.sum(exp_terms, axis=-1, keepdims=True))
    mixed_heads = jnp.einsum('hqk,khd->qhd', low(attention), values, precision=HIGH)
    mixed_heads = low(low_back(mixed_heads.reshape(seq_count, HEADS * HEAD_DIM)))
    branch = low_back(jnp.dot(mixed_heads, output_weight, precision=HIGH) + output_bias)
    middle = hidden + branch
    normed_second = low(norm_rows(middle, gain_second, shift_second))
    upper_units = low_back(jnp.dot(normed_second, expand_weight, precision=HIGH) + expand_bias)
    unit_mask = (jnp.arange(FF) < prefix_width).astype(jnp.float32)
    active = low(jax.nn.gelu(upper_units, approximate=True) * unit_mask)
    result = middle + jnp.dot(active, shrink_weight, precision=HIGH) + shrink_bias
    live_rows = (positions < seq_length).astype(jnp.float32)[:, None]
    return result * live_rows

def reference(window_input, cotangent, lengths, widths, gain_first, shift_first, project_weight, project_bias, output_weight, output_bias, gain_second, shift_second, expand_weight, expand_bias, shrink_weight, shrink_bias):
    stacked = tuple((weight.astype(jnp.float32) for weight in (gain_first, shift_first, project_weight, project_bias, output_weight, output_bias, gain_second, shift_second, expand_weight, expand_bias, shrink_weight, shrink_bias)))
    inputs = window_input.astype(jnp.float32).reshape(MICRO * SEQS_ALL, SEQ_LEN, D)
    seq_lengths = lengths.reshape(MICRO * SEQS_ALL)
    prefixes = jnp.repeat(widths, SEQS_ALL)
    bridge = jnp.zeros((MICRO * SEQS_ALL, SEQ_LEN, D), jnp.float32)
    run_layer = jax.vmap(one_layer, in_axes=(None, 0, 0, 0))

    def forward(inputs, stacked, bridge):
        first_params = tuple((weight[0] for weight in stacked))
        second_params = tuple((weight[1] for weight in stacked))
        first_out = run_layer(first_params, inputs, seq_lengths, prefixes)
        first_out = low_back(low(first_out)) + bridge
        second_out = run_layer(second_params, first_out, seq_lengths, prefixes)
        return (first_out, second_out)
    (first_out, second_out), pullback = jax.vjp(forward, inputs, stacked, bridge)
    cot_rows = cotangent.astype(jnp.float32).reshape(MICRO * SEQS_ALL, SEQ_LEN, D)
    grad_inputs, grad_stacked, grad_bridge = pullback((jnp.zeros_like(first_out), cot_rows))
    activations = jnp.stack([first_out, second_out]).reshape(2, MICRO, SEQS_ALL, SEQ_LEN, D).astype(jnp.bfloat16)
    input_grads = jnp.stack([grad_inputs, grad_bridge]).reshape(2, MICRO, SEQS_ALL, SEQ_LEN, D).astype(jnp.bfloat16)
    return (activations, input_grads, grad_stacked[0], grad_stacked[1], grad_stacked[2], grad_stacked[3], grad_stacked[4], grad_stacked[5], grad_stacked[6], grad_stacked[7], grad_stacked[8], grad_stacked[9], grad_stacked[10], grad_stacked[11])
```

```python
import jax
import jax.numpy as jnp
import numpy as np
from jax import lax
from jax.experimental import pallas as pl
from jax.experimental.pallas import tpu as pltpu
from jax.sharding import PartitionSpec as P

MESH = pl.DeviceIdType.MESH
ANY = pl.BlockSpec(memory_space=pl.ANY)
VM = pl.BlockSpec(memory_space=pltpu.VMEM)
EPS = 1e-05
MASKED = -1e9
BF = jnp.bfloat16
F32 = jnp.float32
D = 1536
T = 64
TG = 256
HW = 384
QW = 1152
SCALE = 128 ** -0.5
GC = (2 / np.pi) ** 0.5
PR, OU, EX, SH = range(4)
FULL = ((D, QW), (HW, D), (D, D), (D, D))
SLAB = ((48, QW), (48, HW), (48, D), (96, 768))


def nn(a, b):
    return jnp.dot(a, b, preferred_element_type=F32)


def nt(a, b):
    return lax.dot_general(a, b, (((1,), (1,)), ((), ())), preferred_element_type=F32)


def tn(a, b):
    return lax.dot_general(a, b, (((0,), (0,)), ((), ())), preferred_element_type=F32)


def tiles(count, body):
    def step(i, carry):
        body(i)
        return carry
    lax.fori_loop(0, count, step, 0)


def span(i, size):
    return pl.ds(pl.multiple_of(i * size, size), size)


def at(start, size, unit):
    return pl.ds(pl.multiple_of(start, unit), size)


def stats(x):
    mean = jnp.mean(x, axis=-1, keepdims=True)
    c = x - mean
    var = jnp.mean(c * c, axis=-1, keepdims=True)
    rs = lax.rsqrt(var + EPS)
    return c * rs, rs


def colsum(v):
    return jnp.sum(v, axis=0, keepdims=True)


def to32(v):
    v = v.astype(F32)
    return jnp.concatenate([v, jnp.zeros((8, v.shape[1]), F32)], axis=0).astype(BF)


def core_kernel(h_ref, cot_ref, len_ref, mask_ref, pack_ref, cos_ref, sin_ref, pw, ow, ew, sw,
                act_out, ig_out, sm_out, fp, fo, fe, fs,
                wp, wo, we, ws, r0p, r0o, r0e, r0s, r1p, r1o, r1e, r1s, r2p, r2o, r2e, r2s,
                vp, vo, ve, vs, up, uo, ue, us_,
                normed, ns, gall, dball, qkv, probs, mixed, gder, active, xh1, xh2, rd1, rd2,
                pf, sb, rb, dup, dj, dmix, vis, lens, keep, ostage,
                sp, so, se, cp, co, ce, cs, bp, bo, be, fss,
                tmp, allp, small, smt, sme,
                y_s, y_r, w_sem, x_s, x_r, l_s, l_r, z_s, zo_s, z_r, zs_r, p_s, p_r,
                a_s, a_r, b_s, b_r, c_s, c_r, o_sem, q0_s, q0_r, q1_s, q1_r, q2_s, q2_r, t_sem,
                f_s, f_r, e_s, e_r):
    s = lax.axis_index("section")
    chip = lax.axis_index("dp")
    y, x, z = chip // 16, (chip // 4) % 4, chip % 4
    t = y
    zp = z % 2
    zh = z // 2
    first = s == 0

    def dev(core, cy, cx, cz):
        return (core, cy * 16 + cx * 4 + cz)

    def ypeer(d):
        return dev(s, (y + d) % 4, x, z)

    a_me = jnp.where(first, x, z)
    b_me = jnp.where(first, z, x)

    def grid(a, b):
        return jnp.where(first, a, b), jnp.where(first, b, a)

    def apeer(d):
        cx, cz = grid((a_me + d) % 4, b_me)
        return dev(s, y, cx, cz)

    def bpeer(d):
        cx, cz = grid(a_me, (b_me + d) % 4)
        return dev(s, y, cx, cz)

    sib = dev(1 - s, y, x, z)
    own = at(t * T, T, T)

    bar = pltpu.get_barrier_semaphore()

    def greet(who):
        pl.semaphore_signal(bar, inc=1, device_id=who, device_id_type=MESH)

    for d in (1, 2, 3):
        for core in (s, 1 - s):
            greet(dev(core, (y + d) % 4, x, z))
    for d in (0, 1, 2, 3):
        for core in (s, 1 - s):
            greet(dev(core, (y + d) % 4, x, 2 * zh + 1 - zp))
    greet(sib)
    for d in (1, 2, 3):
        greet(dev(s, y, (x + d) % 4, z))
    for d in (0, 1):
        greet(dev(s, y, x, 2 * (1 - zh) + d))
    pl.semaphore_wait(bar, 20)

    def remote(src, dst, ssem, rsem, who):
        return pltpu.make_async_remote_copy(src_ref=src, dst_ref=dst, send_sem=ssem, recv_sem=rsem,
                                            device_id=who, device_id_type=MESH)

    def wait_for(ref, sem):
        pltpu.make_async_copy(ref, ref, sem).wait()

    w_hbm = (wp, wo, we, ws)
    w_v = (vp, vo, ve, vs)
    g_v = (up, uo, ue, us_)
    r0 = (r0p, r0o, r0e, r0s)
    r1 = (r1p, r1o, r1e, r1s)
    r2 = (r2p, r2o, r2e, r2s)

    def slab_at(k, j, cx, cz):
        if k in (PR, EX):
            return at(48 * (8 * (2 * (cz % 2) + j) + 2 * cx + cz // 2), 48, 48), slice(None)
        if k == OU:
            return at(48 * (2 * cx + cz // 2), 48, 48), at(HW * (2 * (cz % 2) + j), HW, HW)
        return at(96 * (4 * cx + cz), 96, 96), at(768 * j, 768, 768)

    def slab_of(ref, k, a, b):
        cx, cz = grid(a, b)
        return ref.at[slab_at(k, s, cx, cz)]

    def parts_of(ref, k, j):
        if k in (PR, EX):
            return [ref.at[at(HW * (2 * p + j), HW, HW)] for p in (0, 1)]
        if k == OU:
            return [ref.at[:, at(HW * (2 * p + j), HW, HW)] for p in (0, 1)]
        return [ref.at[:, at(768 * j, 768, 768)]]

    def bulk(ref, k, slabs):
        if k in (PR, EX):
            return ref.at[pl.ds(0, 48 * slabs)]
        if k == OU:
            return ref.at[pl.ds(0, 12 * slabs)] if slabs > 3 else ref.at[pl.ds(0, 144), pl.ds(0, HW)]
        return ref.at[pl.ds(0, 48 * slabs)]

    def piece_target(yt):
        return dev(y % 2, yt, x, 2 * zh + y // 2), (yt == y) & (s == y % 2) & (zp == y // 2)

    def out_target(q):
        return dev(q % 2, y, x, 2 * zh + q // 2), (zp == q // 2) & (s == q % 2)

    def send_or_keep(src, dst, ssem, rsem, who, is_me):
        @pl.when(is_me)
        def _():
            pltpu.make_async_copy(src, dst, rsem).start()

        @pl.when(jnp.logical_not(is_me))
        def _():
            remote(src, dst, ssem, rsem, who).start()

    def sent(src, dst, ssem, rsem, who, is_me):
        @pl.when(jnp.logical_not(is_me))
        def _():
            remote(src, dst, ssem, rsem, who).wait_send()

    def shard_moves():
        out = []
        for yt in range(4):
            who, me = piece_target(yt)
            out.append((sp.at[yt], cp.at[s, zp], z_s.at[0, yt], z_r.at[0, s, zp], who, me))
        for q in range(4):
            who, me = out_target(q)
            out.append((so.at[q], co.at[s, zp], z_s.at[1, q], z_r.at[1, s, zp], who, me))
        for yt in range(4):
            who, me = piece_target(yt)
            out.append((se.at[yt], ce.at[s, zp], z_s.at[2, yt], z_r.at[2, s, zp], who, me))
        for j in range(2):
            out.append((sw.at[0, :, pl.ds(768 * j, 768)], cs.at[s], zo_s.at[j], zs_r.at[s],
                        dev(j, y, x, z), s == j))
        return out

    moves = shard_moves()
    for yt in range(4):
        sp[yt] = to32(jnp.concatenate([pw[0, :, p * D + HW * yt:p * D + HW * (yt + 1)] for p in range(3)], axis=1))
    for m in moves[:4]:
        send_or_keep(*m)
    for q in range(4):
        so[q] = to32(ow[0, :, HW * q:HW * (q + 1)])
    for m in moves[4:8]:
        send_or_keep(*m)
    for yt in range(4):
        se[yt] = to32(ew[0, :, D * yt:D * (yt + 1)])
    for m in moves[8:]:
        send_or_keep(*m)

    allp[s, pl.ds(chip, 1)] = pack_ref[...][None]

    def pack_copies(stage):
        out = []
        for d in (1, 2, 3):
            if stage == 0:
                blk, who = allp.at[s, pl.ds(chip, 1)], dev(s, y, x, (z + d) % 4)
            elif stage == 1:
                blk, who = allp.at[s, at(chip - z, 4, 4)], dev(s, y, (x + d) % 4, z)
            else:
                blk, who = allp.at[s, at(16 * y, 16, 16)], ypeer(d)
            out.append(remote(blk, blk, p_s.at[stage, d - 1], p_r.at[stage, d - 1], who))
        return out

    def pack_go(stage):
        for c in pack_copies(stage):
            c.start()

    def pack_end(stage):
        for c in pack_copies(stage):
            c.wait()

    pack_go(0)

    lens[pl.ds(t, 1)] = len_ref[...][None]
    lcs = []
    for d in (1, 2, 3):
        c = remote(lens.at[pl.ds(t, 1)], lens.at[pl.ds(t, 1)], l_s.at[d - 1], l_r.at[d - 1], ypeer(d))
        c.start()
        lcs.append(c)

    got = (cp, co, ce, cs)
    bld = (bp, bo, be, cs)

    def a_copies(l, k):
        src = bld[k].at[l]
        return [remote(src, slab_of(w_hbm[k].at[l], k, a_me, b_me), a_s.at[l, k], a_r.at[l, k], apeer(d))
                for d in (1, 2, 3)]

    def own_copy(l, k):
        return pltpu.make_async_copy(bld[k].at[l], slab_of(w_hbm[k].at[l], k, a_me, b_me), o_sem.at[l, k])

    def gather_a(l, k):
        if k == SH:
            wait_for(cs.at[l], zs_r.at[l])
        else:
            zk = (0, 1, 2)[k]
            for p in (0, 1):
                wait_for(got[k].at[l, p], z_r.at[zk, l, p])
            halves = [got[k][l, p].astype(F32)[:24] for p in (0, 1)]
            bld[k][l] = jnp.concatenate(halves, axis=0).astype(BF)
        for c in a_copies(l, k):
            c.start()
        own_copy(l, k).start()

    def gather_b(l, k):
        w = w_hbm[k].at[l]
        wait_for(bulk(w, k, 3), a_r.at[l, k])
        own_copy(l, k).wait()
        for da in (0, 1, 2, 3):
            src = slab_of(w, k, (a_me + da) % 4, b_me)
            for d in (1, 2, 3):
                remote(src, src, b_s.at[l, k], b_r.at[l, k], bpeer(d)).start()

    def gather_c(l, k):
        w = w_hbm[k].at[l]
        wait_for(bulk(w, k, 12), b_r.at[l, k])
        for blk in parts_of(w, k, s):
            remote(blk, blk, c_s.at[l, k], c_r.at[l, k], sib).start()

    def gather_d(l, k):
        wait_for(bulk(w_hbm[k].at[l], k, 16), c_r.at[l, k])

    def gather_drain(l, k):
        w = w_hbm[k].at[l]
        wait_for(bulk(w, k, 3), a_s.at[l, k])
        wait_for(bulk(w, k, 12), b_s.at[l, k])
        wait_for(bulk(w, k, 16), c_s.at[l, k])

    def sum0_go(l, k):
        for i, blk in enumerate(parts_of(g_v[k], k, 1 - s)):
            dst = r0[k].at[l, i] if k != SH else r0[k].at[l]
            remote(blk, dst, q0_s.at[l, k], q0_r.at[l, k], sib).start()

    def halves_tmp(k):
        if k in (PR, EX):
            return [tmp.at[pl.ds(HW * p, HW), pl.ds(0, FULL[k][1])] for p in (0, 1)]
        if k == OU:
            return [tmp.at[pl.ds(HW * p, HW), pl.ds(0, HW)] for p in (0, 1)]
        return [tmp.at[:, pl.ds(768 * p, 768)] for p in (0, 1)]

    def sum0_end(l, k):
        wait_for(r0[k].at[l], q0_r.at[l, k])
        srcs = [r0[k].at[l, i] for i in (0, 1)] if k != SH else [r0[k].at[l, pl.ds(768 * i, 768)] for i in (0, 1)]
        cps = [pltpu.make_async_copy(a, b, t_sem.at[i]) for i, (a, b) in enumerate(zip(srcs, halves_tmp(k)))]
        for c in cps:
            c.start()
        for p in (0, 1):
            cps[p].wait()

            def add(i):
                if k in (PR, EX):
                    rows, cols, n = at(HW * (2 * p + s) + 96 * i, 96, 96), slice(None), FULL[k][1]
                    other = tmp[pl.ds(pl.multiple_of(HW * p + 96 * i, 96), 96), 0:n]
                elif k == OU:
                    rows, cols = span(i, 96), at(HW * (2 * p + s), HW, HW)
                    other = tmp[pl.ds(pl.multiple_of(HW * p + 96 * i, 96), 96), 0:HW]
                else:
                    rows, cols = at(768 * p + 96 * i, 96, 96), at(768 * s, 768, 768)
                    other = tmp[span(i, 96), 768 * p:768 * p + 768]
                g_v[k][rows, cols] = (g_v[k][rows, cols].astype(F32) + other.astype(F32)).astype(BF)
            tiles(8 if k == SH else 4, add)
        for d in (1, 2, 3):
            for da in (0, 1, 2, 3):
                a = (a_me + da) % 4
                remote(slab_of(g_v[k], k, a, (b_me + d) % 4), r1[k].at[l, d - 1, da],
                       q1_s.at[l, k], q1_r.at[l, k], bpeer(d)).start()

    def tmp_slab(k, i):
        rows, cols = SLAB[k]
        if k == SH:
            return pl.ds(rows * (i % 6), rows), pl.ds(768 * (i // 6), 768)
        return pl.ds(rows * i, rows), pl.ds(0, cols)

    def sum1_end(l, k):
        wait_for(r1[k].at[l], q1_r.at[l, k])
        cps = []
        for d in range(3):
            for da in range(4):
                c = pltpu.make_async_copy(r1[k].at[l, d, da], tmp.at[tmp_slab(k, d * 4 + da)], t_sem.at[2 + d * 4 + da])
                c.start()
                cps.append(c)
        for c in cps:
            c.wait()
        for da in (1, 2, 3, 0):
            cx, cz = grid((a_me + da) % 4, b_me)
            where = slab_at(k, s, cx, cz)
            total = g_v[k][where].astype(F32)
            for d in range(3):
                total = total + tmp[tmp_slab(k, d * 4 + da)].astype(F32)
            if da == 0:
                bld[k][l] = total.astype(BF)
            else:
                g_v[k][where] = total.astype(BF)
                remote(slab_of(g_v[k], k, (a_me + da) % 4, b_me), r2[k].at[l, da - 1],
                       q2_s.at[l, k], q2_r.at[l, k], apeer(da)).start()

    fsend = (sp, so, se, fss)
    frecv = (fp, fo, fe, fs)

    def last_moves(l, k):
        out = []
        if k == SH:
            out.append((fss.at[l], fs.at[s], f_s.at[l, k, 0], f_r.at[k, s], dev(l, y, x, z), s == l))
            return out
        for p in (0, 1):
            if k == OU:
                q = 2 * zp + s
                who, me, slot = dev(l, y, x, 2 * zh + p), (s == l) & (zp == p), q
            else:
                yo = 2 * zp + s
                who, me, slot = dev(l, yo, x, 2 * zh + p), (s == l) & (yo == y) & (zp == p), y
            out.append((fsend[k].at[2 * l + p], frecv[k].at[slot], f_s.at[l, k, p], f_r.at[k, slot], who, me))
        return out

    def sum2_end(l, k):
        wait_for(r2[k].at[l], q2_r.at[l, k])
        cps = []
        for d in range(3):
            c = pltpu.make_async_copy(r2[k].at[l, d], tmp.at[tmp_slab(k, d)], t_sem.at[2 + d])
            c.start()
            cps.append(c)
        for c in cps:
            c.wait()
        total = bld[k][l].astype(F32)
        for d in range(3):
            total = total + tmp[tmp_slab(k, d)].astype(F32)
        if k == SH:
            fss[l] = total.astype(BF)
        else:
            for p in (0, 1):
                fsend[k][2 * l + p] = to32(total[24 * p:24 * (p + 1)])
        for m in last_moves(l, k):
            send_or_keep(*m)

    def sum_drain(l, k):
        wait_for(r0[k].at[l], q0_s.at[l, k])
        wait_for(r1[k].at[l], q1_s.at[l, k])
        wait_for(r2[k].at[l], q2_s.at[l, k])

    def finish_weights():
        for l in (0, 1):
            for k in range(4):
                for m in last_moves(l, k):
                    sent(*m)
        for k in range(4):
            for i in range(2 if k == SH else 4):
                wait_for(frecv[k].at[i], f_r.at[k, i])

    def vec_copies(stage):
        out = []
        if stage == 0:
            out.append(remote(smt.at[1 - s], sme.at[0, 0], e_s.at[0, 0], e_r.at[0, 0], sib))
            return out
        for d in (1, 2, 3):
            if stage == 1:
                who = dev(s, y, x, (z + d) % 4)
            elif stage == 2:
                who = dev(s, y, (x + d) % 4, z)
            else:
                out.append(remote(sm_out.at[t], sm_out.at[t], e_s.at[3, d - 1], e_r.at[3, d - 1], ypeer(d)))
                continue
            out.append(remote(smt.at[2 + stage], sme.at[stage, d - 1], e_s.at[stage, d - 1], e_r.at[stage, d - 1], who))
        return out

    def vec_go(stage):
        for c in vec_copies(stage):
            c.start()

    def vec_end(stage):
        for c in vec_copies(stage):
            c.wait()
        if stage == 0:
            smt[3] = smt[pl.ds(s, 1)][0] + sme[0, 0]
        elif stage == 1:
            smt[4] = smt[3] + sme[1, 0] + sme[1, 1] + sme[1, 2]
        elif stage == 2:
            sm_out[pl.ds(t, 1)] = (smt[4] + sme[2, 0] + sme[2, 1] + sme[2, 2])[None]

    def wcopy(k, l):
        return pltpu.make_async_copy(w_hbm[k].at[l], w_v[k], w_sem.at[k])

    def ag_copies(buf, idx):
        return [remote(buf.at[own], buf.at[own], y_s.at[idx, d - 1], y_r.at[idx, d - 1], ypeer(d)) for d in (1, 2, 3)]

    def go(cps):
        for c in cps:
            c.start()

    def end(cps):
        for c in cps:
            c.wait()

    def reduce_go(idx):
        cps = []
        for d in (1, 2, 3):
            r = (t + d) % 4
            sb[d - 1] = pf[at(r * T, T, T), :].astype(BF)
            c = remote(sb.at[d - 1], rb.at[idx % 2, d - 1], y_s.at[8 + idx, d - 1], y_r.at[8 + idx, d - 1], ypeer(d))
            c.start()
            cps.append(c)
        return cps

    def reduce_end(cps, idx):
        end(cps)
        total = pf[own, :]
        for d in (1, 2, 3):
            total = total + rb[idx % 2, d - 1].astype(F32)
        return total

    live = lax.broadcasted_iota(jnp.int32, (T, 128), 0).astype(F32) < len_ref[0:1, :]
    livef = jnp.concatenate([jnp.where(live, 1.0, 0.0)] * 12, axis=1)

    def put_result(l, ref, value, way):
        @pl.when(s == l)
        def _():
            ref[pl.ds(s, 1)] = value[None]

        @pl.when(s != l)
        def _():
            ostage[way] = value
            remote(ostage.at[way], ref.at[s], x_s.at[way], x_r.at[way], sib).start()

    def finish_results():
        for way, ref in enumerate((act_out, ig_out)):
            remote(ostage.at[way], ref.at[s], x_s.at[way], x_r.at[way], sib).wait()

    def nothing():
        pass

    def forward(l, hidden, hooks):
        hook = lambda name: hooks.get(name, nothing)()
        xh, rsd = stats(hidden)
        xh1[l] = xh
        rd1[l] = jnp.broadcast_to(rsd, (T, 128))
        normed[l, own, :] = (xh * small[l, 0:1, :] + small[l, 1:2, :]).astype(BF)
        cps = ag_copies(normed.at[l], l * 2)
        go(cps)
        hook("normed")
        end(cps)
        wcopy(PR, l).wait()
        for part in range(3):
            joined = nn(normed[l], vp[:, part * HW:(part + 1) * HW]) + small[l, 7:8, part * HW:(part + 1) * HW]
            for h in range(3):
                v = joined[:, h * 128:(h + 1) * 128]
                if part < 2:
                    v = v * cos_ref[...] + pltpu.roll(v, 64, 1) * sin_ref[...]
                qkv[l, :, part * HW + h * 128:part * HW + (h + 1) * 128] = v.astype(BF)
        hook("joined")
        for h in range(3):
            q = qkv[l, :, h * 128:(h + 1) * 128]
            k = qkv[l, :, HW + h * 128:HW + (h + 1) * 128]
            v = qkv[l, :, 2 * HW + h * 128:2 * HW + (h + 1) * 128]
            sc = jnp.where(vis[...] > 0.5, nt(q, k) * SCALE, MASKED)
            top = jnp.max(sc, axis=-1, keepdims=True)
            ex = jnp.exp(sc - top)
            p = ex * (1.0 / jnp.sum(ex, axis=-1, keepdims=True))
            probs[l, h] = p
            mixed[l, :, h * 128:(h + 1) * 128] = nn(p.astype(BF), v).astype(BF)
        wcopy(OU, l).wait()

        def out_tile(i):
            pf[:, span(i, 512)] = nn(mixed[l], vo[:, span(i, 512)])
        tiles(3, out_tile)
        cps = reduce_go(l * 2)
        hook("mixed")
        middle = hidden + reduce_end(cps, l * 2) + small[l, 2:3, :]
        xh, rsd = stats(middle)
        xh2[l] = xh
        rd2[l] = jnp.broadcast_to(rsd, (T, 128))
        ns[l, own, :] = (xh * small[l, 3:4, :] + small[l, 4:5, :]).astype(BF)
        keep[...] = middle
        cps = ag_copies(ns.at[l], l * 2 + 1)
        go(cps)
        hook("second")
        end(cps)
        wcopy(EX, l).wait()

        def up_tile(i):
            c = span(i, 256)
            u = nn(ns[l], ve[:, c]) + small[l, 6:7, c]
            m = mask_ref[0:1, c]
            u2 = u * u
            th = jnp.tanh(GC * u * (1.0 + 0.044715 * u2))
            half = 0.5 * (1.0 + th)
            active[l, :, c] = (u * half * m).astype(BF)
            gder[l, :, c] = m * (half + 0.5 * u * (1.0 - th * th) * (GC * (1.0 + 3 * 0.044715 * u2)))
        tiles(6, up_tile)
        hook("upper")
        wcopy(SH, l).wait()

        def down_tile(i):
            pf[:, span(i, 256)] = nn(active[l], vs[:, span(i, 256)])
        tiles(6, down_tile)
        cps = reduce_go(l * 2 + 1)
        hook("down")
        result = (keep[...] + reduce_end(cps, l * 2 + 1) + small[l, 5:6, :]) * livef
        result = result.astype(BF)
        put_result(l, act_out, result, 0)
        return result

    def norm_back(dn, xh, rsd, gain):
        e = dn * gain
        return rsd[:, 0:1] * (e - jnp.mean(e, axis=-1, keepdims=True)
                              - xh * jnp.mean(e * xh, axis=-1, keepdims=True))

    def backward(l, g, hooks):
        hook = lambda name: hooks.get(name, nothing)()
        g32 = g.astype(F32)
        smt[l, 5:6, :] = colsum(g32)
        gall[own, :] = g
        cps = ag_copies(gall, 4 + l * 2)
        go(cps)
        hook("grad")
        end(cps)
        if l == 0:
            wcopy(SH, 0).wait()

        def dact_tile(i):
            c = span(i, 256)
            da = nt(gall[...], vs[c, :]) * gder[l, :, c]
            da = da.astype(BF)
            dup[:, c] = da
            smt[l, 6:7, c] = colsum(da.astype(F32))
        tiles(6, dact_tile)
        if l == 1:
            wcopy(SH, 0).start()
        else:
            wcopy(EX, 0).wait()

        def e_tile(i):
            c = span(i, 256)
            pf[:, c] = nt(dup[...], ve[c, :])
        tiles(6, e_tile)
        if l == 1:
            wcopy(EX, 0).start()
        cps = reduce_go(4 + l * 2)
        hook("upper")

        def gs_tile(i):
            c = span(i, 256)
            us_[c, :] = tn(active[l, :, c], gall[...]).astype(BF)
        tiles(6, gs_tile)
        sum0_go(l, SH)
        dn = reduce_end(cps, 4 + l * 2)
        smt[l, 3:4, :] = colsum(dn * xh2[l])
        smt[l, 4:5, :] = colsum(dn)
        dmid = g32 + norm_back(dn, xh2[l], rd2[l], small[l, 3:4, :])
        db = dmid.astype(BF)
        smt[l, 2:3, :] = colsum(db.astype(F32))
        keep[...] = dmid
        dball[own, :] = db
        cps = ag_copies(dball, 4 + l * 2 + 1)
        go(cps)

        def ge_tile(i):
            c = span(i, 256)
            ue[c, :] = tn(ns[l, :, c], dup[...]).astype(BF)
        tiles(6, ge_tile)
        sum0_go(l, EX)
        hook("middle")
        end(cps)
        if l == 0:
            wcopy(OU, 0).wait()
        dmix[...] = nt(dball[...], vo[...]).astype(BF)
        if l == 1:
            wcopy(OU, 0).start()
        for h in range(3):
            c = slice(h * 128, (h + 1) * 128)
            q = qkv[l, :, h * 128:(h + 1) * 128]
            k = qkv[l, :, HW + h * 128:HW + (h + 1) * 128]
            v = qkv[l, :, 2 * HW + h * 128:2 * HW + (h + 1) * 128]
            p = probs[l, h]
            dm = dmix[:, c]
            dj[:, 2 * HW + h * 128:2 * HW + (h + 1) * 128] = tn(p.astype(BF), dm).astype(BF)
            dp = nt(dm, v)
            dsc = (p * (dp - jnp.sum(dp * p, axis=-1, keepdims=True))).astype(BF)
            for part, v in ((0, nn(dsc, k)), (1, tn(dsc, q))):
                v = v * SCALE
                v = v * cos_ref[...] - pltpu.roll(v, 64, 1) * sin_ref[...]
                dj[:, part * HW + h * 128:part * HW + (h + 1) * 128] = v.astype(BF)
        smt[l, 7:8, :] = jnp.zeros((1, D), F32)
        smt[l, 7:8, 0:QW] = colsum(dj[...].astype(F32))
        if l == 0:
            wcopy(PR, 0).wait()

        def d_tile(i):
            c = span(i, 256)
            pf[:, c] = nt(dj[...], vp[c, :])
        tiles(6, d_tile)
        if l == 1:
            wcopy(PR, 0).start()
        cps = reduce_go(4 + l * 2 + 1)
        hook("joined")
        uo[...] = tn(mixed[l], dball[...]).astype(BF)
        sum0_go(l, OU)

        def gp_tile(i):
            c = span(i, 256)
            up[c, :] = tn(normed[l, :, c], dj[...]).astype(BF)
        tiles(6, gp_tile)
        sum0_go(l, PR)
        hook("project")
        dn = reduce_end(cps, 4 + l * 2 + 1)
        smt[l, 0:1, :] = colsum(dn * xh1[l])
        smt[l, 1:2, :] = colsum(dn)
        dh = keep[...] + norm_back(dn, xh1[l], rd1[l], small[l, 0:1, :])
        res = dh.astype(BF)
        put_result(l, ig_out, res, 1)
        return res

    gather_a(0, PR)
    gather_a(0, OU)
    pack_end(0)
    pack_go(1)
    gather_a(0, EX)
    gather_a(0, SH)
    gather_b(0, PR)
    pack_end(1)
    pack_go(2)
    gather_b(0, OU)
    gather_b(0, EX)
    gather_b(0, SH)
    pack_end(2)
    pltpu_pack = remote(allp.at[s], allp.at[s], p_s.at[3, 0], p_r.at[3, 0], sib)
    pltpu_pack.start()
    gather_c(0, PR)
    end(lcs)
    row = lax.broadcasted_iota(jnp.int32, (TG, TG), 0)
    col = lax.broadcasted_iota(jnp.int32, (TG, TG), 1)
    limit = jnp.zeros((1, TG), F32)
    blk = lax.broadcasted_iota(jnp.int32, (1, TG), 1) // T
    for r in range(4):
        one = lens[r][0:1, :]
        limit = jnp.where(blk == r, jnp.concatenate([one, one], axis=1), limit)
    ok = (row // T == col // T) & (col <= row) & ((col % T).astype(F32) < limit)
    vis[...] = jnp.where(ok, 1.0, 0.0)
    pltpu_pack.wait()

    def spread(rows, width, total):
        n = lax.broadcasted_iota(jnp.int32, (128, total), 1)
        i = lax.broadcasted_iota(jnp.int32, (128, total), 0)
        pick = jnp.where(n - (n // width) * width == i, 1.0, 0.0).astype(BF)
        wide = nn(rows.astype(BF), pick)
        n = lax.broadcasted_iota(jnp.int32, (64, total), 1)
        c = lax.broadcasted_iota(jnp.int32, (64, total), 0)
        return colsum(jnp.where(n // width == c, wide, 0.0))

    for l in (0, 1):
        for r in range(6):
            small[l, r:r + 1, :] = spread(allp[l, :, r, :], 24, D)
        mine = allp[l, at(16 * t, 16, 16), 6, :]
        n = lax.broadcasted_iota(jnp.int32, (128, D), 1)
        i = lax.broadcasted_iota(jnp.int32, (128, D), 0)
        pick = jnp.where(n - (n // 96) * 96 == i, 1.0, 0.0).astype(BF)
        wide = nn(mine.astype(BF), pick)
        n = lax.broadcasted_iota(jnp.int32, (16, D), 1)
        c = lax.broadcasted_iota(jnp.int32, (16, D), 0)
        small[l, 6:7, :] = colsum(jnp.where(n // 96 == c, wide, 0.0))
        n = lax.broadcasted_iota(jnp.int32, (128, QW), 1)
        i = lax.broadcasted_iota(jnp.int32, (128, QW), 0)
        n = n + (n // HW) * (D - HW) + HW * t
        pick = jnp.where(n - (n // 72) * 72 == i, 1.0, 0.0).astype(BF)
        wide = nn(allp[l, :, 7, :].astype(BF), pick)
        n = lax.broadcasted_iota(jnp.int32, (64, QW), 1)
        c = lax.broadcasted_iota(jnp.int32, (64, QW), 0)
        n = n + (n // HW) * (D - HW) + HW * t
        small[l, 7:8, 0:QW] = colsum(jnp.where(n // 72 == c, wide, 0.0))

    def f0_normed():
        gather_d(0, PR)
        wcopy(PR, 0).start()
        gather_c(0, OU)

    def f0_joined():
        for k in range(4):
            gather_a(1, k)
        gather_d(0, OU)
        wcopy(OU, 0).start()

    def f0_mixed():
        gather_c(0, EX)
        gather_b(1, PR)
        gather_b(1, OU)

    def f0_second():
        gather_d(0, EX)
        wcopy(EX, 0).start()
        gather_c(0, SH)
        gather_b(1, EX)
        gather_b(1, SH)

    def f0_upper():
        gather_d(0, SH)
        wcopy(SH, 0).start()
        gather_c(1, PR)

    def f0_down():
        gather_d(1, PR)
        wcopy(PR, 1).start()
        gather_c(1, OU)

    def f1_normed():
        gather_d(1, OU)
        wcopy(OU, 1).start()

    def f1_mixed():
        gather_c(1, EX)

    def f1_second():
        gather_d(1, EX)
        wcopy(EX, 1).start()
        gather_c(1, SH)

    def f1_upper():
        gather_d(1, SH)
        wcopy(SH, 1).start()

    h0 = h_ref[...].astype(F32)
    a1 = forward(0, h0, dict(normed=f0_normed, joined=f0_joined, mixed=f0_mixed, second=f0_second,
                             upper=f0_upper, down=f0_down))
    forward(1, a1.astype(F32), dict(normed=f1_normed, mixed=f1_mixed, second=f1_second, upper=f1_upper))

    for k in range(4):
        for l in (0, 1):
            gather_drain(l, k)
    for m in moves:
        sent(*m)

    def b1_middle():
        sum0_end(1, SH)

    def b1_joined():
        sum0_end(1, EX)

    def b0_grad():
        sum0_end(1, OU)
        sum0_end(1, PR)

    def b0_upper():
        sum1_end(1, SH)
        sum1_end(1, EX)
        sum_drain(1, SH)
        sum_drain(1, EX)

    def b0_middle():
        sum0_end(0, SH)
        sum1_end(1, OU)
        sum1_end(1, PR)

    def b0_joined():
        sum0_end(0, EX)
        sum2_end(1, SH)
        sum2_end(1, EX)
        sum_drain(1, OU)
        sum_drain(1, PR)

    g2 = (cot_ref[...].astype(F32) * livef).astype(BF)
    ig2 = backward(1, g2, dict(middle=b1_middle, joined=b1_joined))
    g1 = (ig2.astype(F32) * livef).astype(BF)
    backward(0, g1, dict(grad=b0_grad, upper=b0_upper, middle=b0_middle, joined=b0_joined))
    vec_go(0)
    sum0_end(0, OU)
    sum0_end(0, PR)
    vec_end(0)
    vec_go(1)
    sum1_end(0, SH)
    sum1_end(0, EX)
    vec_end(1)
    vec_go(2)
    sum2_end(1, OU)
    sum2_end(1, PR)
    vec_end(2)
    vec_go(3)
    sum1_end(0, OU)
    sum1_end(0, PR)
    for k in (SH, EX, OU, PR):
        sum2_end(0, k)
    vec_end(3)
    finish_weights()
    finish_results()
    for k in range(4):
        sum_drain(0, k)


def core_call(h, cot, lens, mask, pack, cos2, sin2, pw, ow, ew, sw):
    sd = jax.ShapeDtypeStruct
    V = pltpu.VMEM
    DMA = pltpu.SemaphoreType.DMA
    hbm = [sd((2,) + f, BF) for f in FULL]
    hbm += [sd((2, 2, HW, QW), BF), sd((2, 2, HW, HW), BF), sd((2, 2, HW, D), BF), sd((2, D, 768), BF)]
    hbm += [sd((2, 3, 4) + f, BF) for f in SLAB]
    hbm += [sd((2, 3) + f, BF) for f in SLAB]
    out = pl.pallas_call(
        core_kernel,
        out_shape=[sd((2, T, D), BF), sd((2, T, D), BF), sd((4, 8, D), F32),
                   sd((4, 32, QW), BF), sd((4, 32, HW), BF), sd((4, 32, D), BF), sd((2, 96, 768), BF)] + hbm,
        in_specs=[VM] * 11,
        out_specs=[VM] * 7 + [ANY] * 16,
        scratch_shapes=[
            V((D, QW), BF), V((HW, D), BF), V((D, D), BF), V((D, D), BF),
            V((D, QW), BF), V((HW, D), BF), V((D, D), BF), V((D, D), BF),
            V((2, TG, D), BF), V((2, TG, D), BF), V((TG, D), BF), V((TG, D), BF),
            V((2, TG, QW), BF), V((2, 3, TG, TG), F32), V((2, TG, HW), BF),
            V((2, TG, D), F32), V((2, TG, D), BF),
            V((2, T, D), F32), V((2, T, D), F32), V((2, T, 128), F32), V((2, T, 128), F32),
            V((TG, D), F32), V((3, T, D), BF), V((2, 3, T, D), BF),
            V((TG, D), BF), V((TG, QW), BF), V((TG, HW), BF), V((TG, TG), F32), V((4, 8, 128), F32),
            V((T, D), F32), V((2, T, D), BF),
            V((4, 32, QW), BF), V((4, 32, HW), BF), V((4, 32, D), BF),
            V((2, 2, 32, QW), BF), V((2, 2, 32, HW), BF), V((2, 2, 32, D), BF), V((2, 96, 768), BF),
            V((2, 48, QW), BF), V((2, 48, HW), BF), V((2, 48, D), BF),
            V((2, 96, 768), BF),
            V((768, D), BF), V((2, 64, 8, 128), F32), V((2, 8, D), F32), V((5, 8, D), F32), V((3, 3, 8, D), F32),
            DMA((16, 3)), DMA((16, 3)), DMA((4,)), DMA((4,)), DMA((4,)), DMA((3,)), DMA((3,)),
            DMA((3, 4)), DMA((2,)), DMA((3, 2, 2)), DMA((2,)), DMA((4, 3)), DMA((4, 3)),
            DMA((2, 4)), DMA((2, 4)), DMA((2, 4)), DMA((2, 4)), DMA((2, 4)), DMA((2, 4)), DMA((2, 4)),
            DMA((2, 4)), DMA((2, 4)), DMA((2, 4)), DMA((2, 4)), DMA((2, 4)), DMA((2, 4)), DMA((14,)),
            DMA((2, 4, 2)), DMA((4, 4)), DMA((4, 3)), DMA((4, 3)),
        ],
        compiler_params=pltpu.CompilerParams(collective_id=1, has_side_effects=True,
                                             vmem_limit_bytes=64 * 2**20 - 2**16),
    )(h, cot, lens, mask, pack, cos2, sin2, pw, ow, ew, sw)
    return out[:7]


def rotary():
    half = 64
    rates = (np.float32(10000.0) ** (-np.arange(half, dtype=np.float32) / np.float32(half))).astype(np.float32)
    ang = np.arange(T, dtype=np.float32)[:, None] * rates[None, :]
    cos, sin = np.cos(ang), np.sin(ang)
    cos2 = np.concatenate([cos, cos], axis=1)
    sin2 = np.concatenate([-sin, sin], axis=1)
    return np.tile(cos2, (4, 1)).astype(np.float32), np.tile(sin2, (4, 1)).astype(np.float32)


def per_device(window_input, cotangent, lengths, widths, gain_first, shift_first, project_weight, project_bias,
               output_weight, output_bias, gain_second, shift_second, expand_weight, expand_bias,
               shrink_weight, shrink_bias):
    s = lax.axis_index("section")
    chip = lax.axis_index("dp")
    t = chip // 16
    vectors = (gain_first, shift_first, output_bias, gain_second, shift_second, shrink_bias, expand_bias, project_bias)
    pack = jnp.concatenate([jnp.pad(v, ((0, 0), (0, 128 - v.shape[1]))) for v in vectors], axis=0).astype(F32)
    length = jnp.where(s == 0, lengths[0, 0], lengths[1, 0]).astype(F32)
    lens = jnp.broadcast_to(length, (8, 128))
    width = jnp.where(s == 0, widths[0], widths[1])
    mask = ((jnp.arange(D) + D * t) < width).astype(F32)[None]
    cos2, sin2 = rotary()

    def mine_of(rows):
        return jnp.where(s == 0, rows[0, 0], rows[1, 0])

    act, ig, sums, fp, fo, fe, fs = core_call(
        mine_of(window_input), mine_of(cotangent), lens, mask, pack, jnp.asarray(cos2), jnp.asarray(sin2),
        project_weight, output_weight, expand_weight, shrink_weight)
    d_pw = fp[:, :24].astype(F32).reshape(4, 24, 3, HW).transpose(1, 2, 0, 3).reshape(1, 24, 3 * D)
    d_ow = fo[:, :24].astype(F32).transpose(1, 0, 2).reshape(1, 24, D)
    d_ew = fe[:, :24].astype(F32).transpose(1, 0, 2).reshape(1, 24, 4 * D)
    d_sw = fs.astype(F32).transpose(1, 0, 2).reshape(1, 96, D)
    totals = jnp.sum(sums[:, :6], axis=0)
    mine = lax.dynamic_slice_in_dim(totals, 24 * chip, 24, axis=1)
    d_eb = lax.dynamic_slice_in_dim(sums[:, 6].reshape(1, 4 * D), 96 * chip, 96, axis=1)
    d_pb = sums[:, 7, :QW].reshape(4, 3, HW).transpose(1, 0, 2).reshape(1, 3 * D)
    d_pb = lax.dynamic_slice_in_dim(d_pb, 72 * chip, 72, axis=1)
    g1, s1, ob, g2, s2, sbias = (mine[i:i + 1] for i in range(6))
    return (act[None, :, None], ig[None, :, None], g1, s1, d_pw, d_pb, d_ow, ob, g2, s2, d_ew, d_eb, d_sw, sbias)


def solution(mesh):
    row = P("section", "dp")
    mat = P("section", "dp", None)
    params = (row, row, mat, row, mat, row, row, row, mat, row, mat, row)
    seq = P(None, "dp", None, None)
    out = P("section", None, "dp", None, None)
    return jax.shard_map(
        per_device, mesh=mesh,
        in_specs=(seq, seq, P(None, "dp"), P()) + params,
        out_specs=(out, out) + params,
        check_vma=False,
    )
```

```python
import jax
import jax.numpy as jnp
import numpy as np
from jax import lax
from jax.experimental import pallas as pl
from jax.experimental.pallas import tpu as pltpu
from jax.sharding import PartitionSpec as P

MESH = pl.DeviceIdType.MESH
ANY = pl.BlockSpec(memory_space=pl.ANY)
VM = pl.BlockSpec(memory_space=pltpu.VMEM)
EPS = 1e-05
MASKED = -1e9
BF = jnp.bfloat16
F32 = jnp.float32
D = 1536
T = 64
TG = 256
HW = 384
QW = 1152
SCALE = 128 ** -0.5
GC = (2 / np.pi) ** 0.5
PR, OU, EX, SH = range(4)
FULL = ((D, QW), (HW, D), (D, D), (D, D))
SLAB = ((48, QW), (48, HW), (48, D), (96, 768))


def nn(a, b):
    return jnp.dot(a, b, preferred_element_type=F32)


def nt(a, b):
    return lax.dot_general(a, b, (((1,), (1,)), ((), ())), preferred_element_type=F32)


def tn(a, b):
    return lax.dot_general(a, b, (((0,), (0,)), ((), ())), preferred_element_type=F32)


def tiles(count, body):
    def step(i, carry):
        body(i)
        return carry
    with jax.named_scope(body.__name__):
        lax.fori_loop(0, count, step, 0)


def span(i, size):
    return pl.ds(pl.multiple_of(i * size, size), size)


def at(start, size, unit):
    return pl.ds(pl.multiple_of(start, unit), size)


def stats(x):
    mean = jnp.mean(x, axis=-1, keepdims=True)
    c = x - mean
    var = jnp.mean(c * c, axis=-1, keepdims=True)
    rs = lax.rsqrt(var + EPS)
    return c * rs, rs


def named(name):
    def deco(fn):
        def inner(*args):
            with jax.named_scope(name):
                return fn(*args)
        return inner
    return deco


def colsum(v):
    return jnp.sum(v, axis=0, keepdims=True)


def to32(v):
    v = v.astype(F32)
    return jnp.concatenate([v, jnp.zeros((8, v.shape[1]), F32)], axis=0).astype(BF)


def core_kernel(win_ref, cot_ref, len_ref, wid_ref, v0, v1, v2, v3, v4, v5, v6, v7, cos_ref, sin_ref, pw, ow, ew, sw,
                act_out, ig_out, sm_out, fp, fo, fe, fs,
                wp, wo, we, ws, r0p, r0o, r0e, r0s, r1p, r1o, r1e, r1s, r2p, r2o, r2e, r2s,
                vp, vo, ve, vs, up, uo, ue, us_,
                normed, ns, gall, dball, qkv, probs, mixed, gder, active, xh1, xh2, rd1, rd2,
                pf, sb, rb, dup, dj, dmix, vis, lens, keep, ostage,
                sp, so, se, cp, co, ce, cs, bp, bo, be, fss,
                tmp, tmp1, allp, small, smt, sme,
                y_s, y_r, w_sem, x_s, x_r, l_s, l_r, z_s, zo_s, z_r, zs_r, p_s, p_r,
                a_s, a_r, b_s, b_r, c_s, c_r, o_sem, q0_s, q0_r, q1_s, q1_r, q2_s, q2_r, t_sem,
                f_s, f_r, e_s, e_r, m_s, m_r, token, f2_r, qf_r, v_sem):
    s = lax.axis_index("section")
    chip = lax.axis_index("dp")
    y, x, z = chip // 16, (chip // 4) % 4, chip % 4
    t = y
    zp = z % 2
    zh = z // 2
    first = s == 0

    def dev(core, cy, cx, cz):
        return (core, cy * 16 + cx * 4 + cz)

    def ypeer(d):
        return dev(s, (y + d) % 4, x, z)

    a_me = jnp.where(first, x, z)
    b_me = jnp.where(first, z, x)

    def grid(a, b):
        return jnp.where(first, a, b), jnp.where(first, b, a)

    def apeer(d):
        cx, cz = grid((a_me + d) % 4, b_me)
        return dev(s, y, cx, cz)

    def bpeer(d):
        cx, cz = grid(a_me, (b_me + d) % 4)
        return dev(s, y, cx, cz)

    sib = dev(1 - s, y, x, z)
    own = at(t * T, T, T)

    bar = pltpu.get_barrier_semaphore()

    def greet(who):
        pl.semaphore_signal(bar, inc=1, device_id=who, device_id_type=MESH)

    with jax.named_scope("greet"):
        for d in (1, 2, 3):
            for core in (s, 1 - s):
                greet(dev(core, (y + d) % 4, x, z))
        for d in (0, 1, 2, 3):
            for core in (s, 1 - s):
                greet(dev(core, (y + d) % 4, x, 2 * zh + 1 - zp))
        greet(sib)
        for d in (1, 2, 3):
            greet(dev(s, y, (x + d) % 4, z))
        for d in (0, 1):
            greet(dev(s, y, x, 2 * (1 - zh) + d))

    def remote(src, dst, ssem, rsem, who):
        return pltpu.make_async_remote_copy(src_ref=src, dst_ref=dst, send_sem=ssem, recv_sem=rsem,
                                            device_id=who, device_id_type=MESH)

    def wait_for(ref, sem):
        pltpu.make_async_copy(ref, ref, sem).wait()

    w_hbm = (wp, wo, we, ws)
    w_v = (vp, vo, ve, vs)
    g_v = (up, uo, ue, us_)
    r0 = (r0p, r0o, r0e, r0s)
    r1 = (r1p, r1o, r1e, r1s)
    r2 = (r2p, r2o, r2e, r2s)

    def slab_at(k, j, cx, cz):
        if k in (PR, EX):
            return at(48 * (8 * (2 * (cz % 2) + j) + 2 * cx + cz // 2), 48, 48), slice(None)
        if k == OU:
            return at(48 * (2 * cx + cz // 2), 48, 48), at(HW * (2 * (cz % 2) + j), HW, HW)
        return at(96 * (4 * cx + cz), 96, 96), at(768 * j, 768, 768)

    def slab_of(ref, k, a, b):
        cx, cz = grid(a, b)
        return ref.at[slab_at(k, s, cx, cz)]

    def parts_of(ref, k, j):
        if k in (PR, EX):
            return [ref.at[at(HW * (2 * p + j), HW, HW)] for p in (0, 1)]
        if k == OU:
            return [ref.at[:, at(HW * (2 * p + j), HW, HW)] for p in (0, 1)]
        return [ref.at[:, at(768 * j, 768, 768)]]

    def bulk(ref, k, slabs):
        if k in (PR, EX):
            return ref.at[pl.ds(0, 48 * slabs)]
        if k == OU:
            return ref.at[pl.ds(0, 12 * slabs)] if slabs > 3 else ref.at[pl.ds(0, 144), pl.ds(0, HW)]
        return ref.at[pl.ds(0, 48 * slabs)]

    def piece_target(yt):
        return dev(y % 2, yt, x, 2 * zh + y // 2), (yt == y) & (s == y % 2) & (zp == y // 2)

    def out_target(q):
        return dev(q % 2, y, x, 2 * zh + q // 2), (zp == q // 2) & (s == q % 2)

    def send_or_keep(src, dst, ssem, rsem, who, is_me):
        @pl.when(is_me)
        def _():
            pltpu.make_async_copy(src, dst, rsem).start()

        @pl.when(jnp.logical_not(is_me))
        def _():
            remote(src, dst, ssem, rsem, who).start()

    def sent(src, dst, ssem, rsem, who, is_me):
        @pl.when(jnp.logical_not(is_me))
        def _():
            remote(src, dst, ssem, rsem, who).wait_send()

    def shard_moves():
        out = []
        for yt in range(4):
            who, me = piece_target(yt)
            out.append((sp.at[yt], cp.at[s, zp], z_s.at[0, yt], z_r.at[0, s, zp], who, me))
        for q in range(4):
            who, me = out_target(q)
            out.append((so.at[q], co.at[s, zp], z_s.at[1, q], z_r.at[1, s, zp], who, me))
        for yt in range(4):
            who, me = piece_target(yt)
            out.append((se.at[yt], ce.at[s, zp], z_s.at[2, yt], z_r.at[2, s, zp], who, me))
        for j in range(2):
            out.append((sw.at[0, :, pl.ds(768 * j, 768)], cs.at[s], zo_s.at[j], zs_r.at[s],
                        dev(j, y, x, z), s == j))
        return out

    moves = shard_moves()
    with jax.named_scope("shards"):
        for yt in range(4):
            sp[yt] = to32(jnp.concatenate([pw[0, :, p * D + HW * yt:p * D + HW * (yt + 1)] for p in range(3)], axis=1))
        for q in range(4):
            so[q] = to32(ow[0, :, HW * q:HW * (q + 1)])
        for yt in range(4):
            se[yt] = to32(ew[0, :, D * yt:D * (yt + 1)])

    allp[s, pl.ds(chip, 1)] = jnp.zeros((1, 8, 128), F32)
    for r, v in enumerate((v0, v1, v2, v3, v4, v5, v6, v7)):
        allp[s, pl.ds(chip, 1), r:r + 1, 0:v.shape[1]] = v[...].astype(F32)[None]

    def pack_copies(stage):
        out = []
        for d in (1, 2, 3):
            if stage == 0:
                blk, who = allp.at[s, pl.ds(chip, 1)], dev(s, y, x, (z + d) % 4)
            elif stage == 1:
                blk, who = allp.at[s, at(chip - z, 4, 4)], dev(s, y, (x + d) % 4, z)
            else:
                blk, who = allp.at[s, at(16 * y, 16, 16)], ypeer(d)
            out.append(remote(blk, blk, p_s.at[stage, d - 1], p_r.at[stage, d - 1], who))
        return out

    @named("pack go")
    def pack_go(stage):
        for c in pack_copies(stage):
            c.start()

    @named("pack wait")
    def pack_end(stage):
        for c in pack_copies(stage):
            c.wait()

    length = len_ref[s, 0].astype(F32)
    width = wid_ref[s]
    lens[pl.ds(t, 1)] = jnp.full((1, 8, 128), length, F32)
    lcs = [remote(lens.at[pl.ds(t, 1)], lens.at[pl.ds(t, 1)], l_s.at[d - 1], l_r.at[d - 1], ypeer(d)) for d in (1, 2, 3)]

    got = (cp, co, ce, cs)
    bld = (bp, bo, be, cs)

    def home(l, k):
        return w_hbm[k].at[1] if l else w_v[k]

    def a_copies(l, k):
        src = bld[k].at[l]
        return [remote(src, slab_of(home(l, k), k, a_me, b_me), a_s.at[l, k], a_r.at[l, k], apeer(d))
                for d in (1, 2, 3)]

    def own_copy(l, k):
        return pltpu.make_async_copy(bld[k].at[l], slab_of(home(l, k), k, a_me, b_me), o_sem.at[l, k])

    @named("gather a")
    def gather_a(l, k):
        if k == SH:
            wait_for(cs.at[l], zs_r.at[l])
        else:
            zk = (0, 1, 2)[k]
            for p in (0, 1):
                wait_for(got[k].at[l, p], z_r.at[zk, l, p])
            halves = [got[k][l, p].astype(F32)[:24] for p in (0, 1)]
            bld[k][l] = jnp.concatenate(halves, axis=0).astype(BF)
        for c in a_copies(l, k):
            c.start()
        own_copy(l, k).start()

    @named("gather b")
    def gather_b(l, k):
        w = home(l, k)
        wait_for(bulk(w, k, 3), a_r.at[l, k])
        own_copy(l, k).wait()
        for a in range(4):
            src = slab_of(w, k, a, b_me)
            for side, d in ((0, 1), (1, 3)):
                remote(src, src, b_s.at[l, k], b_r.at[side, l, k], bpeer(d)).start()

    @named("gather f")
    def gather_f(l, k):
        w = home(l, k)
        for side, d in ((0, 1), (1, 3)):
            wait_for(bulk(w, k, 4), b_r.at[side, l, k])
            for a in (2 * side, 2 * side + 1):
                src = slab_of(w, k, a, (b_me + 4 - d) % 4)
                remote(src, src, b_s.at[l, k], f2_r.at[l, k], bpeer(d)).start()

    @named("gather c")
    def gather_c(l, k):
        w = home(l, k)
        wait_for(bulk(w, k, 4), f2_r.at[l, k])
        for blk in parts_of(w, k, s):
            remote(blk, blk, c_s.at[l, k], c_r.at[l, k], sib).start()

    @named("gather d")
    def gather_d(l, k):
        wait_for(bulk(home(l, k), k, 16), c_r.at[l, k])
        if l == 0:
            save(k).start()

    def save(k):
        return pltpu.make_async_copy(w_v[k], w_hbm[k].at[0], v_sem.at[k])

    @named("gather drain")
    def gather_drain(l, k):
        w = home(l, k)
        wait_for(bulk(w, k, 3), a_s.at[l, k])
        wait_for(bulk(w, k, 12), b_s.at[l, k])
        wait_for(bulk(w, k, 16), c_s.at[l, k])

    def gbuf(l, k):
        if l == 0 and k == PR:
            return us_.at[:, pl.ds(0, QW)]
        return g_v[k] if l else w_v[k]

    @named("sum0 go")
    def sum0_go(l, k):
        for i, blk in enumerate(parts_of(gbuf(l, k), k, 1 - s)):
            dst = r0[k].at[l, i] if k != SH else r0[k].at[l]
            remote(blk, dst, q0_s.at[l, k], q0_r.at[l, k], sib).start()

    def halves_tmp(k):
        if k in (PR, EX):
            return [tmp.at[pl.ds(HW * p, HW), pl.ds(0, FULL[k][1])] for p in (0, 1)]
        if k == OU:
            return [tmp.at[pl.ds(HW * p, HW), pl.ds(0, HW)] for p in (0, 1)]
        return [tmp.at[:, pl.ds(768 * p, 768)] for p in (0, 1)]

    def sum0_copies(l, k):
        srcs = [r0[k].at[l, i] for i in (0, 1)] if k != SH else [r0[k].at[l, pl.ds(768 * i, 768)] for i in (0, 1)]
        return [pltpu.make_async_copy(a, b, t_sem.at[i]) for i, (a, b) in enumerate(zip(srcs, halves_tmp(k)))]

    @named("sum0 load")
    def sum0_load(l, k):
        wait_for(r0[k].at[l], q0_r.at[l, k])
        for c in sum0_copies(l, k):
            c.start()

    @named("sum0")
    def sum0_fin(l, k):
        g = gbuf(l, k)
        cps = sum0_copies(l, k)
        for p in (0, 1):
            cps[p].wait()

            def add(i):
                if k in (PR, EX):
                    rows, cols, n = at(HW * (2 * p + s) + 96 * i, 96, 96), slice(None), FULL[k][1]
                    other = tmp[pl.ds(pl.multiple_of(HW * p + 96 * i, 96), 96), 0:n]
                elif k == OU:
                    rows, cols = span(i, 96), at(HW * (2 * p + s), HW, HW)
                    other = tmp[pl.ds(pl.multiple_of(HW * p + 96 * i, 96), 96), 0:HW]
                else:
                    rows, cols = at(768 * p + 96 * i, 96, 96), at(768 * s, 768, 768)
                    other = tmp[span(i, 96), 768 * p:768 * p + 768]
                g[rows, cols] = (g[rows, cols].astype(F32) + other.astype(F32)).astype(BF)
            tiles(8 if k == SH else 4, add)
        for a in (0, 2, 1, 3):
            far = 1 if a < 2 else 3
            remote(slab_of(g, k, a, (b_me + 2) % 4), r1_slab(l, k, 0, a), q1_s.at[l, k], qf_r.at[l, k], bpeer(far)).start()
        for a in (0, 2, 1, 3):
            near = 3 if a < 2 else 1
            remote(slab_of(g, k, a, (b_me + near) % 4), r1_slab(l, k, near, a), q1_s.at[l, k], q1_r.at[l, k],
                   bpeer(near)).start()

    def r1_slab(l, k, d, a):
        rows = SLAB[k][0]
        return r1[k].at[l, (0, 1, None, 2)[d], pl.ds(rows * a, rows)]

    def tmp_set(k, side):
        rows, cols = SLAB[k]
        if k == SH:
            return tmp1.at[pl.ds(0, 4 * rows), pl.ds(cols * side, cols)]
        return tmp1.at[pl.ds(4 * rows * side, 4 * rows), pl.ds(0, cols)]

    def tmp_slab(k, side, a):
        rows, cols = SLAB[k]
        if k == SH:
            return tmp1[at(rows * a, rows, rows), cols * side:cols * (side + 1)].astype(F32)
        return tmp1[at(4 * rows * side + rows * a, rows, rows), 0:cols].astype(F32)

    @named("sum1 pass on")
    def sum1_mid(l, k):
        g = gbuf(l, k)
        wait_for(r1[k].at[l, 0], qf_r.at[l, k])
        c = pltpu.make_async_copy(r1[k].at[l, 0], tmp_set(k, 0), t_sem.at[2])
        c.start()
        c.wait()
        for a in range(4):
            d = 1 if a < 2 else 3
            cx, cz = grid(a, (b_me + d) % 4)
            where = slab_at(k, s, cx, cz)
            g[where] = (g[where].astype(F32) + tmp_slab(k, 0, a)).astype(BF)
            remote(g.at[where], r1_slab(l, k, d, a), q1_s.at[l, k], q1_r.at[l, k], bpeer(d)).start()

    @named("sum1")
    def sum1_end(l, k):
        g = gbuf(l, k)
        wait_for(r1[k].at[l, pl.ds(1, 2)], q1_r.at[l, k])
        cps = [pltpu.make_async_copy(r1[k].at[l, 1 + i], tmp_set(k, i), t_sem.at[3 + i]) for i in (0, 1)]
        go(cps)
        end(cps)
        for da in (2, 1, 3, 0):
            a = (a_me + da) % 4
            cx, cz = grid(a, b_me)
            where = slab_at(k, s, cx, cz)
            total = g[where].astype(F32) + tmp_slab(k, 0, a) + tmp_slab(k, 1, a)
            if da == 0:
                bld[k][l] = total.astype(BF)
            else:
                g[where] = total.astype(BF)
                remote(g.at[where], r2[k].at[l, da - 1], q2_s.at[l, k], q2_r.at[l, k], apeer(da)).start()

    fsend = (sp, so, se, fss)
    frecv = (fp, fo, fe, fs)

    def last_moves(l, k):
        out = []
        if k == SH:
            out.append((fss.at[l], fs.at[s], f_s.at[l, k, 0], f_r.at[k, s], dev(l, y, x, z), s == l))
            return out
        for p in (0, 1):
            if k == OU:
                q = 2 * zp + s
                who, me, slot = dev(l, y, x, 2 * zh + p), (s == l) & (zp == p), q
            else:
                yo = 2 * zp + s
                who, me, slot = dev(l, yo, x, 2 * zh + p), (s == l) & (yo == y) & (zp == p), y
            out.append((fsend[k].at[2 * l + p], frecv[k].at[slot], f_s.at[l, k, p], f_r.at[k, slot], who, me))
        return out

    @named("sum2")
    def sum2_end(l, k):
        wait_for(r2[k].at[l], q2_r.at[l, k])
        rows, cols = SLAB[k]
        spots = [tmp1.at[pl.ds(rows * d, rows), pl.ds(0, cols)] for d in range(3)]
        cps = [pltpu.make_async_copy(r2[k].at[l, d], spots[d], t_sem.at[5 + d]) for d in range(3)]
        go(cps)
        end(cps)
        total = bld[k][l].astype(F32)
        for d in range(3):
            total = total + tmp1[rows * d:rows * (d + 1), 0:cols].astype(F32)
        if k == SH:
            fss[l] = total.astype(BF)
        else:
            for p in (0, 1):
                fsend[k][2 * l + p] = to32(total[24 * p:24 * (p + 1)])
        for m in last_moves(l, k):
            send_or_keep(*m)

    @named("sum drain")
    def sum_drain(l, k):
        wait_for(r0[k].at[l], q0_s.at[l, k])
        wait_for(r1[k].at[l], q1_s.at[l, k])
        wait_for(r2[k].at[l], q2_s.at[l, k])

    @named("last weights")
    def finish_weights():
        for l in (0, 1):
            for k in range(4):
                for m in last_moves(l, k):
                    sent(*m)
        for k in range(4):
            for i in range(2 if k == SH else 4):
                wait_for(frecv[k].at[i], f_r.at[k, i])

    def vec_copies(stage):
        out = []
        if stage == 0:
            out.append(remote(smt.at[1 - s], sme.at[0, 0], e_s.at[0, 0], e_r.at[0, 0], sib))
            return out
        for d in (1, 2, 3):
            if stage == 1:
                who = apeer(d)
            elif stage == 2:
                who = bpeer(d)
            else:
                out.append(remote(sm_out.at[t], sm_out.at[t], e_s.at[3, d - 1], e_r.at[3, d - 1], ypeer(d)))
                continue
            out.append(remote(smt.at[2 + stage], sme.at[stage, d - 1], e_s.at[stage, d - 1], e_r.at[stage, d - 1], who))
        return out

    @named("vectors go")
    def vec_go(stage):
        for c in vec_copies(stage):
            c.start()

    @named("vectors wait")
    def vec_end(stage):
        for c in vec_copies(stage):
            c.wait()
        if stage == 0:
            smt[3] = smt[pl.ds(s, 1)][0] + sme[0, 0]
        elif stage == 1:
            smt[4] = smt[3] + sme[1, 0] + sme[1, 1] + sme[1, 2]
        elif stage == 2:
            sm_out[pl.ds(t, 1)] = (smt[4] + sme[2, 0] + sme[2, 1] + sme[2, 2])[None]

    def wcopy(k, l):
        return pltpu.make_async_copy(w_hbm[k].at[l], w_v[k], w_sem.at[k])

    LEFT, RIGHT = slice(0, 768), slice(768, D)
    COLS = (pl.ds(0, 768), pl.ds(768, 768))
    right, left = ypeer(1), ypeer(3)

    def rows_of(d):
        return at((t + d) % 4 * T, T, T)

    def ysent(buf, i):
        for side in (0, 1):
            wait_for(buf.at[pl.ds(0, 96)], y_s.at[i, side])

    def ag_go(buf, idx):
        for c, side, slot in ((0, 0, 0), (1, 1, 1), (1, 0, 2), (0, 1, 3)):
            blk = buf.at[own, COLS[c]]
            remote(blk, blk, y_s.at[idx, side], y_r.at[idx, slot], (right, left)[side]).start()

    @named("y pass on")
    def ag_pass(buf, idx):
        for side, d in ((0, 3), (1, 1)):
            wait_for(buf.at[pl.ds(0, T), COLS[side]], y_r.at[idx, side])
            blk = buf.at[rows_of(d), COLS[side]]
            remote(blk, blk, y_s.at[idx, side], y_r.at[idx, 2 + side], (right, left)[side]).start()

    @named("y wait")
    def ag_end(buf, idx):
        for slot in (2, 3):
            wait_for(buf.at[pl.ds(0, T)], y_r.at[idx, slot])
        ysent(buf, idx)

    def go(cps):
        for c in cps:
            c.start()

    @named("y wait")
    def end(cps):
        for c in cps:
            c.wait()

    def reduce_go(idx, name, product):
        def tile(i):
            c = span(i, 768)
            pf[:, c] = product(c)
            sb[0, :, c] = pf[rows_of(2), c].astype(BF)
            remote(sb.at[0, :, c], rb.at[idx % 2, 2, :, c], y_s.at[8 + idx, i], y_r.at[8 + idx, i], ypeer(1 + 2 * i)).start()
            sb[1, :, c] = pf[rows_of(3 - 2 * i), c].astype(BF)
            remote(sb.at[1, :, c], rb.at[idx % 2, 1 - i, :, c], y_s.at[8 + idx, 1 - i], y_r.at[8 + idx, 3 - i],
                   ypeer(3 - 2 * i)).start()
        tile.__name__ = name
        tiles(2, tile)

    @named("y pass on")
    def reduce_pass(idx):
        for side, d in ((0, 1), (1, 3)):
            c = (LEFT, RIGHT)[side]
            wait_for(rb.at[idx % 2, 2, :, COLS[side]], y_r.at[8 + idx, side])
            sb[2, :, c] = (pf[rows_of(d), c] + rb[idx % 2, 2, :, c].astype(F32)).astype(BF)
            remote(sb.at[2, :, COLS[side]], rb.at[idx % 2, side, :, COLS[side]], y_s.at[8 + idx, side],
                   y_r.at[8 + idx, 2 + side], (right, left)[side]).start()

    @named("y wait")
    def reduce_end(idx):
        for side in (0, 1):
            wait_for(rb.at[idx % 2, side], y_r.at[8 + idx, 2 + side])
        ysent(gall, 8 + idx)
        return pf[own, :] + rb[idx % 2, 0].astype(F32) + rb[idx % 2, 1].astype(F32)

    livef = jnp.where(lax.broadcasted_iota(jnp.int32, (T, D), 0).astype(F32) < length, 1.0, 0.0)

    def put_result(l, ref, value, way):
        @pl.when(s == l)
        def _():
            ref[pl.ds(s, 1)] = value[None]

        @pl.when(s != l)
        def _():
            ostage[way] = value
            remote(ostage.at[way], ref.at[s], x_s.at[way], x_r.at[way], sib).start()

    @named("last results")
    def finish_results():
        for way, ref in enumerate((act_out, ig_out)):
            remote(ostage.at[way], ref.at[s], x_s.at[way], x_r.at[way], sib).wait()

    def nothing():
        pass

    def forward(l, hidden, hooks):
        hook = lambda name: hooks.get(name, nothing)()
        if l:
            with jax.named_scope("norm first"):
                xh, rsd = stats(hidden)
                xh1[l] = xh
                rd1[l] = jnp.broadcast_to(rsd, (T, 128))
                normed[l, own, :] = (xh * small[l, 0:1, :] + small[l, 1:2, :]).astype(BF)
            ag_go(normed.at[l], l * 2)
            hook("normed")
            ag_pass(normed.at[l], l * 2)
            hook("normed2")
            ag_end(normed.at[l], l * 2)
        if l:
            wcopy(PR, 1).wait()
        with jax.named_scope("queries keys values"):
            for part in range(3):
                joined = nn(normed[l], vp[:, part * HW:(part + 1) * HW]) + small[l, 7:8, part * HW:(part + 1) * HW]
                for h in range(3):
                    v = joined[:, h * 128:(h + 1) * 128]
                    if part < 2:
                        v = v * cos_ref[...] + pltpu.roll(v, 64, 1) * sin_ref[...]
                    qkv[l, :, part * HW + h * 128:part * HW + (h + 1) * 128] = v.astype(BF)
        hook("joined")
        with jax.named_scope("attention"):
            for h in range(3):
                q = qkv[l, :, h * 128:(h + 1) * 128]
                k = qkv[l, :, HW + h * 128:HW + (h + 1) * 128]
                v = qkv[l, :, 2 * HW + h * 128:2 * HW + (h + 1) * 128]
                sc = jnp.where(vis[...] > 0.5, nt(q, k) * SCALE, MASKED)
                top = jnp.max(sc, axis=-1, keepdims=True)
                ex = jnp.exp(sc - top)
                p = ex * (1.0 / jnp.sum(ex, axis=-1, keepdims=True))
                probs[l, h] = p
                mixed[l, :, h * 128:(h + 1) * 128] = nn(p.astype(BF), v).astype(BF)
        if l:
            wcopy(OU, 1).wait()
        reduce_go(l * 2, "out_tile", lambda c: nn(mixed[l], vo[:, c]))
        hook("mixed")
        reduce_pass(l * 2)
        hook("mixed2")
        middle = hidden + reduce_end(l * 2) + small[l, 2:3, :]
        with jax.named_scope("norm second"):
            xh, rsd = stats(middle)
            xh2[l] = xh
            rd2[l] = jnp.broadcast_to(rsd, (T, 128))
            ns[l, own, :] = (xh * small[l, 3:4, :] + small[l, 4:5, :]).astype(BF)
            keep[...] = middle
        ag_go(ns.at[l], l * 2 + 1)
        hook("second")
        ag_pass(ns.at[l], l * 2 + 1)
        hook("second2")
        ag_end(ns.at[l], l * 2 + 1)
        if l:
            wcopy(EX, 1).wait()

        def up_tile(i):
            c = span(i, 256)
            u = nn(ns[l], ve[:, c]) + small[l, 6:7, c]
            unit = lax.broadcasted_iota(jnp.int32, (1, 256), 1) + (i * 256 + D * t)
            m = jnp.where(unit < width, 1.0, 0.0)
            u2 = u * u
            th = jnp.tanh(GC * u * (1.0 + 0.044715 * u2))
            half = 0.5 * (1.0 + th)
            active[l, :, c] = (u * half * m).astype(BF)
            gder[l, :, c] = m * (half + 0.5 * u * (1.0 - th * th) * (GC * (1.0 + 3 * 0.044715 * u2)))
        tiles(6, up_tile)
        hook("upper")
        if l:
            wcopy(SH, 1).wait()
        reduce_go(l * 2 + 1, "down_tile", lambda c: nn(active[l], vs[:, c]))
        if l == 0:
            hook("down")
            reduce_pass(1)
            hook("down2")
            return out_rows(0)

    def out_rows(l):
        result = (keep[...] + reduce_end(l * 2 + 1) + small[l, 5:6, :]) * livef
        result = result.astype(BF)
        put_result(l, act_out, result, 0)
        return result

    def norm_back(dn, xh, rsd, gain):
        e = dn * gain
        return rsd[:, 0:1] * (e - jnp.mean(e, axis=-1, keepdims=True)
                              - xh * jnp.mean(e * xh, axis=-1, keepdims=True))

    def backward(l, g, hooks):
        hook = lambda name: hooks.get(name, nothing)()
        g32 = g.astype(F32)
        smt[l, 5:6, :] = colsum(g32)
        if l == 0:
            gall[own, :] = g
        if l == 0:
            ag_go(gall, 4)
            hook("grad")
            ag_pass(gall, 4)
            hook("grad2")
            ag_end(gall, 4)

        def gs_tile(i):
            c = span(i, 256)
            gbuf(l, SH)[c, :] = tn(active[l, :, c], gall[...]).astype(BF)

        def dact_tile(i):
            c = span(i, 256)
            da = nt(gall[...], vs[c, :]) * gder[l, :, c]
            da = da.astype(BF)
            dup[:, c] = da
            smt[l, 6:7, c] = colsum(da.astype(F32))

        def ge_tile(i):
            c = span(i, 256)
            gbuf(l, EX)[c, :] = tn(ns[l, :, c], dup[...]).astype(BF)

        if l == 0:
            wcopy(SH, 0).wait()
            tiles(6, dact_tile)
            wcopy(EX, 0).wait()
        else:
            end(g_cps)
            tiles(6, gs_tile)
            sum0_go(1, SH)
            tiles(6, dact_tile)
            wcopy(SH, 0).start()
            hook("result")
            reduce_pass(3)
            hook("result2")
            out_rows(1)
        reduce_go(4 + l * 2, "e_tile", lambda c: nt(dup[...], ve[c, :]))
        if l == 1:
            wcopy(EX, 0).start()
        else:
            tiles(6, gs_tile)
            sum0_go(0, SH)
        tiles(6, ge_tile)
        sum0_go(l, EX)
        hook("upper")
        reduce_pass(4 + l * 2)
        hook("upper2")
        dn = reduce_end(4 + l * 2)
        with jax.named_scope("norm second back"):
            smt[l, 3:4, :] = colsum(dn * xh2[l])
            smt[l, 4:5, :] = colsum(dn)
            dmid = g32 + norm_back(dn, xh2[l], rd2[l], small[l, 3:4, :])
            db = dmid.astype(BF)
            smt[l, 2:3, :] = colsum(db.astype(F32))
            keep[...] = dmid
            dball[own, :] = db
        ag_go(dball, 4 + l * 2 + 1)
        hook("middle")
        ag_pass(dball, 4 + l * 2 + 1)
        hook("middle2")
        ag_end(dball, 4 + l * 2 + 1)
        if l == 0:
            wcopy(OU, 0).wait()
        dmix[...] = nt(dball[...], vo[...]).astype(BF)
        if l == 1:
            wcopy(OU, 0).start()
        with jax.named_scope("attention back"):
            for h in range(3):
                c = slice(h * 128, (h + 1) * 128)
                q = qkv[l, :, h * 128:(h + 1) * 128]
                k = qkv[l, :, HW + h * 128:HW + (h + 1) * 128]
                v = qkv[l, :, 2 * HW + h * 128:2 * HW + (h + 1) * 128]
                p = probs[l, h]
                dm = dmix[:, c]
                dj[:, 2 * HW + h * 128:2 * HW + (h + 1) * 128] = tn(p.astype(BF), dm).astype(BF)
                dp = nt(dm, v)
                dsc = (p * (dp - jnp.sum(dp * p, axis=-1, keepdims=True))).astype(BF)
                for part, v in ((0, nn(dsc, k)), (1, tn(dsc, q))):
                    v = v * SCALE
                    v = v * cos_ref[...] - pltpu.roll(v, 64, 1) * sin_ref[...]
                    dj[:, part * HW + h * 128:part * HW + (h + 1) * 128] = v.astype(BF)
        smt[l, 7:8, :] = jnp.zeros((1, D), F32)
        smt[l, 7:8, 0:QW] = colsum(dj[...].astype(F32))
        if l == 0:
            wcopy(PR, 0).wait()

        def gp_tile(i):
            c = span(i, 256)
            gbuf(l, PR)[c, :] = tn(normed[l, :, c], dj[...]).astype(BF)
        tiles(6, gp_tile)
        sum0_go(l, PR)
        reduce_go(4 + l * 2 + 1, "d_tile", lambda c: nt(dj[...], vp[c, :]))
        if l == 1:
            wcopy(PR, 0).start()
        with jax.named_scope("output term"):
            gbuf(l, OU)[...] = tn(mixed[l], dball[...]).astype(BF)
        sum0_go(l, OU)
        hook("joined")
        reduce_pass(4 + l * 2 + 1)
        hook("joined2")
        dn = reduce_end(4 + l * 2 + 1)
        with jax.named_scope("norm first back"):
            smt[l, 0:1, :] = colsum(dn * xh1[l])
            smt[l, 1:2, :] = colsum(dn)
            dh = keep[...] + norm_back(dn, xh1[l], rd1[l], small[l, 0:1, :])
            res = dh.astype(BF)
        put_result(l, ig_out, res, 1)
        return res

    hall = dball
    hall[own, :] = win_ref[s]
    h_cps = [remote(hall.at[own], hall.at[own], m_s.at[d - 1], m_r.at[d - 1], ypeer(d)) for d in (1, 2, 3)]
    g_cps = [remote(gall.at[own], gall.at[own], m_s.at[2 + d], m_r.at[2 + d], ypeer(d)) for d in (1, 2, 3)]
    pack_last = remote(allp.at[s], allp.at[s], p_s.at[3, 0], p_r.at[3, 0], sib)
    with jax.named_scope("greet wait"):
        pl.semaphore_wait(bar, 20)
    pack_go(0)
    go(lcs)

    @pl.when(first)
    def _():
        for m in moves[:4]:
            send_or_keep(*m)
    go(h_cps)
    gather_a(0, PR)

    @pl.when(first)
    def _():
        for m in moves[4:8]:
            send_or_keep(*m)
    for m in moves[12:]:
        send_or_keep(*m)
    pack_end(0)
    pack_go(1)
    gather_b(0, PR)
    gather_a(0, OU)
    pack_end(1)
    pack_go(2)
    end(lcs)
    row = lax.broadcasted_iota(jnp.int32, (TG, TG), 0)
    col = lax.broadcasted_iota(jnp.int32, (TG, TG), 1)
    limit = jnp.zeros((1, TG), F32)
    blk = lax.broadcasted_iota(jnp.int32, (1, TG), 1) // T
    for r in range(4):
        one = lens[r][0:1, :]
        limit = jnp.where(blk == r, jnp.concatenate([one, one], axis=1), limit)
    ok = (row // T == col // T) & (col <= row) & ((col % T).astype(F32) < limit)
    vis[...] = jnp.where(ok, 1.0, 0.0)
    hidden0 = win_ref[s].astype(F32)
    xh, rsd = stats(hidden0)
    xh1[0] = xh
    rd1[0] = jnp.broadcast_to(rsd, (T, 128))
    gall[own, :] = (cot_ref[s].astype(F32) * livef).astype(BF)
    gather_f(0, PR)

    @pl.when(first)
    def _():
        for m in moves[8:12]:
            send_or_keep(*m)
    gather_b(0, OU)
    pack_end(2)
    pack_last.start()
    gather_c(0, PR)
    gather_a(0, EX)
    gather_a(0, SH)
    gather_f(0, OU)
    go(g_cps)
    end(h_cps)
    pack_last.wait()

    def spread(rows, width, total):
        n = lax.broadcasted_iota(jnp.int32, (128, total), 1)
        i = lax.broadcasted_iota(jnp.int32, (128, total), 0)
        pick = jnp.where(n - (n // width) * width == i, 1.0, 0.0).astype(BF)
        wide = nn(rows.astype(BF), pick)
        n = lax.broadcasted_iota(jnp.int32, (64, total), 1)
        c = lax.broadcasted_iota(jnp.int32, (64, total), 0)
        return colsum(jnp.where(n // width == c, wide, 0.0))

    @named("spread")
    def unpack(l, wanted):
        for r in wanted:
            if r < 6:
                small[l, r:r + 1, :] = spread(allp[l, :, r, :], 24, D)
            elif r == 6:
                mine = allp[l, at(16 * t, 16, 16), 6, :]
                n = lax.broadcasted_iota(jnp.int32, (128, D), 1)
                i = lax.broadcasted_iota(jnp.int32, (128, D), 0)
                pick = jnp.where(n - (n // 96) * 96 == i, 1.0, 0.0).astype(BF)
                wide = nn(mine.astype(BF), pick)
                n = lax.broadcasted_iota(jnp.int32, (16, D), 1)
                c = lax.broadcasted_iota(jnp.int32, (16, D), 0)
                small[l, 6:7, :] = colsum(jnp.where(n // 96 == c, wide, 0.0))
            else:
                n = lax.broadcasted_iota(jnp.int32, (128, QW), 1)
                i = lax.broadcasted_iota(jnp.int32, (128, QW), 0)
                n = n + (n // HW) * (D - HW) + HW * t
                pick = jnp.where(n - (n // 72) * 72 == i, 1.0, 0.0).astype(BF)
                wide = nn(allp[l, :, 7, :].astype(BF), pick)
                n = lax.broadcasted_iota(jnp.int32, (64, QW), 1)
                c = lax.broadcasted_iota(jnp.int32, (64, QW), 0)
                n = n + (n // HW) * (D - HW) + HW * t
                small[l, 7:8, 0:QW] = colsum(jnp.where(n // 72 == c, wide, 0.0))

    unpack(0, (0, 1, 7))

    def norm_tile(i):
        rows = span(i, T)
        wide, _ = stats(hall[rows, :].astype(F32))
        normed[0, rows, :] = (wide * small[0, 0:1, :] + small[0, 1:2, :]).astype(BF)
    tiles(4, norm_tile)
    gather_b(0, EX)
    gather_c(0, OU)
    gather_d(0, PR)

    def steps(*todo):
        def run():
            for what, *args in todo:
                what(*args)
        return run

    def second_shards():
        @pl.when(jnp.logical_not(first))
        def _():
            for m in moves[8:12]:
                send_or_keep(*m)

    def reload(k):
        gather_drain(0, k)
        save(k).wait()
        gather_d(1, k)
        wcopy(k, 1).start()

    ga, gb, gf, gc, gd = gather_a, gather_b, gather_f, gather_c, gather_d
    def second_first():
        @pl.when(jnp.logical_not(first))
        def _():
            for m in moves[:8]:
                send_or_keep(*m)

    first_hooks = dict(
        joined=steps((gb, 0, SH), (gd, 0, OU)),
        mixed=steps((second_first,), (unpack, 0, (2, 3, 4, 5, 6))),
        mixed2=steps((gf, 0, EX), (second_shards,), (ga, 1, PR), (ga, 1, OU), (gc, 0, EX)),
        second=steps((gf, 0, SH)),
        second2=steps((gb, 1, PR), (ga, 1, EX), (gc, 0, SH), (gd, 0, EX)),
        upper=steps((gb, 1, OU), (gd, 0, SH)),
        down=steps((unpack, 1, (0, 1, 2, 3, 4, 5, 6, 7)), (ga, 1, SH)),
        down2=steps((gf, 1, PR), (gb, 1, EX), (gf, 1, OU), (gc, 1, PR)))
    second_hooks = dict(
        normed2=steps((gb, 1, SH), (gc, 1, OU), (gf, 1, EX), (reload, PR)),
        joined=steps((reload, OU)),
        mixed2=steps((gc, 1, EX), (gf, 1, SH)),
        second2=steps((gc, 1, SH), (reload, EX)),
        upper=steps((reload, SH)))
    a1 = forward(0, hidden0, first_hooks)
    forward(1, a1.astype(F32), second_hooks)

    for k in range(4):
        gather_drain(1, k)
    for m in moves:
        sent(*m)

    load, fin, mid, last = sum0_load, sum0_fin, sum1_mid, sum1_end
    ig2 = backward(1, gall[own, :], dict(
        result2=steps((load, 1, SH), (fin, 1, SH)),
        upper2=steps((mid, 1, SH), (load, 1, EX), (fin, 1, EX)),
        middle2=steps((last, 1, SH), (mid, 1, EX)),
        joined=steps((load, 1, PR), (fin, 1, PR)),
        joined2=steps((load, 1, OU), (last, 1, EX), (fin, 1, OU))))
    g1 = (ig2.astype(F32) * livef).astype(BF)
    backward(0, g1, dict(
        grad=steps((sum2_end, 1, SH), (sum_drain, 1, SH)),
        grad2=steps((mid, 1, PR), (mid, 1, OU), (sum2_end, 1, EX)),
        upper2=steps((load, 0, SH), (last, 1, PR), (fin, 0, SH)),
        middle=steps((load, 0, EX), (last, 1, OU), (fin, 0, EX)),
        middle2=steps((mid, 0, SH), (sum2_end, 1, PR)),
        joined=steps((load, 0, PR), (fin, 0, PR)),
        joined2=steps((load, 0, OU), (mid, 0, EX), (fin, 0, OU), (last, 0, SH))))
    vec_go(0)
    vec_end(0)
    vec_go(1)
    last(0, EX)
    mid(0, PR)
    mid(0, OU)
    sum2_end(1, OU)
    sum2_end(0, SH)
    vec_end(1)
    vec_go(2)
    last(0, PR)
    last(0, OU)
    sum2_end(0, EX)
    vec_end(2)
    vec_go(3)
    sum2_end(0, PR)
    sum2_end(0, OU)
    vec_end(3)
    finish_weights()
    finish_results()
    for k in range(4):
        for l in (0, 1):
            if (l, k) != (1, SH):
                sum_drain(l, k)


def finish_kernel(act, ig, sums, fp, fo, fe, fs,
                  act_out, ig_out, o0, o1, d_pw, o7, d_ow, o2, o3, o4, d_ew, o6, d_sw, o5):
    chip = lax.axis_index("dp")
    act_out[0, :, 0] = act[...]
    ig_out[0, :, 0] = ig[...]
    for r in range(4):
        for p in range(3):
            d_pw[0, :, p * D + HW * r:p * D + HW * (r + 1)] = fp[r, :, HW * p:HW * (p + 1)].astype(F32)[:24]
        d_ow[0, :, HW * r:HW * (r + 1)] = fo[r].astype(F32)[:24]
        d_ew[0, :, D * r:D * (r + 1)] = fe[r].astype(F32)[:24]
    for j in range(2):
        d_sw[0, :, 768 * j:768 * (j + 1)] = fs[j].astype(F32)
    total = sums[0] + sums[1] + sums[2] + sums[3]
    mine = pltpu.roll(total, (D - 24 * chip) % D, 1)
    for r, o in enumerate((o0, o1, o2, o3, o4, o5)):
        o[...] = mine[r:r + 1, :24]
    units = sums[chip // 16]
    o6[...] = pltpu.roll(units, (D - 96 * (chip % 16)) % D, 1)[6:7, :96]
    cols = jnp.concatenate([sums[r, :, HW * p:HW * (p + 1)] for p in range(3) for r in range(4)], axis=1)
    o7[...] = pltpu.roll(cols, (3 * D - 72 * chip) % (3 * D), 1)[7:8, :72]


def core_call(*args):
    sd = jax.ShapeDtypeStruct
    V = pltpu.VMEM
    DMA = pltpu.SemaphoreType.DMA
    hbm = [sd((2,) + f, BF) for f in FULL]
    hbm += [sd((2, 2, HW, QW), BF), sd((2, 2, HW, HW), BF), sd((2, 2, HW, D), BF), sd((2, D, 768), BF)]
    hbm += [sd((2, 3, 4 * f[0], f[1]), BF) for f in SLAB]
    hbm += [sd((2, 3) + f, BF) for f in SLAB]
    out = pl.pallas_call(
        core_kernel,
        out_shape=[sd((2, T, D), BF), sd((2, T, D), BF), sd((4, 8, D), F32),
                   sd((4, 32, QW), BF), sd((4, 32, HW), BF), sd((4, 32, D), BF), sd((2, 96, 768), BF)] + hbm,
        in_specs=[VM] * 2 + [pl.BlockSpec(memory_space=pltpu.SMEM)] * 2 + [VM] * 14,
        out_specs=[VM] * 7 + [ANY] * 16,
        scratch_shapes=[
            V((D, QW), BF), V((HW, D), BF), V((D, D), BF), V((D, D), BF),
            V((D, QW), BF), V((HW, D), BF), V((D, D), BF), V((D, D), BF),
            V((2, TG, D), BF), V((2, TG, D), BF), V((TG, D), BF), V((TG, D), BF),
            V((2, TG, QW), BF), V((2, 3, TG, TG), F32), V((2, TG, HW), BF),
            V((2, TG, D), F32), V((2, TG, D), BF),
            V((2, T, D), F32), V((2, T, D), F32), V((2, T, 128), F32), V((2, T, 128), F32),
            V((TG, D), F32), V((3, T, D), BF), V((2, 3, T, D), BF),
            V((TG, D), BF), V((TG, QW), BF), V((TG, HW), BF), V((TG, TG), F32), V((4, 8, 128), F32),
            V((T, D), F32), V((2, T, D), BF),
            V((4, 32, QW), BF), V((4, 32, HW), BF), V((4, 32, D), BF),
            V((2, 2, 32, QW), BF), V((2, 2, 32, HW), BF), V((2, 2, 32, D), BF), V((2, 96, 768), BF),
            V((2, 48, QW), BF), V((2, 48, HW), BF), V((2, 48, D), BF),
            V((2, 96, 768), BF),
            V((768, D), BF), V((576, D), BF), V((2, 64, 8, 128), F32), V((2, 8, D), F32), V((5, 8, D), F32), V((3, 3, 8, D), F32),
            DMA((16, 2)), DMA((16, 4)), DMA((4,)), DMA((4,)), DMA((4,)), DMA((3,)), DMA((3,)),
            DMA((3, 4)), DMA((2,)), DMA((3, 2, 2)), DMA((2,)), DMA((4, 3)), DMA((4, 3)),
            DMA((2, 4)), DMA((2, 4)), DMA((2, 4)), DMA((2, 2, 4)), DMA((2, 4)), DMA((2, 4)), DMA((2, 4)),
            DMA((2, 4)), DMA((2, 4)), DMA((2, 4)), DMA((2, 4)), DMA((2, 4)), DMA((2, 4)), DMA((8,)),
            DMA((2, 4, 2)), DMA((4, 4)), DMA((4, 3)), DMA((4, 3)), DMA((6,)), DMA((6,)), pltpu.SemaphoreType.REGULAR, DMA((2, 4)), DMA((2, 4)), DMA((4,)),
        ],
        compiler_params=pltpu.CompilerParams(collective_id=1, has_side_effects=True,
                                             vmem_limit_bytes=64 * 2**20 - 2**16),
    )(*args)
    return out[:7]


def finish_call(*args):
    def sd(*shape):
        return jax.ShapeDtypeStruct(shape, F32)
    rows = jax.ShapeDtypeStruct((1, 2, 1, T, D), BF)
    row = sd(1, 24)
    return pl.pallas_call(
        finish_kernel,
        out_shape=[rows, rows, row, row, sd(1, 24, 3 * D), sd(1, 72), sd(1, 24, D), row, row, row,
                   sd(1, 24, 4 * D), sd(1, 96), sd(1, 96, D), row],
        in_specs=[VM] * 7,
        out_specs=[VM] * 14,
        compiler_params=pltpu.CompilerParams(vmem_limit_bytes=64 * 2**20 - 2**16),
    )(*args)


def rotary():
    half = 64
    rates = (np.float32(10000.0) ** (-np.arange(half, dtype=np.float32) / np.float32(half))).astype(np.float32)
    ang = np.arange(T, dtype=np.float32)[:, None] * rates[None, :]
    cos, sin = np.cos(ang), np.sin(ang)
    cos2 = np.concatenate([cos, cos], axis=1)
    sin2 = np.concatenate([-sin, sin], axis=1)
    return np.tile(cos2, (4, 1)).astype(np.float32), np.tile(sin2, (4, 1)).astype(np.float32)


def per_device(window_input, cotangent, lengths, widths, gain_first, shift_first, project_weight, project_bias,
               output_weight, output_bias, gain_second, shift_second, expand_weight, expand_bias,
               shrink_weight, shrink_bias):
    cos2, sin2 = rotary()
    parts = core_call(
        window_input[:, 0], cotangent[:, 0], lengths, widths, gain_first, shift_first, output_bias, gain_second,
        shift_second, shrink_bias, expand_bias, project_bias, jnp.asarray(cos2), jnp.asarray(sin2),
        project_weight, output_weight, expand_weight, shrink_weight)
    return tuple(finish_call(*parts))


def solution(mesh):
    row = P("section", "dp")
    mat = P("section", "dp", None)
    params = (row, row, mat, row, mat, row, row, row, mat, row, mat, row)
    seq = P(None, "dp", None, None)
    out = P("section", None, "dp", None, None)
    return jax.shard_map(
        per_device, mesh=mesh,
        in_specs=(seq, seq, P(None, "dp"), P()) + params,
        out_specs=(out, out) + params,
        check_vma=False,
    )
```

```python
import jax
import jax.numpy as jnp
import numpy as np
from jax import lax
from jax.experimental import pallas as pl
from jax.experimental.pallas import tpu as pltpu
from jax.sharding import PartitionSpec as P

MESH = pl.DeviceIdType.MESH
ANY = pl.BlockSpec(memory_space=pl.ANY)
VM = pl.BlockSpec(memory_space=pltpu.VMEM)
EPS = 1e-05
MASKED = -1e9
BF = jnp.bfloat16
F32 = jnp.float32
D = 1536
T = 64
TG = 256
HW = 384
QW = 1152
SCALE = 128 ** -0.5
GC = (2 / np.pi) ** 0.5
PR, OU, EX, SH = range(4)
PARTS = (4, 5, 6)
FULL = ((D, QW), (HW, D), (D, D), (D, D))
SLAB = ((48, QW), (48, HW), (48, D), (96, 768))


def nn(a, b):
    return jnp.dot(a, b, preferred_element_type=F32)


def nt(a, b):
    return lax.dot_general(a, b, (((1,), (1,)), ((), ())), preferred_element_type=F32)


def tn(a, b):
    return lax.dot_general(a, b, (((0,), (0,)), ((), ())), preferred_element_type=F32)


def tiles(count, body):
    def step(i, carry):
        body(i)
        return carry
    with jax.named_scope(body.__name__):
        lax.fori_loop(0, count, step, 0)


def span(i, size):
    return pl.ds(pl.multiple_of(i * size, size), size)


def at(start, size, unit):
    return pl.ds(pl.multiple_of(start, unit), size)


def stats(x):
    mean = jnp.mean(x, axis=-1, keepdims=True)
    c = x - mean
    var = jnp.mean(c * c, axis=-1, keepdims=True)
    rs = lax.rsqrt(var + EPS)
    return c * rs, rs


def named(name):
    def deco(fn):
        def inner(*args):
            with jax.named_scope(name):
                return fn(*args)
        return inner
    return deco


def colsum(v):
    return jnp.sum(v, axis=0, keepdims=True)


def to32(v):
    v = v.astype(F32)
    return jnp.concatenate([v, jnp.zeros((8, v.shape[1]), F32)], axis=0).astype(BF)


def core_kernel(win_ref, cot_ref, len_ref, wid_ref, v0, v1, v2, v3, v4, v5, v6, v7, cos_ref, sin_ref, pw, ow, ew, sw,
                act_out, ig_out, sm_out, fp, fo, fe, fs,
                wp, wo, we, ws, r0p, r0o, r0e, r0s, r1p, r1o, r1e, r1s, r2p, r2o, r2e, r2s,
                vp, vo, ve, vs, up, uo, ue, us_,
                normed, ns, gall, dball, qkv, probs, mixed, gder, active, xh1, xh2, rd1, rd2,
                pf, sb, rb, dup, dj, dmix, vis, lens, keep, ostage,
                sp, so, se, cp, co, ce, cs, bp, bo, be, fss,
                tmp, tmp1, allp, small, smt, sme,
                y_s, y_r, w_sem, x_s, x_r, l_s, l_r, z_s, zo_s, z_r, zs_r, p_s, p_r,
                a_s, a_r, b_s, b_r, c_s, c_r, o_sem, q0_s, q0_r, q1_s, q1_r, q2_s, q2_r, t_sem,
                f_s, f_r, e_s, e_r, m_s, m_r, token, f2_r, qf_r, v_sem):
    s = lax.axis_index("section")
    chip = lax.axis_index("dp")
    y, x, z = chip // 16, (chip // 4) % 4, chip % 4
    t = y
    zp = z % 2
    zh = z // 2
    first = s == 0

    def dev(core, cy, cx, cz):
        return (core, cy * 16 + cx * 4 + cz)

    def ypeer(d):
        return dev(s, (y + d) % 4, x, z)

    class Axes:
        def __init__(self, straight):
            self.straight = straight
            self.a, self.b = self.grid(x, z)

        def grid(self, a, b):
            return jnp.where(self.straight, a, b), jnp.where(self.straight, b, a)

        def apeer(self, d):
            cx, cz = self.grid((self.a + d) % 4, self.b)
            return dev(s, y, cx, cz)

        def bpeer(self, d):
            cx, cz = self.grid(self.a, (self.b + d) % 4)
            return dev(s, y, cx, cz)

    crossed, same = Axes(first), Axes(False)
    gather_axes = (crossed, same, crossed, crossed, crossed, crossed, crossed)
    sum_axes = (crossed, crossed, crossed, crossed)

    sib = dev(1 - s, y, x, z)
    own = at(t * T, T, T)

    bar = pltpu.get_barrier_semaphore()

    def greet(who):
        pl.semaphore_signal(bar, inc=1, device_id=who, device_id_type=MESH)

    with jax.named_scope("greet"):
        for d in (1, 2, 3):
            for core in (s, 1 - s):
                greet(dev(core, (y + d) % 4, x, z))
        for d in (0, 1, 2, 3):
            for core in (s, 1 - s):
                greet(dev(core, (y + d) % 4, x, 2 * zh + 1 - zp))
        greet(sib)
        for d in (1, 2, 3):
            greet(dev(s, y, (x + d) % 4, z))
        for d in (0, 1):
            greet(dev(s, y, x, 2 * (1 - zh) + d))

    def remote(src, dst, ssem, rsem, who):
        return pltpu.make_async_remote_copy(src_ref=src, dst_ref=dst, send_sem=ssem, recv_sem=rsem,
                                            device_id=who, device_id_type=MESH)

    def wait_for(ref, sem):
        pltpu.make_async_copy(ref, ref, sem).wait()

    w_hbm = (wp, wo, we, ws)
    w_v = (vp, vo, ve, vs)
    g_v = (up, uo, ue, us_)
    r0 = (r0p, r0o, r0e, r0s)
    r1 = (r1p, r1o, r1e, r1s)
    r2 = (r2p, r2o, r2e, r2s)

    def slab_at(k, j, cx, cz):
        if k not in (OU, SH):
            half = 1 - cz % 2 if k == EX else cz % 2
            return at(48 * (8 * (2 * half + j) + 2 * cx + cz // 2), 48, 48), slice(None)
        if k == OU:
            return at(48 * (2 * cx + cz // 2), 48, 48), at(HW * (2 * (cz % 2) + j), HW, HW)
        return at(96 * (4 * cx + cz), 96, 96), at(768 * j, 768, 768)

    def slab_of(ref, k, axes, a, b):
        cx, cz = axes.grid(a, b)
        return ref.at[slab_at(k, s, cx, cz)]

    def parts_of(ref, k, j):
        if k not in (OU, SH):
            return [ref.at[at(HW * (2 * p + j), HW, HW)] for p in (0, 1)]
        if k == OU:
            return [ref.at[:, at(HW * (2 * p + j), HW, HW)] for p in (0, 1)]
        return [ref.at[:, at(768 * j, 768, 768)]]

    def bulk(ref, k, slabs):
        if k == OU:
            return ref.at[pl.ds(0, 12 * slabs)] if slabs > 3 else ref.at[pl.ds(0, 144), pl.ds(0, HW)]
        return ref.at[pl.ds(0, 48 * slabs)]

    def piece_target(yt, half):
        return dev(y % 2, yt, x, 2 * zh + half), (yt == y) & (s == y % 2) & (zp == half)

    def out_target(q):
        return dev(q % 2, y, x, 2 * zh + q // 2), (zp == q // 2) & (s == q % 2)

    def send_or_keep(src, dst, ssem, rsem, who, is_me):
        @pl.when(is_me)
        def _():
            pltpu.make_async_copy(src, dst, rsem).start()

        @pl.when(jnp.logical_not(is_me))
        def _():
            remote(src, dst, ssem, rsem, who).start()

    def sent(src, dst, ssem, rsem, who, is_me):
        @pl.when(jnp.logical_not(is_me))
        def _():
            remote(src, dst, ssem, rsem, who).wait_send()

    def shard_moves():
        out = []
        for yt in range(4):
            who, me = piece_target(yt, y // 2)
            out.append((sp.at[yt], cp.at[s, zp], z_s.at[0, yt], z_r.at[0, s, zp], who, me))
        for q in range(4):
            who, me = out_target(q)
            out.append((so.at[q], co.at[s, zp], z_s.at[1, q], z_r.at[1, s, zp], who, me))
        for yt in range(4):
            who, me = piece_target(yt, 1 - y // 2)
            out.append((se.at[yt], ce.at[s, zp], z_s.at[2, yt], z_r.at[2, s, zp], who, me))
        for j in range(2):
            out.append((sw.at[0, :, pl.ds(768 * j, 768)], cs.at[s], zo_s.at[j], zs_r.at[s],
                        dev(j, y, x, z), s == j))
        return out

    moves = shard_moves()
    with jax.named_scope("shards"):
        for yt in range(4):
            sp[yt] = to32(jnp.concatenate([pw[0, :, p * D + HW * yt:p * D + HW * (yt + 1)] for p in range(3)], axis=1))
        for q in range(4):
            so[q] = to32(ow[0, :, HW * q:HW * (q + 1)])
        for yt in range(4):
            se[yt] = to32(ew[0, :, D * yt:D * (yt + 1)])

    spot = (chip % 16) * 4 + y
    allp[s, pl.ds(spot, 1)] = jnp.zeros((1, 8, 128), F32)
    for r, v in enumerate((v0, v1, v2, v3, v4, v5, v6, v7)):
        allp[s, pl.ds(spot, 1), r:r + 1, 0:v.shape[1]] = v[...].astype(F32)[None]

    def pack_copies(stage):
        out = []
        for d in (1, 2, 3):
            if stage == 0:
                blk, who = allp.at[s, pl.ds(spot, 1)], ypeer(d)
            elif stage == 1:
                blk, who = allp.at[s, at(spot - y, 4, 4)], dev(s, y, x, (z + d) % 4)
            else:
                blk, who = allp.at[s, at(16 * x, 16, 16)], dev(s, y, (x + d) % 4, z)
            out.append(remote(blk, blk, p_s.at[stage, d - 1], p_r.at[stage, d - 1], who))
        return out

    @named("pack go")
    def pack_go(stage):
        for c in pack_copies(stage):
            c.start()

    @named("pack wait")
    def pack_end(stage):
        for c in pack_copies(stage):
            c.wait()

    length = len_ref[s].astype(F32)
    width = wid_ref[s]
    lens[pl.ds(t, 1)] = jnp.full((1, 8, 128), length, F32)
    lcs = [remote(lens.at[pl.ds(t, 1)], lens.at[pl.ds(t, 1)], l_s.at[d - 1], l_r.at[d - 1], ypeer(d)) for d in (1, 2, 3)]

    got = (cp, co, ce, cs)
    bld = (bp, bo, be, cs)

    def home(l, k):
        if k in PARTS:
            return w_v[PR].at[:, pl.ds(HW * (k - 4), HW)]
        return w_hbm[k].at[1] if l else w_v[k]

    def slab_in(l, k):
        return bld[PR].at[l, :, pl.ds(HW * (k - 4), HW)] if k in PARTS else bld[k].at[l]

    def a_copies(l, k):
        src = slab_in(l, k)
        ax = gather_axes[k]
        return [remote(src, slab_of(home(l, k), k, ax, ax.a, ax.b), a_s.at[l, k], a_r.at[l, k], ax.apeer(d))
                for d in (1, 2, 3)]

    def own_copy(l, k):
        ax = gather_axes[k]
        return pltpu.make_async_copy(slab_in(l, k), slab_of(home(l, k), k, ax, ax.a, ax.b), o_sem.at[l, k])

    @named("gather a")
    def gather_a(l, k):
        if k == SH:
            wait_for(cs.at[l], zs_r.at[l])
        else:
            zk = (0, 1, 2)[k]
            for p in (0, 1):
                wait_for(got[k].at[l, p], z_r.at[zk, l, p])
            halves = [got[k][l, p].astype(F32)[:24] for p in (0, 1)]
            bld[k][l] = jnp.concatenate(halves, axis=0).astype(BF)
        for item in PARTS if (l, k) == (0, PR) else (k,):
            go(a_copies(l, item))
            own_copy(l, item).start()

    @named("gather b")
    def gather_b(l, k):
        w, ax = home(l, k), gather_axes[k]
        wait_for(bulk(w, k, 3), a_r.at[l, k])
        own_copy(l, k).wait()
        for a in range(4):
            src = slab_of(w, k, ax, a, ax.b)
            for side, d in ((0, 1), (1, 3)):
                remote(src, src, b_s.at[l, k], b_r.at[side, l, k], ax.bpeer(d)).start()

    @named("gather f")
    def gather_f(l, k):
        w, ax = home(l, k), gather_axes[k]
        for side, d in ((0, 1), (1, 3)):
            wait_for(bulk(w, k, 4), b_r.at[side, l, k])
            for a in (2 * side, 2 * side + 1):
                src = slab_of(w, k, ax, a, (ax.b + 4 - d) % 4)
                remote(src, src, b_s.at[l, k], f2_r.at[l, k], ax.bpeer(d)).start()

    @named("gather c")
    def gather_c(l, k):
        w = home(l, k)
        wait_for(bulk(w, k, 4), f2_r.at[l, k])
        for blk in parts_of(w, k, s):
            remote(blk, blk, c_s.at[l, k], c_r.at[l, k], sib).start()

    @named("gather d")
    def gather_d(l, k):
        wait_for(bulk(home(l, k), k, 16), c_r.at[l, k])
        if l == 0 and k not in (4, 5):
            save(PR if k == 6 else k).start()

    def save(k):
        return pltpu.make_async_copy(w_v[k], w_hbm[k].at[0], v_sem.at[k])

    @named("gather drain")
    def gather_drain(l, k):
        for item in PARTS if (l, k) == (0, PR) else (k,):
            w = home(l, item)
            wait_for(bulk(w, item, 3), a_s.at[l, item])
            wait_for(bulk(w, item, 12), b_s.at[l, item])
            wait_for(bulk(w, item, 16), c_s.at[l, item])

    def gbuf(l, k):
        if l == 0 and k == PR:
            return us_.at[:, pl.ds(0, QW)]
        if l == 0 and k == SH:
            return ue
        return g_v[k] if l else w_v[k]

    @named("sum0 go")
    def sum0_go(l, k):
        for i, blk in enumerate(parts_of(gbuf(l, k), k, 1 - s)):
            dst = r0[k].at[l, i] if k != SH else r0[k].at[l]
            remote(blk, dst, q0_s.at[l, k], q0_r.at[l, k], sib).start()

    def halves_tmp(k):
        if k in (PR, EX):
            return [tmp.at[pl.ds(HW * p, HW), pl.ds(0, FULL[k][1])] for p in (0, 1)]
        if k == OU:
            return [tmp.at[pl.ds(HW * p, HW), pl.ds(0, HW)] for p in (0, 1)]
        return [tmp.at[:, pl.ds(768 * p, 768)] for p in (0, 1)]

    def sum0_copies(l, k):
        srcs = [r0[k].at[l, i] for i in (0, 1)] if k != SH else [r0[k].at[l, pl.ds(768 * i, 768)] for i in (0, 1)]
        return [pltpu.make_async_copy(a, b, t_sem.at[i]) for i, (a, b) in enumerate(zip(srcs, halves_tmp(k)))]

    @named("sum0 load")
    def sum0_load(l, k):
        wait_for(r0[k].at[l], q0_r.at[l, k])
        for c in sum0_copies(l, k):
            c.start()

    @named("sum0")
    def sum0_fin(l, k):
        g, ax = gbuf(l, k), sum_axes[k]
        cps = sum0_copies(l, k)
        for p in (0, 1):
            cps[p].wait()

            def add(i):
                if k in (PR, EX):
                    rows, cols, n = at(HW * (2 * p + s) + 96 * i, 96, 96), slice(None), FULL[k][1]
                    other = tmp[pl.ds(pl.multiple_of(HW * p + 96 * i, 96), 96), 0:n]
                elif k == OU:
                    rows, cols = span(i, 96), at(HW * (2 * p + s), HW, HW)
                    other = tmp[pl.ds(pl.multiple_of(HW * p + 96 * i, 96), 96), 0:HW]
                else:
                    rows, cols = at(768 * p + 96 * i, 96, 96), at(768 * s, 768, 768)
                    other = tmp[span(i, 96), 768 * p:768 * p + 768]
                g[rows, cols] = (g[rows, cols].astype(F32) + other.astype(F32)).astype(BF)
            tiles(8 if k == SH else 4, add)
        for a in (0, 2, 1, 3):
            far = 1 if a < 2 else 3
            remote(slab_of(g, k, ax, a, (ax.b + 2) % 4), r1_slab(l, k, 0, a), q1_s.at[l, k], qf_r.at[l, k],
                   ax.bpeer(far)).start()
        for a in (0, 2, 1, 3):
            near = 3 if a < 2 else 1
            remote(slab_of(g, k, ax, a, (ax.b + near) % 4), r1_slab(l, k, near, a), q1_s.at[l, k], q1_r.at[l, k],
                   ax.bpeer(near)).start()

    def r1_slab(l, k, d, a):
        rows = SLAB[k][0]
        return r1[k].at[l, (0, 1, None, 2)[d], pl.ds(rows * a, rows)]

    def tmp_set(k, side):
        rows, cols = SLAB[k]
        if k == SH:
            return tmp1.at[pl.ds(0, 4 * rows), pl.ds(cols * side, cols)]
        return tmp1.at[pl.ds(4 * rows * side, 4 * rows), pl.ds(0, cols)]

    def tmp_slab(k, side, a):
        rows, cols = SLAB[k]
        if k == SH:
            return tmp1[at(rows * a, rows, rows), cols * side:cols * (side + 1)].astype(F32)
        return tmp1[at(4 * rows * side + rows * a, rows, rows), 0:cols].astype(F32)

    def mid_copies(l, k):
        rows, cols = SLAB[k]
        if k != SH:
            return [pltpu.make_async_copy(r1[k].at[l, 0], tmp1.at[pl.ds(384, 192), pl.ds(0, cols)], t_sem.at[2])]
        return [pltpu.make_async_copy(r1[k].at[l, 0, pl.ds(192 * i, 192)], tmp1.at[pl.ds(384, 192), pl.ds(768 * i, 768)],
                                      t_sem.at[(2, 8)[i]]) for i in (0, 1)]

    def mid_slab(k, a):
        rows, cols = SLAB[k]
        if k != SH:
            return tmp1[384 + 48 * a:432 + 48 * a, 0:cols].astype(F32)
        return tmp1[384 + 96 * (a % 2):480 + 96 * (a % 2), 768 * (a // 2):768 * (a // 2) + 768].astype(F32)

    @named("sum1 pass load")
    def mid_load(l, k):
        wait_for(r1[k].at[l, 0], qf_r.at[l, k])
        go(mid_copies(l, k))

    @named("sum1 pass on")
    def mid_fin(l, k):
        g, ax = gbuf(l, k), sum_axes[k]
        end(mid_copies(l, k))
        for a in range(4):
            d = 1 if a < 2 else 3
            cx, cz = ax.grid(a, (ax.b + d) % 4)
            where = slab_at(k, s, cx, cz)
            g[where] = (g[where].astype(F32) + mid_slab(k, a)).astype(BF)
            remote(g.at[where], r1_slab(l, k, d, a), q1_s.at[l, k], q1_r.at[l, k], ax.bpeer(d)).start()

    def last_copies(l, k):
        return [pltpu.make_async_copy(r1[k].at[l, 1 + i], tmp_set(k, i), t_sem.at[3 + i]) for i in (0, 1)]

    @named("sum1 load")
    def last_load(l, k):
        wait_for(r1[k].at[l, pl.ds(1, 2)], q1_r.at[l, k])
        go(last_copies(l, k))

    @named("sum1")
    def last_fin(l, k):
        g, ax = gbuf(l, k), sum_axes[k]
        end(last_copies(l, k))
        for da in (2, 1, 3, 0):
            a = (ax.a + da) % 4
            cx, cz = ax.grid(a, ax.b)
            where = slab_at(k, s, cx, cz)
            total = g[where].astype(F32) + tmp_slab(k, 0, a) + tmp_slab(k, 1, a)
            if da == 0:
                bld[k][l] = total.astype(BF)
            else:
                g[where] = total.astype(BF)
                remote(g.at[where], r2[k].at[l, da - 1], q2_s.at[l, k], q2_r.at[l, k], ax.apeer(da)).start()

    fsend = (sp, so, se, fss)
    frecv = (fp, fo, fe, fs)

    def last_moves(l, k):
        out = []
        if k == SH:
            out.append((fss.at[l], fs.at[s], f_s.at[l, k, 0], f_r.at[k, s], dev(l, y, x, z), s == l))
            return out
        for p in (0, 1):
            if k == OU:
                q = 2 * zp + s
                who, me, slot = dev(l, y, x, 2 * zh + p), (s == l) & (zp == p), q
            else:
                yo = 2 * (zp if k == PR else 1 - zp) + s
                who, me, slot = dev(l, yo, x, 2 * zh + p), (s == l) & (yo == y) & (zp == p), y
            out.append((fsend[k].at[2 * l + p], frecv[k].at[slot], f_s.at[l, k, p], f_r.at[k, slot], who, me))
        return out

    @named("sum2")
    def sum2_end(l, k):
        wait_for(r2[k].at[l], q2_r.at[l, k])
        rows, cols = SLAB[k]
        spots = [tmp1.at[pl.ds(rows * d, rows), pl.ds(0, cols)] for d in range(3)]
        cps = [pltpu.make_async_copy(r2[k].at[l, d], spots[d], t_sem.at[5 + d]) for d in range(3)]
        go(cps)
        end(cps)
        total = bld[k][l].astype(F32)
        for d in range(3):
            total = total + tmp1[rows * d:rows * (d + 1), 0:cols].astype(F32)
        if k == SH:
            fss[l] = total.astype(BF)
        else:
            for p in (0, 1):
                fsend[k][2 * l + p] = to32(total[24 * p:24 * (p + 1)])
        for m in last_moves(l, k):
            send_or_keep(*m)

    @named("sum drain")
    def sum_drain(l, k):
        wait_for(r0[k].at[l], q0_s.at[l, k])
        wait_for(r1[k].at[l], q1_s.at[l, k])
        wait_for(r2[k].at[l], q2_s.at[l, k])

    @named("last weights")
    def finish_weights():
        for l in (0, 1):
            for k in range(4):
                for m in last_moves(l, k):
                    sent(*m)
        for k in range(4):
            for i in range(2 if k == SH else 4):
                wait_for(frecv[k].at[i], f_r.at[k, i])

    def vec_copies(stage):
        out = []
        if stage == 0:
            out.append(remote(smt.at[1 - s], sme.at[0, 0], e_s.at[0, 0], e_r.at[0, 0], sib))
            return out
        for d in (1, 2, 3):
            if stage == 1:
                who = crossed.apeer(d)
            elif stage == 2:
                who = crossed.bpeer(d)
            else:
                out.append(remote(sm_out.at[t], sm_out.at[t], e_s.at[3, d - 1], e_r.at[3, d - 1], ypeer(d)))
                continue
            out.append(remote(smt.at[2 + stage], sme.at[stage, d - 1], e_s.at[stage, d - 1], e_r.at[stage, d - 1], who))
        return out

    @named("vectors go")
    def vec_go(stage):
        for c in vec_copies(stage):
            c.start()

    @named("vectors wait")
    def vec_end(stage):
        for c in vec_copies(stage):
            c.wait()
        if stage == 0:
            smt[3] = smt[pl.ds(s, 1)][0] + sme[0, 0]
        elif stage == 1:
            smt[4] = smt[3] + sme[1, 0] + sme[1, 1] + sme[1, 2]
        elif stage == 2:
            sm_out[pl.ds(t, 1)] = (smt[4] + sme[2, 0] + sme[2, 1] + sme[2, 2])[None]

    def wcopy(k, l):
        return pltpu.make_async_copy(w_hbm[k].at[l], w_v[k], w_sem.at[k])

    LEFT, RIGHT = slice(0, 768), slice(768, D)
    COLS = (pl.ds(0, 768), pl.ds(768, 768))
    right, left = ypeer(1), ypeer(3)

    def rows_of(d):
        return at((t + d) % 4 * T, T, T)

    def ysent(buf, i):
        for side in (0, 1):
            wait_for(buf.at[pl.ds(0, 96)], y_s.at[i, side])

    def ag_go(buf, idx):
        for c, side, slot in ((0, 0, 0), (1, 1, 1), (1, 0, 2), (0, 1, 3)):
            blk = buf.at[own, COLS[c]]
            remote(blk, blk, y_s.at[idx, side], y_r.at[idx, slot], (right, left)[side]).start()

    @named("y pass on")
    def ag_pass(buf, idx):
        for side, d in ((0, 3), (1, 1)):
            wait_for(buf.at[pl.ds(0, T), COLS[side]], y_r.at[idx, side])
            blk = buf.at[rows_of(d), COLS[side]]
            remote(blk, blk, y_s.at[idx, side], y_r.at[idx, 2 + side], (right, left)[side]).start()

    @named("y wait")
    def ag_end(buf, idx):
        for slot in (2, 3):
            wait_for(buf.at[pl.ds(0, T)], y_r.at[idx, slot])
        ysent(buf, idx)

    def go(cps):
        for c in cps:
            c.start()

    @named("y wait")
    def end(cps):
        for c in cps:
            c.wait()

    def reduce_go(idx, name, product):
        def tile(i):
            c = span(i, 768)
            pf[:, c] = product(c)
            sb[0, :, c] = pf[rows_of(2), c].astype(BF)
            remote(sb.at[0, :, c], rb.at[idx % 2, 2, :, c], y_s.at[8 + idx, i], y_r.at[8 + idx, i], ypeer(1 + 2 * i)).start()
            sb[1, :, c] = pf[rows_of(3 - 2 * i), c].astype(BF)
            remote(sb.at[1, :, c], rb.at[idx % 2, 1 - i, :, c], y_s.at[8 + idx, 1 - i], y_r.at[8 + idx, 3 - i],
                   ypeer(3 - 2 * i)).start()
        tile.__name__ = name
        tiles(2, tile)

    @named("y pass on")
    def reduce_pass(idx):
        for side, d in ((0, 1), (1, 3)):
            c = (LEFT, RIGHT)[side]
            wait_for(rb.at[idx % 2, 2, :, COLS[side]], y_r.at[8 + idx, side])
            sb[2, :, c] = (pf[rows_of(d), c] + rb[idx % 2, 2, :, c].astype(F32)).astype(BF)
            remote(sb.at[2, :, COLS[side]], rb.at[idx % 2, side, :, COLS[side]], y_s.at[8 + idx, side],
                   y_r.at[8 + idx, 2 + side], (right, left)[side]).start()

    @named("y wait")
    def reduce_end(idx):
        for side in (0, 1):
            wait_for(rb.at[idx % 2, side], y_r.at[8 + idx, 2 + side])
        ysent(gall, 8 + idx)
        return pf[own, :] + rb[idx % 2, 0].astype(F32) + rb[idx % 2, 1].astype(F32)

    livef = jnp.where(lax.broadcasted_iota(jnp.int32, (T, D), 0).astype(F32) < length, 1.0, 0.0)

    def put_result(l, ref, value, way):
        @pl.when(s == l)
        def _():
            ref[pl.ds(s, 1)] = value[None]

        @pl.when(s != l)
        def _():
            ostage[way] = value
            remote(ostage.at[way], ref.at[s], x_s.at[way], x_r.at[way], sib).start()

    @named("last results")
    def finish_results():
        for way, ref in enumerate((act_out, ig_out)):
            remote(ostage.at[way], ref.at[s], x_s.at[way], x_r.at[way], sib).wait()

    def nothing():
        pass

    def forward(l, hidden, hooks):
        hook = lambda name: hooks.get(name, nothing)()
        if l:
            with jax.named_scope("norm first"):
                xh, rsd = stats(hidden)
                xh1[l] = xh
                rd1[l] = jnp.broadcast_to(rsd, (T, 128))
                normed[l, own, :] = (xh * small[l, 0:1, :] + small[l, 1:2, :]).astype(BF)
            ag_go(normed.at[l], l * 2)
            hook("normed")
            ag_pass(normed.at[l], l * 2)
            hook("normed2")
            ag_end(normed.at[l], l * 2)
        if l:
            wcopy(PR, 1).wait()
        with jax.named_scope("queries keys values"):
            for part in range(3):
                if l == 0:
                    gather_d(0, PARTS[part])
                joined = nn(normed[l], vp[:, part * HW:(part + 1) * HW]) + small[l, 7:8, part * HW:(part + 1) * HW]
                for h in range(3):
                    v = joined[:, h * 128:(h + 1) * 128]
                    if part < 2:
                        v = v * cos_ref[...] + pltpu.roll(v, 64, 1) * sin_ref[...]
                    qkv[l, :, part * HW + h * 128:part * HW + (h + 1) * 128] = v.astype(BF)
        hook("joined")
        with jax.named_scope("attention"):
            for h in range(3):
                q = qkv[l, :, h * 128:(h + 1) * 128]
                k = qkv[l, :, HW + h * 128:HW + (h + 1) * 128]
                v = qkv[l, :, 2 * HW + h * 128:2 * HW + (h + 1) * 128]
                sc = jnp.where(vis[...] > 0.5, nt(q, k) * SCALE, MASKED)
                top = jnp.max(sc, axis=-1, keepdims=True)
                ex = jnp.exp(sc - top)
                p = ex * (1.0 / jnp.sum(ex, axis=-1, keepdims=True))
                probs[l, h] = p
                mixed[l, :, h * 128:(h + 1) * 128] = nn(p.astype(BF), v).astype(BF)
        if l:
            wcopy(OU, 1).wait()
        reduce_go(l * 2, "out_tile", lambda c: nn(mixed[l], vo[:, c]))
        hook("mixed")
        reduce_pass(l * 2)
        hook("mixed2")
        middle = hidden + reduce_end(l * 2) + small[l, 2:3, :]
        with jax.named_scope("norm second"):
            xh, rsd = stats(middle)
            xh2[l] = xh
            rd2[l] = jnp.broadcast_to(rsd, (T, 128))
            ns[l, own, :] = (xh * small[l, 3:4, :] + small[l, 4:5, :]).astype(BF)
            keep[...] = middle
        ag_go(ns.at[l], l * 2 + 1)
        hook("second")
        ag_pass(ns.at[l], l * 2 + 1)
        hook("second2")
        ag_end(ns.at[l], l * 2 + 1)
        if l:
            wcopy(EX, 1).wait()

        def up_tile(i):
            c = span(i, 256)
            u = nn(ns[l], ve[:, c]) + small[l, 6:7, c]
            unit = lax.broadcasted_iota(jnp.int32, (1, 256), 1) + (i * 256 + D * t)
            m = jnp.where(unit < width, 1.0, 0.0)
            u2 = u * u
            th = jnp.tanh(GC * u * (1.0 + 0.044715 * u2))
            half = 0.5 * (1.0 + th)
            active[l, :, c] = (u * half * m).astype(BF)
            gder[l, :, c] = m * (half + 0.5 * u * (1.0 - th * th) * (GC * (1.0 + 3 * 0.044715 * u2)))
        tiles(6, up_tile)
        hook("upper")
        if l:
            wcopy(SH, 1).wait()
        reduce_go(l * 2 + 1, "down_tile", lambda c: nn(active[l], vs[:, c]))
        if l == 0:
            hook("down")
            reduce_pass(1)
            hook("down2")
            return out_rows(0)

    def out_rows(l):
        result = (keep[...] + reduce_end(l * 2 + 1) + small[l, 5:6, :]) * livef
        result = result.astype(BF)
        put_result(l, act_out, result, 0)
        return result

    def norm_back(dn, xh, rsd, gain):
        e = dn * gain
        return rsd[:, 0:1] * (e - jnp.mean(e, axis=-1, keepdims=True)
                              - xh * jnp.mean(e * xh, axis=-1, keepdims=True))

    def backward(l, g, hooks):
        hook = lambda name: hooks.get(name, nothing)()
        g32 = g.astype(F32)
        smt[l, 5:6, :] = colsum(g32)
        if l == 0:
            gall[own, :] = g
        if l == 0:
            ag_go(gall, 4)
            hook("grad")
            ag_pass(gall, 4)
            hook("grad2")
            ag_end(gall, 4)

        def gs_tile(i):
            c = span(i, 256)
            gbuf(l, SH)[c, :] = tn(active[l, :, c], gall[...]).astype(BF)

        def dact_tile(i):
            c = span(i, 256)
            da = nt(gall[...], vs[c, :]) * gder[l, :, c]
            da = da.astype(BF)
            dup[:, c] = da
            smt[l, 6:7, c] = colsum(da.astype(F32))

        def ge_tile(i):
            c = span(i, 256)
            gbuf(l, EX)[c, :] = tn(ns[l, :, c], dup[...]).astype(BF)

        if l == 0:
            tiles(6, gs_tile)
            sum0_go(0, SH)
            wcopy(SH, 0).wait()
            tiles(6, dact_tile)
            wcopy(EX, 0).wait()
        else:
            end(g_cps)
            tiles(6, gs_tile)
            sum0_go(1, SH)
            tiles(6, dact_tile)
            wcopy(SH, 0).start()
            hook("result")
            reduce_pass(3)
            hook("result2")
            out_rows(1)
        reduce_go(4 + l * 2, "e_tile", lambda c: nt(dup[...], ve[c, :]))
        if l == 1:
            wcopy(EX, 0).start()
        hook("partial")
        tiles(6, ge_tile)
        sum0_go(l, EX)
        hook("upper")
        reduce_pass(4 + l * 2)
        hook("upper2")
        dn = reduce_end(4 + l * 2)
        with jax.named_scope("norm second back"):
            smt[l, 3:4, :] = colsum(dn * xh2[l])
            smt[l, 4:5, :] = colsum(dn)
            dmid = g32 + norm_back(dn, xh2[l], rd2[l], small[l, 3:4, :])
            db = dmid.astype(BF)
            smt[l, 2:3, :] = colsum(db.astype(F32))
            keep[...] = dmid
            dball[own, :] = db
        ag_go(dball, 4 + l * 2 + 1)
        hook("middle")
        ag_pass(dball, 4 + l * 2 + 1)
        hook("middle2")
        ag_end(dball, 4 + l * 2 + 1)
        if l == 0:
            wcopy(OU, 0).wait()
        dmix[...] = nt(dball[...], vo[...]).astype(BF)
        if l == 1:
            wcopy(OU, 0).start()
        with jax.named_scope("attention back"):
            for h in range(3):
                c = slice(h * 128, (h + 1) * 128)
                q = qkv[l, :, h * 128:(h + 1) * 128]
                k = qkv[l, :, HW + h * 128:HW + (h + 1) * 128]
                v = qkv[l, :, 2 * HW + h * 128:2 * HW + (h + 1) * 128]
                p = probs[l, h]
                dm = dmix[:, c]
                dj[:, 2 * HW + h * 128:2 * HW + (h + 1) * 128] = tn(p.astype(BF), dm).astype(BF)
                dp = nt(dm, v)
                dsc = (p * (dp - jnp.sum(dp * p, axis=-1, keepdims=True))).astype(BF)
                for part, v in ((0, nn(dsc, k)), (1, tn(dsc, q))):
                    v = v * SCALE
                    v = v * cos_ref[...] - pltpu.roll(v, 64, 1) * sin_ref[...]
                    dj[:, part * HW + h * 128:part * HW + (h + 1) * 128] = v.astype(BF)
        smt[l, 7:8, :] = jnp.zeros((1, D), F32)
        smt[l, 7:8, 0:QW] = colsum(dj[...].astype(F32))
        if l == 0:
            wcopy(PR, 0).wait()

        hook("scores")

        def gp_tile(i):
            c = span(i, 256)
            gbuf(l, PR)[c, :] = tn(normed[l, :, c], dj[...]).astype(BF)
        tiles(6, gp_tile)
        sum0_go(l, PR)
        hook("project")
        reduce_go(4 + l * 2 + 1, "d_tile", lambda c: nt(dj[...], vp[c, :]))
        if l == 1:
            wcopy(PR, 0).start()
        with jax.named_scope("output term"):
            gbuf(l, OU)[...] = tn(mixed[l], dball[...]).astype(BF)
        sum0_go(l, OU)
        hook("joined")
        reduce_pass(4 + l * 2 + 1)
        hook("joined2")
        dn = reduce_end(4 + l * 2 + 1)
        with jax.named_scope("norm first back"):
            smt[l, 0:1, :] = colsum(dn * xh1[l])
            smt[l, 1:2, :] = colsum(dn)
            dh = keep[...] + norm_back(dn, xh1[l], rd1[l], small[l, 0:1, :])
            res = dh.astype(BF)
        put_result(l, ig_out, res, 1)
        return res

    hall = dball
    hall[own, :] = win_ref[s]
    gall[own, :] = (cot_ref[s].astype(F32) * livef).astype(BF)
    h_cps = [remote(hall.at[own], hall.at[own], m_s.at[d - 1], m_r.at[d - 1], ypeer(d)) for d in (1, 2, 3)]
    g_cps = [remote(gall.at[own], gall.at[own], m_s.at[2 + d], m_r.at[2 + d], ypeer(d)) for d in (1, 2, 3)]
    pack_last = remote(allp.at[s], allp.at[s], p_s.at[3, 0], p_r.at[3, 0], sib)
    with jax.named_scope("greet wait"):
        pl.semaphore_wait(bar, 20)
    pack_go(0)
    go(lcs)

    @pl.when(first)
    def _():
        for m in moves[:4]:
            send_or_keep(*m)
    gather_a(0, PR)
    pack_end(0)
    pack_go(1)
    go(h_cps)

    @pl.when(first)
    def _():
        for m in moves[4:8]:
            send_or_keep(*m)
    for m in moves[12:]:
        send_or_keep(*m)
    for k in PARTS:
        gather_b(0, k)

    @pl.when(first)
    def _():
        for m in moves[8:12]:
            send_or_keep(*m)
    pack_end(1)
    pack_go(2)
    gather_a(0, OU)
    for k in PARTS:
        gather_f(0, k)
    gather_b(0, OU)
    go(g_cps)
    end(lcs)
    row = lax.broadcasted_iota(jnp.int32, (TG, TG), 0)
    col = lax.broadcasted_iota(jnp.int32, (TG, TG), 1)
    limit = jnp.zeros((1, TG), F32)
    blk = lax.broadcasted_iota(jnp.int32, (1, TG), 1) // T
    for r in range(4):
        one = lens[r][0:1, :]
        limit = jnp.where(blk == r, jnp.concatenate([one, one], axis=1), limit)
    ok = (row // T == col // T) & (col <= row) & ((col % T).astype(F32) < limit)
    vis[...] = jnp.where(ok, 1.0, 0.0)
    hidden0 = win_ref[s].astype(F32)
    xh, rsd = stats(hidden0)
    xh1[0] = xh
    rd1[0] = jnp.broadcast_to(rsd, (T, 128))
    pack_end(2)
    pack_last.start()
    gather_a(0, EX)
    for k in PARTS:
        gather_c(0, k)
    gather_f(0, OU)
    end(h_cps)
    pack_last.wait()

    def spread(l, r, width, total, feature):
        n = feature(lax.broadcasted_iota(jnp.int32, (128, total), 1))
        i = lax.broadcasted_iota(jnp.int32, (128, total), 0)
        pick = jnp.where(n - (n // width) * width == i, 1.0, 0.0).astype(BF)
        wide = nn(allp[l, :, r, :].astype(BF), pick)
        n = feature(lax.broadcasted_iota(jnp.int32, (64, total), 1))
        i = lax.broadcasted_iota(jnp.int32, (64, total), 0)
        small[l, r:r + 1, 0:total] = colsum(jnp.where(n // width == (i % 4) * 16 + i // 4, wide, 0.0))

    @named("spread")
    def unpack(l, wanted):
        for r in wanted:
            if r < 6:
                spread(l, r, 24, D, lambda n: n)
            elif r == 6:
                spread(l, r, 96, D, lambda n: n + D * t)
            else:
                spread(l, r, 72, QW, lambda n: n + (n // HW) * (D - HW) + HW * t)

    unpack(0, (0, 1, 7))

    def norm_tile(i):
        rows = span(i, T)
        wide, _ = stats(hall[rows, :].astype(F32))
        normed[0, rows, :] = (wide * small[0, 0:1, :] + small[0, 1:2, :]).astype(BF)
    tiles(4, norm_tile)
    gather_c(0, OU)
    gather_b(0, EX)
    gather_a(0, SH)

    def steps(*todo):
        def run():
            for what, *args in todo:
                what(*args)
        return run

    def second_shards():
        @pl.when(jnp.logical_not(first))
        def _():
            for m in moves[8:12]:
                send_or_keep(*m)

    def reload(k):
        gather_drain(0, k)
        save(k).wait()
        gather_d(1, k)
        wcopy(k, 1).start()

    ga, gb, gf, gc, gd = gather_a, gather_b, gather_f, gather_c, gather_d
    def second_first():
        @pl.when(jnp.logical_not(first))
        def _():
            for m in moves[:8]:
                send_or_keep(*m)

    first_hooks = dict(
        joined=steps((gd, 0, OU)),
        mixed=steps((unpack, 0, (2, 3, 4, 5, 6)), (gf, 0, EX), (gb, 0, SH)),
        mixed2=steps((second_first,), (gc, 0, EX)),
        second=steps((unpack, 1, (0, 1, 2, 3, 4, 5, 6, 7)), (ga, 1, PR), (ga, 1, OU)),
        second2=steps((gf, 0, SH), (second_shards,), (gd, 0, EX)),
        upper=steps((gb, 1, PR), (gb, 1, OU), (gc, 0, SH), (gd, 0, SH)),
        down=steps((ga, 1, EX), (ga, 1, SH)),
        down2=steps((gf, 1, PR), (gf, 1, OU), (gb, 1, EX), (gc, 1, PR)))
    second_hooks = dict(
        normed2=steps((gc, 1, OU), (gb, 1, SH), (gf, 1, EX), (reload, PR)),
        joined=steps((reload, OU)),
        mixed=steps((gf, 1, SH)),
        mixed2=steps((gc, 1, EX)),
        second2=steps((gc, 1, SH), (reload, EX)),
        upper=steps((reload, SH)))
    a1 = forward(0, hidden0, first_hooks)
    forward(1, a1.astype(F32), second_hooks)

    for k in range(4):
        gather_drain(1, k)
    for m in moves:
        sent(*m)

    load, fin, ml, mf, ll, lf = sum0_load, sum0_fin, mid_load, mid_fin, last_load, last_fin

    def mid(l, k):
        mid_load(l, k)
        mid_fin(l, k)

    def last(l, k):
        last_load(l, k)
        last_fin(l, k)

    ig2 = backward(1, gall[own, :], dict(
        result2=steps((load, 1, SH), (fin, 1, SH)),
        upper2=steps((ml, 1, SH), (load, 1, EX), (mf, 1, SH), (fin, 1, EX)),
        middle2=steps((ll, 1, SH), (ml, 1, EX), (mf, 1, EX), (lf, 1, SH)),
        joined=steps((load, 1, PR), (fin, 1, PR)),
        joined2=steps((load, 1, OU), (ll, 1, EX), (fin, 1, OU), (lf, 1, EX))))
    g1 = (ig2.astype(F32) * livef).astype(BF)
    backward(0, g1, dict(
        grad=steps((sum2_end, 1, SH), (sum_drain, 1, SH)),
        grad2=steps((ml, 1, PR), (mf, 1, PR), (mid, 1, OU), (sum_drain, 1, EX)),
        partial=steps((load, 0, SH), (fin, 0, SH)),
        upper2=steps((ll, 1, PR), (ml, 0, SH), (lf, 1, PR), (mf, 0, SH)),
        middle=steps((load, 0, EX), (ll, 1, OU), (fin, 0, EX), (lf, 1, OU)),
        middle2=steps((sum2_end, 1, EX), (sum2_end, 1, PR)),
        project=steps((ml, 0, EX), (mf, 0, EX)),
        joined=steps((load, 0, PR), (ll, 0, SH), (fin, 0, PR), (lf, 0, SH)),
        joined2=steps((load, 0, OU), (fin, 0, OU), (last, 0, EX))))
    vec_go(0)
    mid(0, PR)
    vec_end(0)
    vec_go(1)
    mid(0, OU)
    sum2_end(0, SH)
    last(0, PR)
    vec_end(1)
    vec_go(2)
    last(0, OU)
    sum2_end(1, OU)
    sum2_end(0, EX)
    vec_end(2)
    vec_go(3)
    sum2_end(0, PR)
    sum2_end(0, OU)
    vec_end(3)
    finish_weights()
    finish_results()
    for k in range(4):
        for l in (0, 1):
            if (l, k) not in ((1, SH), (1, EX)):
                sum_drain(l, k)


def finish_kernel(act, ig, sums, fp, fo, fe, fs,
                  act_out, ig_out, o0, o1, d_pw, o7, d_ow, o2, o3, o4, d_ew, o6, d_sw, o5):
    chip = lax.axis_index("dp")
    act_out[0, :, 0] = act[...]
    ig_out[0, :, 0] = ig[...]
    for r in range(4):
        for p in range(3):
            d_pw[0, :, p * D + HW * r:p * D + HW * (r + 1)] = fp[r, :, HW * p:HW * (p + 1)].astype(F32)[:24]
        d_ow[0, :, HW * r:HW * (r + 1)] = fo[r].astype(F32)[:24]
        d_ew[0, :, D * r:D * (r + 1)] = fe[r].astype(F32)[:24]
    for j in range(2):
        d_sw[0, :, 768 * j:768 * (j + 1)] = fs[j].astype(F32)
    total = sums[0] + sums[1] + sums[2] + sums[3]
    mine = pltpu.roll(total, (D - 24 * chip) % D, 1)
    for r, o in enumerate((o0, o1, o2, o3, o4, o5)):
        o[...] = mine[r:r + 1, :24]
    units = sums[chip // 16]
    o6[...] = pltpu.roll(units, (D - 96 * (chip % 16)) % D, 1)[6:7, :96]
    cols = jnp.concatenate([sums[r, :, HW * p:HW * (p + 1)] for p in range(3) for r in range(4)], axis=1)
    o7[...] = pltpu.roll(cols, (3 * D - 72 * chip) % (3 * D), 1)[7:8, :72]


def core_call(*args):
    sd = jax.ShapeDtypeStruct
    V = pltpu.VMEM
    DMA = pltpu.SemaphoreType.DMA
    hbm = [sd((2,) + f, BF) for f in FULL]
    hbm += [sd((2, 2, HW, QW), BF), sd((2, 2, HW, HW), BF), sd((2, 2, HW, D), BF), sd((2, D, 768), BF)]
    hbm += [sd((2, 3, 4 * f[0], f[1]), BF) for f in SLAB]
    hbm += [sd((2, 3) + f, BF) for f in SLAB]
    out = pl.pallas_call(
        core_kernel,
        out_shape=[sd((2, T, D), BF), sd((2, T, D), BF), sd((4, 8, D), F32),
                   sd((4, 32, QW), BF), sd((4, 32, HW), BF), sd((4, 32, D), BF), sd((2, 96, 768), BF)] + hbm,
        in_specs=[VM] * 2 + [pl.BlockSpec(memory_space=pltpu.SMEM)] * 2 + [VM] * 14,
        out_specs=[VM] * 7 + [ANY] * 16,
        scratch_shapes=[
            V((D, QW), BF), V((HW, D), BF), V((D, D), BF), V((D, D), BF),
            V((D, QW), BF), V((HW, D), BF), V((D, D), BF), V((D, D), BF),
            V((2, TG, D), BF), V((2, TG, D), BF), V((TG, D), BF), V((TG, D), BF),
            V((2, TG, QW), BF), V((2, 3, TG, TG), F32), V((2, TG, HW), BF),
            V((2, TG, D), F32), V((2, TG, D), BF),
            V((2, T, D), F32), V((2, T, D), F32), V((2, T, 128), F32), V((2, T, 128), F32),
            V((TG, D), F32), V((3, T, D), BF), V((2, 3, T, D), BF),
            V((TG, D), BF), V((TG, QW), BF), V((TG, HW), BF), V((TG, TG), F32), V((4, 8, 128), F32),
            V((T, D), F32), V((2, T, D), BF),
            V((4, 32, QW), BF), V((4, 32, HW), BF), V((4, 32, D), BF),
            V((2, 2, 32, QW), BF), V((2, 2, 32, HW), BF), V((2, 2, 32, D), BF), V((2, 96, 768), BF),
            V((2, 48, QW), BF), V((2, 48, HW), BF), V((2, 48, D), BF),
            V((2, 96, 768), BF),
            V((768, D), BF), V((576, D), BF), V((2, 64, 8, 128), F32), V((2, 8, D), F32), V((5, 8, D), F32), V((3, 3, 8, D), F32),
            DMA((16, 2)), DMA((16, 4)), DMA((4,)), DMA((4,)), DMA((4,)), DMA((3,)), DMA((3,)),
            DMA((3, 4)), DMA((2,)), DMA((3, 2, 2)), DMA((2,)), DMA((4, 3)), DMA((4, 3)),
            DMA((2, 7)), DMA((2, 7)), DMA((2, 7)), DMA((2, 2, 7)), DMA((2, 7)), DMA((2, 7)), DMA((2, 7)),
            DMA((2, 4)), DMA((2, 4)), DMA((2, 4)), DMA((2, 4)), DMA((2, 4)), DMA((2, 4)), DMA((9,)),
            DMA((2, 4, 2)), DMA((4, 4)), DMA((4, 3)), DMA((4, 3)), DMA((6,)), DMA((6,)), pltpu.SemaphoreType.REGULAR, DMA((2, 7)), DMA((2, 4)), DMA((4,)),
        ],
        compiler_params=pltpu.CompilerParams(collective_id=1, has_side_effects=True,
                                             vmem_limit_bytes=64 * 2**20 - 2**16),
    )(*args)
    return out[:7]


def finish_call(*args):
    def sd(*shape):
        return jax.ShapeDtypeStruct(shape, F32)
    rows = jax.ShapeDtypeStruct((1, 2, 1, T, D), BF)
    row = sd(1, 24)
    return pl.pallas_call(
        finish_kernel,
        out_shape=[rows, rows, row, row, sd(1, 24, 3 * D), sd(1, 72), sd(1, 24, D), row, row, row,
                   sd(1, 24, 4 * D), sd(1, 96), sd(1, 96, D), row],
        in_specs=[VM] * 7,
        out_specs=[VM] * 14,
        compiler_params=pltpu.CompilerParams(vmem_limit_bytes=64 * 2**20 - 2**16),
    )(*args)


def rotary():
    half = 64
    rates = (np.float32(10000.0) ** (-np.arange(half, dtype=np.float32) / np.float32(half))).astype(np.float32)
    ang = np.arange(T, dtype=np.float32)[:, None] * rates[None, :]
    cos, sin = np.cos(ang), np.sin(ang)
    cos2 = np.concatenate([cos, cos], axis=1)
    sin2 = np.concatenate([-sin, sin], axis=1)
    return np.tile(cos2, (4, 1)).astype(np.float32), np.tile(sin2, (4, 1)).astype(np.float32)


def per_device(window_input, cotangent, lengths, widths, gain_first, shift_first, project_weight, project_bias,
               output_weight, output_bias, gain_second, shift_second, expand_weight, expand_bias,
               shrink_weight, shrink_bias):
    cos2, sin2 = rotary()
    parts = core_call(
        window_input[:, 0], cotangent[:, 0], lengths.reshape(2), widths, gain_first, shift_first, output_bias, gain_second,
        shift_second, shrink_bias, expand_bias, project_bias, jnp.asarray(cos2), jnp.asarray(sin2),
        project_weight, output_weight, expand_weight, shrink_weight)
    return tuple(finish_call(*parts))


def solution(mesh):
    row = P("section", "dp")
    mat = P("section", "dp", None)
    params = (row, row, mat, row, mat, row, row, row, mat, row, mat, row)
    seq = P(None, "dp", None, None)
    out = P("section", None, "dp", None, None)
    return jax.shard_map(
        per_device, mesh=mesh,
        in_specs=(seq, seq, P(None, "dp"), P()) + params,
        out_specs=(out, out) + params,
        check_vma=False,
    )
```

```python
import jax
import jax.numpy as jnp
import numpy as np
from jax import lax
from jax.experimental import pallas as pl
from jax.experimental.pallas import tpu as pltpu
from jax.sharding import PartitionSpec as P

MESH = pl.DeviceIdType.MESH
ANY = pl.BlockSpec(memory_space=pl.ANY)
VM = pl.BlockSpec(memory_space=pltpu.VMEM)
EPS = 1e-05
MASKED = -1e9
BF = jnp.bfloat16
F32 = jnp.float32
D = 1536
T = 64
TG = 256
HW = 384
QW = 1152
SCALE = 128 ** -0.5
GC = (2 / np.pi) ** 0.5
PR, OU, EX, SH = range(4)
PARTS = (4, 5, 6)
FULL = ((D, QW), (HW, D), (D, D), (D, D))
SLAB = ((48, QW), (48, HW), (48, D), (96, 768))


def nn(a, b):
    return jnp.dot(a, b, preferred_element_type=F32)


def nt(a, b):
    return lax.dot_general(a, b, (((1,), (1,)), ((), ())), preferred_element_type=F32)


def tn(a, b):
    return lax.dot_general(a, b, (((0,), (0,)), ((), ())), preferred_element_type=F32)


def tiles(count, body):
    def step(i, carry):
        body(i)
        return carry
    with jax.named_scope(body.__name__):
        lax.fori_loop(0, count, step, 0)


def span(i, size):
    return pl.ds(pl.multiple_of(i * size, size), size)


def at(start, size, unit):
    return pl.ds(pl.multiple_of(start, unit), size)


def stats(x):
    mean = jnp.mean(x, axis=-1, keepdims=True)
    c = x - mean
    var = jnp.mean(c * c, axis=-1, keepdims=True)
    rs = lax.rsqrt(var + EPS)
    return c * rs, rs


def named(name):
    def deco(fn):
        def inner(*args):
            with jax.named_scope(name):
                return fn(*args)
        return inner
    return deco


def colsum(v):
    return jnp.sum(v, axis=0, keepdims=True)


def to32(v):
    v = v.astype(F32)
    return jnp.concatenate([v, jnp.zeros((8, v.shape[1]), F32)], axis=0).astype(BF)


def core_kernel(win_ref, cot_ref, len_ref, wid_ref, v0, v1, v2, v3, v4, v5, v6, v7, cos_ref, sin_ref, pw, ow, ew, sw,
                act_out, ig_out, sm_out, fp, fo, fe, fs,
                wp, wo, we, ws, r0p, r0o, r0e, r0s, r1p, r1o, r1e, r1s, r2p, r2o, r2e, r2s,
                vp, vo, ve, vs, up, uo, ue, us_,
                normed, ns, gall, dball, qkv, probs, mixed, gder, active, xh1, xh2, rd1, rd2,
                pf, sb, rb, dup, dj, dmix, vis, lens, keep, ostage,
                sp, so, se, cp, co, ce, cs, bp, bo, be, fss,
                tmp, tmp1, allp, small, smt, sme,
                y_s, y_r, w_sem, x_s, x_r, l_s, l_r, z_s, zo_s, z_r, zs_r, p_s, p_r,
                a_s, a_r, b_s, b_r, c_s, c_r, o_sem, q0_s, q0_r, q1_s, q1_r, q2_s, q2_r, t_sem,
                f_s, f_r, e_s, e_r, m_s, m_r, token, f2_r, qf_r, v_sem):
    s = lax.axis_index("section")
    chip = lax.axis_index("dp")
    y, x, z = chip // 16, (chip // 4) % 4, chip % 4
    t = y
    zp = z % 2
    zh = z // 2
    first = s == 0

    def dev(core, cy, cx, cz):
        return (core, cy * 16 + cx * 4 + cz)

    def ypeer(d):
        return dev(s, (y + d) % 4, x, z)

    class Axes:
        def __init__(self, straight):
            self.straight = straight
            self.a, self.b = self.grid(x, z)

        def grid(self, a, b):
            return jnp.where(self.straight, a, b), jnp.where(self.straight, b, a)

        def apeer(self, d):
            cx, cz = self.grid((self.a + d) % 4, self.b)
            return dev(s, y, cx, cz)

        def bpeer(self, d):
            cx, cz = self.grid(self.a, (self.b + d) % 4)
            return dev(s, y, cx, cz)

    crossed, same = Axes(first), Axes(False)
    gather_axes = (crossed, same, crossed, crossed, crossed, crossed, crossed)
    sum_axes = (crossed, crossed, crossed, crossed)

    sib = dev(1 - s, y, x, z)
    own = at(t * T, T, T)

    bar = pltpu.get_barrier_semaphore()

    def greet(who):
        pl.semaphore_signal(bar, inc=1, device_id=who, device_id_type=MESH)

    with jax.named_scope("greet"):
        for d in (1, 2, 3):
            for core in (s, 1 - s):
                greet(dev(core, (y + d) % 4, x, z))
        for d in (0, 1, 2, 3):
            for core in (s, 1 - s):
                greet(dev(core, (y + d) % 4, x, 2 * zh + 1 - zp))
        greet(sib)
        for d in (1, 2, 3):
            greet(dev(s, y, (x + d) % 4, z))
        for d in (0, 1):
            greet(dev(s, y, x, 2 * (1 - zh) + d))

    def remote(src, dst, ssem, rsem, who):
        return pltpu.make_async_remote_copy(src_ref=src, dst_ref=dst, send_sem=ssem, recv_sem=rsem,
                                            device_id=who, device_id_type=MESH)

    def wait_for(ref, sem):
        pltpu.make_async_copy(ref, ref, sem).wait()

    w_hbm = (wp, wo, we, ws)
    w_v = (vp, vo, ve, vs)
    g_v = (up, uo, ue, us_)
    r0 = (r0p, r0o, r0e, r0s)
    r1 = (r1p, r1o, r1e, r1s)
    r2 = (r2p, r2o, r2e, r2s)

    def slab_at(k, j, cx, cz):
        if k not in (OU, SH):
            half = 1 - cz % 2 if k == EX else cz % 2
            return at(48 * (8 * (2 * half + j) + 2 * cx + cz // 2), 48, 48), slice(None)
        if k == OU:
            return at(48 * (2 * cx + cz // 2), 48, 48), at(HW * (2 * (cz % 2) + j), HW, HW)
        return at(96 * (4 * cx + cz), 96, 96), at(768 * j, 768, 768)

    def slab_of(ref, k, axes, a, b):
        cx, cz = axes.grid(a, b)
        return ref.at[slab_at(k, s, cx, cz)]

    def parts_of(ref, k, j):
        if k not in (OU, SH):
            return [ref.at[at(HW * (2 * p + j), HW, HW)] for p in (0, 1)]
        if k == OU:
            return [ref.at[:, at(HW * (2 * p + j), HW, HW)] for p in (0, 1)]
        return [ref.at[:, at(768 * j, 768, 768)]]

    def bulk(ref, k, slabs):
        if k == OU:
            return ref.at[pl.ds(0, 12 * slabs)] if slabs > 3 else ref.at[pl.ds(0, 144), pl.ds(0, HW)]
        return ref.at[pl.ds(0, 48 * slabs)]

    def piece_target(yt, half):
        return dev(y % 2, yt, x, 2 * zh + half), (yt == y) & (s == y % 2) & (zp == half)

    def out_target(q):
        return dev(q % 2, y, x, 2 * zh + q // 2), (zp == q // 2) & (s == q % 2)

    def send_or_keep(src, dst, ssem, rsem, who, is_me):
        @pl.when(is_me)
        def _():
            pltpu.make_async_copy(src, dst, rsem).start()

        @pl.when(jnp.logical_not(is_me))
        def _():
            remote(src, dst, ssem, rsem, who).start()

    def sent(src, dst, ssem, rsem, who, is_me):
        @pl.when(jnp.logical_not(is_me))
        def _():
            remote(src, dst, ssem, rsem, who).wait_send()

    def shard_moves():
        out = []
        for yt in range(4):
            who, me = piece_target(yt, y // 2)
            out.append((sp.at[yt], cp.at[s, zp], z_s.at[0, yt], z_r.at[0, s, zp], who, me))
        for q in range(4):
            who, me = out_target(q)
            out.append((so.at[q], co.at[s, zp], z_s.at[1, q], z_r.at[1, s, zp], who, me))
        for yt in range(4):
            who, me = piece_target(yt, 1 - y // 2)
            out.append((se.at[yt], ce.at[s, zp], z_s.at[2, yt], z_r.at[2, s, zp], who, me))
        for j in range(2):
            out.append((sw.at[0, :, pl.ds(768 * j, 768)], cs.at[s], zo_s.at[j], zs_r.at[s],
                        dev(j, y, x, z), s == j))
        return out

    moves = shard_moves()
    with jax.named_scope("shards"):
        for yt in range(4):
            sp[yt] = to32(jnp.concatenate([pw[0, :, p * D + HW * yt:p * D + HW * (yt + 1)] for p in range(3)], axis=1))
        for q in range(4):
            so[q] = to32(ow[0, :, HW * q:HW * (q + 1)])
        for yt in range(4):
            se[yt] = to32(ew[0, :, D * yt:D * (yt + 1)])

    spot = (chip % 16) * 4 + y
    allp[s, pl.ds(spot, 1)] = jnp.zeros((1, 8, 128), F32)
    for r, v in enumerate((v0, v1, v2, v3, v4, v5, v6, v7)):
        allp[s, pl.ds(spot, 1), r:r + 1, 0:v.shape[1]] = v[...].astype(F32)[None]

    def pack_copies(stage):
        out = []
        for d in (1, 2, 3):
            if stage == 0:
                blk, who = allp.at[s, pl.ds(spot, 1)], ypeer(d)
            elif stage == 1:
                blk, who = allp.at[s, at(spot - y, 4, 4)], dev(s, y, x, (z + d) % 4)
            else:
                blk, who = allp.at[s, at(16 * x, 16, 16)], dev(s, y, (x + d) % 4, z)
            out.append(remote(blk, blk, p_s.at[stage, d - 1], p_r.at[stage, d - 1], who))
        return out

    @named("pack go")
    def pack_go(stage):
        for c in pack_copies(stage):
            c.start()

    @named("pack wait")
    def pack_end(stage):
        for c in pack_copies(stage):
            c.wait()

    length = len_ref[s].astype(F32)
    width = wid_ref[s]
    lens[pl.ds(t, 1)] = jnp.full((1, 8, 128), length, F32)
    lcs = [remote(lens.at[pl.ds(t, 1)], lens.at[pl.ds(t, 1)], l_s.at[d - 1], l_r.at[d - 1], ypeer(d)) for d in (1, 2, 3)]

    got = (cp, co, ce, cs)
    bld = (bp, bo, be, cs)

    def home(l, k):
        if k in PARTS:
            return w_v[PR].at[:, pl.ds(HW * (k - 4), HW)]
        return w_hbm[k].at[1] if l else w_v[k]

    def slab_in(l, k):
        return bld[PR].at[l, :, pl.ds(HW * (k - 4), HW)] if k in PARTS else bld[k].at[l]

    def a_copies(l, k):
        src = slab_in(l, k)
        ax = gather_axes[k]
        return [remote(src, slab_of(home(l, k), k, ax, ax.a, ax.b), a_s.at[l, k], a_r.at[l, k], ax.apeer(d))
                for d in (1, 2, 3)]

    def own_copy(l, k):
        ax = gather_axes[k]
        return pltpu.make_async_copy(slab_in(l, k), slab_of(home(l, k), k, ax, ax.a, ax.b), o_sem.at[l, k])

    @named("gather a")
    def gather_a(l, k):
        if k == SH:
            wait_for(cs.at[l], zs_r.at[l])
        else:
            zk = (0, 1, 2)[k]
            for p in (0, 1):
                wait_for(got[k].at[l, p], z_r.at[zk, l, p])
            halves = [got[k][l, p].astype(F32)[:24] for p in (0, 1)]
            bld[k][l] = jnp.concatenate(halves, axis=0).astype(BF)
        for item in PARTS if (l, k) == (0, PR) else (k,):
            go(a_copies(l, item))
            own_copy(l, item).start()

    @named("gather b")
    def gather_b(l, k):
        w, ax = home(l, k), gather_axes[k]
        wait_for(bulk(w, k, 3), a_r.at[l, k])
        own_copy(l, k).wait()
        for a in range(4):
            src = slab_of(w, k, ax, a, ax.b)
            for side, d in ((0, 1), (1, 3)):
                remote(src, src, b_s.at[l, k], b_r.at[side, l, k], ax.bpeer(d)).start()

    @named("gather f")
    def gather_f(l, k):
        w, ax = home(l, k), gather_axes[k]
        for side, d in ((0, 1), (1, 3)):
            wait_for(bulk(w, k, 4), b_r.at[side, l, k])
            for a in (2 * side, 2 * side + 1):
                src = slab_of(w, k, ax, a, (ax.b + 4 - d) % 4)
                remote(src, src, b_s.at[l, k], f2_r.at[l, k], ax.bpeer(d)).start()

    @named("gather c")
    def gather_c(l, k):
        w = home(l, k)
        wait_for(bulk(w, k, 4), f2_r.at[l, k])
        for blk in parts_of(w, k, s):
            remote(blk, blk, c_s.at[l, k], c_r.at[l, k], sib).start()

    @named("gather d")
    def gather_d(l, k):
        wait_for(bulk(home(l, k), k, 16), c_r.at[l, k])
        if l == 0 and k not in (4, 5):
            save(PR if k == 6 else k).start()

    def save(k):
        return pltpu.make_async_copy(w_v[k], w_hbm[k].at[0], v_sem.at[k])

    @named("gather drain")
    def gather_drain(l, k):
        for item in PARTS if (l, k) == (0, PR) else (k,):
            w = home(l, item)
            wait_for(bulk(w, item, 3), a_s.at[l, item])
            wait_for(bulk(w, item, 12), b_s.at[l, item])
            wait_for(bulk(w, item, 16), c_s.at[l, item])

    def gbuf(l, k):
        if l == 0 and k == PR:
            return us_.at[:, pl.ds(0, QW)]
        if l == 0 and k == SH:
            return ue
        return g_v[k] if l else w_v[k]

    @named("sum0 go")
    def sum0_go(l, k):
        for i, blk in enumerate(parts_of(gbuf(l, k), k, 1 - s)):
            dst = r0[k].at[l, i] if k != SH else r0[k].at[l]
            remote(blk, dst, q0_s.at[l, k], q0_r.at[l, k], sib).start()

    def halves_tmp(k):
        if k in (PR, EX):
            return [tmp.at[pl.ds(HW * p, HW), pl.ds(0, FULL[k][1])] for p in (0, 1)]
        if k == OU:
            return [tmp.at[pl.ds(HW * p, HW), pl.ds(0, HW)] for p in (0, 1)]
        return [tmp.at[:, pl.ds(768 * p, 768)] for p in (0, 1)]

    def sum0_copies(l, k):
        srcs = [r0[k].at[l, i] for i in (0, 1)] if k != SH else [r0[k].at[l, pl.ds(768 * i, 768)] for i in (0, 1)]
        return [pltpu.make_async_copy(a, b, t_sem.at[i]) for i, (a, b) in enumerate(zip(srcs, halves_tmp(k)))]

    @named("sum0 load")
    def sum0_load(l, k):
        wait_for(r0[k].at[l], q0_r.at[l, k])
        for c in sum0_copies(l, k):
            c.start()

    @named("sum0")
    def sum0_fin(l, k):
        g, ax = gbuf(l, k), sum_axes[k]
        cps = sum0_copies(l, k)
        for p in (0, 1):
            cps[p].wait()

            def add(i):
                if k in (PR, EX):
                    rows, cols, n = at(HW * (2 * p + s) + 96 * i, 96, 96), slice(None), FULL[k][1]
                    other = tmp[pl.ds(pl.multiple_of(HW * p + 96 * i, 96), 96), 0:n]
                elif k == OU:
                    rows, cols = span(i, 96), at(HW * (2 * p + s), HW, HW)
                    other = tmp[pl.ds(pl.multiple_of(HW * p + 96 * i, 96), 96), 0:HW]
                else:
                    rows, cols = at(768 * p + 96 * i, 96, 96), at(768 * s, 768, 768)
                    other = tmp[span(i, 96), 768 * p:768 * p + 768]
                g[rows, cols] = (g[rows, cols].astype(F32) + other.astype(F32)).astype(BF)
            tiles(8 if k == SH else 4, add)
        for a in (0, 2, 1, 3):
            far = 1 if a < 2 else 3
            remote(slab_of(g, k, ax, a, (ax.b + 2) % 4), r1_slab(l, k, 0, a), q1_s.at[l, k], qf_r.at[l, k],
                   ax.bpeer(far)).start()
        for a in (0, 2, 1, 3):
            near = 3 if a < 2 else 1
            remote(slab_of(g, k, ax, a, (ax.b + near) % 4), r1_slab(l, k, near, a), q1_s.at[l, k], q1_r.at[l, k],
                   ax.bpeer(near)).start()

    def r1_slab(l, k, d, a):
        rows = SLAB[k][0]
        return r1[k].at[l, (0, 1, None, 2)[d], pl.ds(rows * a, rows)]

    def tmp_set(k, side):
        rows, cols = SLAB[k]
        if k == SH:
            return tmp1.at[pl.ds(0, 4 * rows), pl.ds(cols * side, cols)]
        return tmp1.at[pl.ds(4 * rows * side, 4 * rows), pl.ds(0, cols)]

    def tmp_slab(k, side, a):
        rows, cols = SLAB[k]
        if k == SH:
            return tmp1[at(rows * a, rows, rows), cols * side:cols * (side + 1)].astype(F32)
        return tmp1[at(4 * rows * side + rows * a, rows, rows), 0:cols].astype(F32)

    def mid_copies(l, k):
        rows, cols = SLAB[k]
        if k != SH:
            return [pltpu.make_async_copy(r1[k].at[l, 0], tmp1.at[pl.ds(384, 192), pl.ds(0, cols)], t_sem.at[2])]
        return [pltpu.make_async_copy(r1[k].at[l, 0, pl.ds(192 * i, 192)], tmp1.at[pl.ds(384, 192), pl.ds(768 * i, 768)],
                                      t_sem.at[(2, 8)[i]]) for i in (0, 1)]

    def mid_slab(k, a):
        rows, cols = SLAB[k]
        if k != SH:
            return tmp1[384 + 48 * a:432 + 48 * a, 0:cols].astype(F32)
        return tmp1[384 + 96 * (a % 2):480 + 96 * (a % 2), 768 * (a // 2):768 * (a // 2) + 768].astype(F32)

    @named("sum1 pass load")
    def mid_load(l, k):
        wait_for(r1[k].at[l, 0], qf_r.at[l, k])
        go(mid_copies(l, k))

    @named("sum1 pass on")
    def mid_fin(l, k):
        g, ax = gbuf(l, k), sum_axes[k]
        end(mid_copies(l, k))
        for a in range(4):
            d = 1 if a < 2 else 3
            cx, cz = ax.grid(a, (ax.b + d) % 4)
            where = slab_at(k, s, cx, cz)
            g[where] = (g[where].astype(F32) + mid_slab(k, a)).astype(BF)
            remote(g.at[where], r1_slab(l, k, d, a), q1_s.at[l, k], q1_r.at[l, k], ax.bpeer(d)).start()

    def last_copies(l, k):
        return [pltpu.make_async_copy(r1[k].at[l, 1 + i], tmp_set(k, i), t_sem.at[3 + i]) for i in (0, 1)]

    @named("sum1 load")
    def last_load(l, k):
        wait_for(r1[k].at[l, pl.ds(1, 2)], q1_r.at[l, k])
        go(last_copies(l, k))

    @named("sum1")
    def last_fin(l, k):
        g, ax = gbuf(l, k), sum_axes[k]
        end(last_copies(l, k))
        for da in (2, 1, 3, 0):
            a = (ax.a + da) % 4
            cx, cz = ax.grid(a, ax.b)
            where = slab_at(k, s, cx, cz)
            total = g[where].astype(F32) + tmp_slab(k, 0, a) + tmp_slab(k, 1, a)
            if da == 0:
                bld[k][l] = total.astype(BF)
            else:
                g[where] = total.astype(BF)
                remote(g.at[where], r2[k].at[l, da - 1], q2_s.at[l, k], q2_r.at[l, k], ax.apeer(da)).start()

    fsend = (sp, so, se, fss)
    frecv = (fp, fo, fe, fs)

    def last_moves(l, k):
        out = []
        if k == SH:
            out.append((fss.at[l], fs.at[s], f_s.at[l, k, 0], f_r.at[k, s], dev(l, y, x, z), s == l))
            return out
        for p in (0, 1):
            if k == OU:
                q = 2 * zp + s
                who, me, slot = dev(l, y, x, 2 * zh + p), (s == l) & (zp == p), q
            else:
                yo = 2 * (zp if k == PR else 1 - zp) + s
                who, me, slot = dev(l, yo, x, 2 * zh + p), (s == l) & (yo == y) & (zp == p), y
            out.append((fsend[k].at[2 * l + p], frecv[k].at[slot], f_s.at[l, k, p], f_r.at[k, slot], who, me))
        return out

    @named("sum2")
    def sum2_end(l, k):
        wait_for(r2[k].at[l], q2_r.at[l, k])
        rows, cols = SLAB[k]
        spots = [tmp1.at[pl.ds(rows * d, rows), pl.ds(0, cols)] for d in range(3)]
        cps = [pltpu.make_async_copy(r2[k].at[l, d], spots[d], t_sem.at[5 + d]) for d in range(3)]
        go(cps)
        end(cps)
        total = bld[k][l].astype(F32)
        for d in range(3):
            total = total + tmp1[rows * d:rows * (d + 1), 0:cols].astype(F32)
        if k == SH:
            fss[l] = total.astype(BF)
        else:
            for p in (0, 1):
                fsend[k][2 * l + p] = to32(total[24 * p:24 * (p + 1)])
        for m in last_moves(l, k):
            send_or_keep(*m)

    @named("sum drain")
    def sum_drain(l, k):
        wait_for(r0[k].at[l], q0_s.at[l, k])
        wait_for(r1[k].at[l], q1_s.at[l, k])
        wait_for(r2[k].at[l], q2_s.at[l, k])

    @named("last weights")
    def finish_weights():
        for l in (0, 1):
            for k in range(4):
                for m in last_moves(l, k):
                    sent(*m)
        for k in range(4):
            for i in range(2 if k == SH else 4):
                wait_for(frecv[k].at[i], f_r.at[k, i])

    def vec_copies(stage):
        out = []
        if stage == 0:
            out.append(remote(smt.at[1 - s], sme.at[0, 0], e_s.at[0, 0], e_r.at[0, 0], sib))
            return out
        for d in (1, 2, 3):
            if stage == 1:
                who = crossed.apeer(d)
            elif stage == 2:
                who = crossed.bpeer(d)
            else:
                out.append(remote(sm_out.at[t], sm_out.at[t], e_s.at[3, d - 1], e_r.at[3, d - 1], ypeer(d)))
                continue
            out.append(remote(smt.at[2 + stage], sme.at[stage, d - 1], e_s.at[stage, d - 1], e_r.at[stage, d - 1], who))
        return out

    @named("vectors go")
    def vec_go(stage):
        for c in vec_copies(stage):
            c.start()

    @named("vectors wait")
    def vec_end(stage):
        for c in vec_copies(stage):
            c.wait()
        if stage == 0:
            smt[3] = smt[pl.ds(s, 1)][0] + sme[0, 0]
        elif stage == 1:
            smt[4] = smt[3] + sme[1, 0] + sme[1, 1] + sme[1, 2]
        elif stage == 2:
            sm_out[pl.ds(t, 1)] = (smt[4] + sme[2, 0] + sme[2, 1] + sme[2, 2])[None]

    def wcopy(k, l):
        return pltpu.make_async_copy(w_hbm[k].at[l], w_v[k], w_sem.at[k])

    LEFT, RIGHT = slice(0, 768), slice(768, D)
    COLS = (pl.ds(0, 768), pl.ds(768, 768))
    right, left = ypeer(1), ypeer(3)

    def rows_of(d):
        return at((t + d) % 4 * T, T, T)

    def ysent(buf, i):
        for side in (0, 1):
            wait_for(buf.at[pl.ds(0, 96)], y_s.at[i, side])

    def ag_go(buf, idx):
        for c, side, slot in ((0, 0, 0), (1, 1, 1), (1, 0, 2), (0, 1, 3)):
            blk = buf.at[own, COLS[c]]
            remote(blk, blk, y_s.at[idx, side], y_r.at[idx, slot], (right, left)[side]).start()

    @named("y pass on")
    def ag_pass(buf, idx):
        for side, d in ((0, 3), (1, 1)):
            wait_for(buf.at[pl.ds(0, T), COLS[side]], y_r.at[idx, side])
            blk = buf.at[rows_of(d), COLS[side]]
            remote(blk, blk, y_s.at[idx, side], y_r.at[idx, 2 + side], (right, left)[side]).start()

    @named("y wait")
    def ag_end(buf, idx):
        for slot in (2, 3):
            wait_for(buf.at[pl.ds(0, T)], y_r.at[idx, slot])
        ysent(buf, idx)

    def go(cps):
        for c in cps:
            c.start()

    @named("y wait")
    def end(cps):
        for c in cps:
            c.wait()

    def reduce_go(idx, name, product):
        def tile(i):
            c = span(i, 768)
            pf[:, c] = product(c)
            sb[0, :, c] = pf[rows_of(2), c].astype(BF)
            remote(sb.at[0, :, c], rb.at[idx % 2, 2, :, c], y_s.at[8 + idx, i], y_r.at[8 + idx, i], ypeer(1 + 2 * i)).start()
            sb[1, :, c] = pf[rows_of(3 - 2 * i), c].astype(BF)
            remote(sb.at[1, :, c], rb.at[idx % 2, 1 - i, :, c], y_s.at[8 + idx, 1 - i], y_r.at[8 + idx, 3 - i],
                   ypeer(3 - 2 * i)).start()
        tile.__name__ = name
        tiles(2, tile)

    @named("y pass on")
    def reduce_pass(idx):
        for side, d in ((0, 1), (1, 3)):
            c = (LEFT, RIGHT)[side]
            wait_for(rb.at[idx % 2, 2, :, COLS[side]], y_r.at[8 + idx, side])
            sb[2, :, c] = (pf[rows_of(d), c] + rb[idx % 2, 2, :, c].astype(F32)).astype(BF)
            remote(sb.at[2, :, COLS[side]], rb.at[idx % 2, side, :, COLS[side]], y_s.at[8 + idx, side],
                   y_r.at[8 + idx, 2 + side], (right, left)[side]).start()

    @named("y wait")
    def reduce_end(idx):
        for side in (0, 1):
            wait_for(rb.at[idx % 2, side], y_r.at[8 + idx, 2 + side])
        ysent(gall, 8 + idx)
        return pf[own, :] + rb[idx % 2, 0].astype(F32) + rb[idx % 2, 1].astype(F32)

    livef = jnp.where(lax.broadcasted_iota(jnp.int32, (T, D), 0).astype(F32) < length, 1.0, 0.0)

    def put_result(l, ref, value, way):
        @pl.when(s == l)
        def _():
            ref[pl.ds(s, 1)] = value[None]

        @pl.when(s != l)
        def _():
            ostage[way] = value
            remote(ostage.at[way], ref.at[s], x_s.at[way], x_r.at[way], sib).start()

    @named("last results")
    def finish_results():
        for way, ref in enumerate((act_out, ig_out)):
            remote(ostage.at[way], ref.at[s], x_s.at[way], x_r.at[way], sib).wait()

    def nothing():
        pass

    def forward(l, hidden, hooks):
        hook = lambda name: hooks.get(name, nothing)()
        if l:
            with jax.named_scope("norm first"):
                xh, rsd = stats(hidden)
                xh1[l] = xh
                rd1[l] = jnp.broadcast_to(rsd, (T, 128))
                normed[l, own, :] = (xh * small[l, 0:1, :] + small[l, 1:2, :]).astype(BF)
            ag_go(normed.at[l], l * 2)
            hook("normed")
            ag_pass(normed.at[l], l * 2)
            hook("normed2")
            ag_end(normed.at[l], l * 2)
        if l:
            wcopy(PR, 1).wait()
        with jax.named_scope("queries keys values"):
            for part in range(3):
                if l == 0:
                    gather_d(0, PARTS[part])
                joined = nn(normed[l], vp[:, part * HW:(part + 1) * HW]) + small[l, 7:8, part * HW:(part + 1) * HW]
                for h in range(3):
                    v = joined[:, h * 128:(h + 1) * 128]
                    if part < 2:
                        v = v * cos_ref[...] + pltpu.roll(v, 64, 1) * sin_ref[...]
                    qkv[l, :, part * HW + h * 128:part * HW + (h + 1) * 128] = v.astype(BF)
        hook("joined")
        with jax.named_scope("attention"):
            for h in range(3):
                q = qkv[l, :, h * 128:(h + 1) * 128]
                k = qkv[l, :, HW + h * 128:HW + (h + 1) * 128]
                v = qkv[l, :, 2 * HW + h * 128:2 * HW + (h + 1) * 128]
                sc = jnp.where(vis[...] > 0.5, nt(q, k) * SCALE, MASKED)
                top = jnp.max(sc, axis=-1, keepdims=True)
                ex = jnp.exp(sc - top)
                p = ex * (1.0 / jnp.sum(ex, axis=-1, keepdims=True))
                probs[l, h] = p
                mixed[l, :, h * 128:(h + 1) * 128] = nn(p.astype(BF), v).astype(BF)
        hook("attended")
        if l:
            wcopy(OU, 1).wait()
        reduce_go(l * 2, "out_tile", lambda c: nn(mixed[l], vo[:, c]))
        hook("mixed")
        reduce_pass(l * 2)
        hook("mixed2")
        middle = hidden + reduce_end(l * 2) + small[l, 2:3, :]
        with jax.named_scope("norm second"):
            xh, rsd = stats(middle)
            xh2[l] = xh
            rd2[l] = jnp.broadcast_to(rsd, (T, 128))
            ns[l, own, :] = (xh * small[l, 3:4, :] + small[l, 4:5, :]).astype(BF)
            keep[...] = middle
        ag_go(ns.at[l], l * 2 + 1)
        hook("second")
        ag_pass(ns.at[l], l * 2 + 1)
        hook("second2")
        ag_end(ns.at[l], l * 2 + 1)
        if l:
            wcopy(EX, 1).wait()

        def up_tile(i):
            c = span(i, 256)
            u = nn(ns[l], ve[:, c]) + small[l, 6:7, c]
            unit = lax.broadcasted_iota(jnp.int32, (1, 256), 1) + (i * 256 + D * t)
            m = jnp.where(unit < width, 1.0, 0.0)
            u2 = u * u
            th = jnp.tanh(GC * u * (1.0 + 0.044715 * u2))
            half = 0.5 * (1.0 + th)
            active[l, :, c] = (u * half * m).astype(BF)
            gder[l, :, c] = m * (half + 0.5 * u * (1.0 - th * th) * (GC * (1.0 + 3 * 0.044715 * u2)))
        tiles(6, up_tile)
        hook("upper")
        if l:
            wcopy(SH, 1).wait()
        reduce_go(l * 2 + 1, "down_tile", lambda c: nn(active[l], vs[:, c]))
        if l == 0:
            hook("down")
            reduce_pass(1)
            hook("down2")
            return out_rows(0)

    def out_rows(l):
        result = (keep[...] + reduce_end(l * 2 + 1) + small[l, 5:6, :]) * livef
        result = result.astype(BF)
        put_result(l, act_out, result, 0)
        return result

    def norm_back(dn, xh, rsd, gain):
        e = dn * gain
        return rsd[:, 0:1] * (e - jnp.mean(e, axis=-1, keepdims=True)
                              - xh * jnp.mean(e * xh, axis=-1, keepdims=True))

    def backward(l, g, hooks):
        hook = lambda name: hooks.get(name, nothing)()
        g32 = g.astype(F32)
        smt[l, 5:6, :] = colsum(g32)
        if l == 0:
            gall[own, :] = g
        if l == 0:
            ag_go(gall, 4)
            hook("grad")
            ag_pass(gall, 4)
            hook("grad2")
            ag_end(gall, 4)

        def gs_tile(i):
            c = span(i, 256)
            gbuf(l, SH)[c, :] = tn(active[l, :, c], gall[...]).astype(BF)

        def dact_tile(i):
            c = span(i, 256)
            da = nt(gall[...], vs[c, :]) * gder[l, :, c]
            da = da.astype(BF)
            dup[:, c] = da
            smt[l, 6:7, c] = colsum(da.astype(F32))

        def ge_tile(i):
            c = span(i, 256)
            gbuf(l, EX)[c, :] = tn(ns[l, :, c], dup[...]).astype(BF)

        if l == 0:
            tiles(6, gs_tile)
            sum0_go(0, SH)
            wcopy(SH, 0).wait()
            tiles(6, dact_tile)
            wcopy(EX, 0).wait()
        else:
            end(g_cps)
            tiles(6, gs_tile)
            sum0_go(1, SH)
            tiles(6, dact_tile)
            wcopy(SH, 0).start()
            hook("result")
            reduce_pass(3)
            hook("result2")
            out_rows(1)
        reduce_go(4 + l * 2, "e_tile", lambda c: nt(dup[...], ve[c, :]))
        if l == 1:
            wcopy(EX, 0).start()
        hook("partial")
        tiles(6, ge_tile)
        sum0_go(l, EX)
        hook("upper")
        reduce_pass(4 + l * 2)
        hook("upper2")
        dn = reduce_end(4 + l * 2)
        with jax.named_scope("norm second back"):
            smt[l, 3:4, :] = colsum(dn * xh2[l])
            smt[l, 4:5, :] = colsum(dn)
            dmid = g32 + norm_back(dn, xh2[l], rd2[l], small[l, 3:4, :])
            db = dmid.astype(BF)
            smt[l, 2:3, :] = colsum(db.astype(F32))
            keep[...] = dmid
            dball[own, :] = db
        ag_go(dball, 4 + l * 2 + 1)
        hook("middle")
        ag_pass(dball, 4 + l * 2 + 1)
        hook("middle2")
        ag_end(dball, 4 + l * 2 + 1)
        if l == 0:
            wcopy(OU, 0).wait()
        dmix[...] = nt(dball[...], vo[...]).astype(BF)
        if l == 1:
            wcopy(OU, 0).start()
        with jax.named_scope("attention back"):
            for h in range(3):
                c = slice(h * 128, (h + 1) * 128)
                q = qkv[l, :, h * 128:(h + 1) * 128]
                k = qkv[l, :, HW + h * 128:HW + (h + 1) * 128]
                v = qkv[l, :, 2 * HW + h * 128:2 * HW + (h + 1) * 128]
                p = probs[l, h]
                dm = dmix[:, c]
                dj[:, 2 * HW + h * 128:2 * HW + (h + 1) * 128] = tn(p.astype(BF), dm).astype(BF)
                dp = nt(dm, v)
                dsc = (p * (dp - jnp.sum(dp * p, axis=-1, keepdims=True))).astype(BF)
                for part, v in ((0, nn(dsc, k)), (1, tn(dsc, q))):
                    v = v * SCALE
                    v = v * cos_ref[...] - pltpu.roll(v, 64, 1) * sin_ref[...]
                    dj[:, part * HW + h * 128:part * HW + (h + 1) * 128] = v.astype(BF)
        smt[l, 7:8, :] = jnp.zeros((1, D), F32)
        smt[l, 7:8, 0:QW] = colsum(dj[...].astype(F32))
        if l == 0:
            wcopy(PR, 0).wait()

        hook("scores")

        def gp_tile(i):
            c = span(i, 256)
            gbuf(l, PR)[c, :] = tn(normed[l, :, c], dj[...]).astype(BF)
        tiles(6, gp_tile)
        sum0_go(l, PR)
        hook("project")
        reduce_go(4 + l * 2 + 1, "d_tile", lambda c: nt(dj[...], vp[c, :]))
        if l == 1:
            wcopy(PR, 0).start()
        with jax.named_scope("output term"):
            gbuf(l, OU)[...] = tn(mixed[l], dball[...]).astype(BF)
        sum0_go(l, OU)
        hook("joined")
        reduce_pass(4 + l * 2 + 1)
        hook("joined2")
        dn = reduce_end(4 + l * 2 + 1)
        with jax.named_scope("norm first back"):
            smt[l, 0:1, :] = colsum(dn * xh1[l])
            smt[l, 1:2, :] = colsum(dn)
            dh = keep[...] + norm_back(dn, xh1[l], rd1[l], small[l, 0:1, :])
            res = dh.astype(BF)
        put_result(l, ig_out, res, 1)
        return res

    hall = dball
    hall[own, :] = win_ref[s]
    gall[own, :] = (cot_ref[s].astype(F32) * livef).astype(BF)
    h_cps = [remote(hall.at[own], hall.at[own], m_s.at[d - 1], m_r.at[d - 1], ypeer(d)) for d in (1, 2, 3)]
    g_cps = [remote(gall.at[own], gall.at[own], m_s.at[2 + d], m_r.at[2 + d], ypeer(d)) for d in (1, 2, 3)]
    pack_last = remote(allp.at[s], allp.at[s], p_s.at[3, 0], p_r.at[3, 0], sib)
    with jax.named_scope("greet wait"):
        pl.semaphore_wait(bar, 20)
    pack_go(0)
    go(lcs)

    @pl.when(first)
    def _():
        for m in moves[:4]:
            send_or_keep(*m)
    gather_a(0, PR)
    pack_end(0)
    pack_go(1)
    go(h_cps)

    @pl.when(first)
    def _():
        for m in moves[4:8]:
            send_or_keep(*m)
    for m in moves[12:]:
        send_or_keep(*m)
    for k in PARTS:
        gather_b(0, k)

    @pl.when(first)
    def _():
        for m in moves[8:12]:
            send_or_keep(*m)
    pack_end(1)
    pack_go(2)
    gather_a(0, OU)
    for k in PARTS:
        gather_f(0, k)
    gather_b(0, OU)

    @pl.when(jnp.logical_not(first))
    def _():
        for m in moves[:8]:
            send_or_keep(*m)
    go(g_cps)
    end(lcs)
    row = lax.broadcasted_iota(jnp.int32, (TG, TG), 0)
    col = lax.broadcasted_iota(jnp.int32, (TG, TG), 1)
    limit = jnp.zeros((1, TG), F32)
    blk = lax.broadcasted_iota(jnp.int32, (1, TG), 1) // T
    for r in range(4):
        one = lens[r][0:1, :]
        limit = jnp.where(blk == r, jnp.concatenate([one, one], axis=1), limit)
    ok = (row // T == col // T) & (col <= row) & ((col % T).astype(F32) < limit)
    vis[...] = jnp.where(ok, 1.0, 0.0)
    hidden0 = win_ref[s].astype(F32)
    xh, rsd = stats(hidden0)
    xh1[0] = xh
    rd1[0] = jnp.broadcast_to(rsd, (T, 128))
    pack_end(2)
    pack_last.start()
    gather_a(0, EX)
    for k in PARTS:
        gather_c(0, k)
    gather_f(0, OU)
    end(h_cps)
    pack_last.wait()

    def spread(l, r, width, total, feature):
        n = feature(lax.broadcasted_iota(jnp.int32, (128, total), 1))
        i = lax.broadcasted_iota(jnp.int32, (128, total), 0)
        pick = jnp.where(n - (n // width) * width == i, 1.0, 0.0).astype(BF)
        wide = nn(allp[l, :, r, :].astype(BF), pick)
        n = feature(lax.broadcasted_iota(jnp.int32, (64, total), 1))
        i = lax.broadcasted_iota(jnp.int32, (64, total), 0)
        small[l, r:r + 1, 0:total] = colsum(jnp.where(n // width == (i % 4) * 16 + i // 4, wide, 0.0))

    @named("spread")
    def unpack(l, wanted):
        for r in wanted:
            if r < 6:
                spread(l, r, 24, D, lambda n: n)
            elif r == 6:
                spread(l, r, 96, D, lambda n: n + D * t)
            else:
                spread(l, r, 72, QW, lambda n: n + (n // HW) * (D - HW) + HW * t)

    unpack(0, (0, 1, 7))

    def norm_tile(i):
        rows = span(i, T)
        wide, _ = stats(hall[rows, :].astype(F32))
        normed[0, rows, :] = (wide * small[0, 0:1, :] + small[0, 1:2, :]).astype(BF)
    tiles(4, norm_tile)
    gather_b(0, EX)

    def steps(*todo):
        def run():
            for what, *args in todo:
                what(*args)
        return run

    def second_shards():
        @pl.when(jnp.logical_not(first))
        def _():
            for m in moves[8:12]:
                send_or_keep(*m)

    def reload(k):
        gather_drain(0, k)
        save(k).wait()
        gather_d(1, k)
        wcopy(k, 1).start()

    ga, gb, gf, gc, gd = gather_a, gather_b, gather_f, gather_c, gather_d
    first_hooks = dict(
        joined=steps((gc, 0, OU), (ga, 0, SH)),
        attended=steps((gd, 0, OU)),
        mixed=steps((unpack, 0, (2, 3, 4, 5, 6)), (gf, 0, EX), (gb, 0, SH)),
        mixed2=steps((ga, 1, PR), (ga, 1, OU), (gc, 0, EX)),
        second=steps((unpack, 1, (0, 1, 2, 3, 4, 5, 6, 7))),
        second2=steps((gf, 0, SH), (gb, 1, PR), (gb, 1, OU), (gd, 0, EX)),
        upper=steps((gc, 0, SH), (second_shards,), (gd, 0, SH)),
        down=steps((gf, 1, PR), (gf, 1, OU), (ga, 1, SH)),
        down2=steps((ga, 1, EX), (gc, 1, PR)))
    second_hooks = dict(
        normed2=steps((gc, 1, OU), (gb, 1, EX), (gb, 1, SH), (reload, PR)),
        joined=steps((reload, OU)),
        mixed=steps((gf, 1, EX)),
        mixed2=steps((gf, 1, SH), (gc, 1, EX)),
        second2=steps((gc, 1, SH), (reload, EX)),
        upper=steps((reload, SH)))
    a1 = forward(0, hidden0, first_hooks)
    forward(1, a1.astype(F32), second_hooks)

    for k in range(4):
        gather_drain(1, k)
    for m in moves:
        sent(*m)

    load, fin, ml, mf, ll, lf = sum0_load, sum0_fin, mid_load, mid_fin, last_load, last_fin

    def mid(l, k):
        mid_load(l, k)
        mid_fin(l, k)

    def last(l, k):
        last_load(l, k)
        last_fin(l, k)

    ig2 = backward(1, gall[own, :], dict(
        result2=steps((load, 1, SH), (fin, 1, SH)),
        upper2=steps((ml, 1, SH), (load, 1, EX), (mf, 1, SH), (fin, 1, EX)),
        middle2=steps((ll, 1, SH), (ml, 1, EX), (mf, 1, EX), (lf, 1, SH)),
        joined=steps((load, 1, PR), (fin, 1, PR)),
        joined2=steps((load, 1, OU), (ll, 1, EX), (fin, 1, OU), (lf, 1, EX))))
    g1 = (ig2.astype(F32) * livef).astype(BF)
    backward(0, g1, dict(
        grad=steps((sum2_end, 1, SH), (sum_drain, 1, SH)),
        grad2=steps((ml, 1, PR), (mf, 1, PR), (mid, 1, OU), (sum_drain, 1, EX)),
        partial=steps((load, 0, SH), (fin, 0, SH)),
        upper2=steps((ll, 1, PR), (ml, 0, SH), (lf, 1, PR), (mf, 0, SH)),
        middle=steps((load, 0, EX), (ll, 1, OU), (fin, 0, EX), (lf, 1, OU)),
        middle2=steps((sum2_end, 1, EX), (sum2_end, 1, PR)),
        project=steps((ml, 0, EX), (mf, 0, EX)),
        joined=steps((load, 0, PR), (ll, 0, SH), (fin, 0, PR), (lf, 0, SH)),
        joined2=steps((load, 0, OU), (fin, 0, OU), (last, 0, EX))))
    vec_go(0)
    mid(0, PR)
    vec_end(0)
    vec_go(1)
    mid(0, OU)
    sum2_end(0, SH)
    last(0, PR)
    vec_end(1)
    vec_go(2)
    last(0, OU)
    sum2_end(1, OU)
    sum2_end(0, EX)
    vec_end(2)
    vec_go(3)
    sum2_end(0, PR)
    sum2_end(0, OU)
    vec_end(3)
    finish_weights()
    finish_results()
    for k in range(4):
        for l in (0, 1):
            if (l, k) not in ((1, SH), (1, EX)):
                sum_drain(l, k)


def finish_kernel(act, ig, sums, fp, fo, fe, fs,
                  act_out, ig_out, o0, o1, d_pw, o7, d_ow, o2, o3, o4, d_ew, o6, d_sw, o5):
    chip = lax.axis_index("dp")
    act_out[0, :, 0] = act[...]
    ig_out[0, :, 0] = ig[...]
    for r in range(4):
        for p in range(3):
            d_pw[0, :, p * D + HW * r:p * D + HW * (r + 1)] = fp[r, :, HW * p:HW * (p + 1)].astype(F32)[:24]
        d_ow[0, :, HW * r:HW * (r + 1)] = fo[r].astype(F32)[:24]
        d_ew[0, :, D * r:D * (r + 1)] = fe[r].astype(F32)[:24]
    for j in range(2):
        d_sw[0, :, 768 * j:768 * (j + 1)] = fs[j].astype(F32)
    total = sums[0] + sums[1] + sums[2] + sums[3]
    mine = pltpu.roll(total, (D - 24 * chip) % D, 1)
    for r, o in enumerate((o0, o1, o2, o3, o4, o5)):
        o[...] = mine[r:r + 1, :24]
    units = sums[chip // 16]
    o6[...] = pltpu.roll(units, (D - 96 * (chip % 16)) % D, 1)[6:7, :96]
    cols = jnp.concatenate([sums[r, :, HW * p:HW * (p + 1)] for p in range(3) for r in range(4)], axis=1)
    o7[...] = pltpu.roll(cols, (3 * D - 72 * chip) % (3 * D), 1)[7:8, :72]


def core_call(*args):
    sd = jax.ShapeDtypeStruct
    V = pltpu.VMEM
    DMA = pltpu.SemaphoreType.DMA
    hbm = [sd((2,) + f, BF) for f in FULL]
    hbm += [sd((2, 2, HW, QW), BF), sd((2, 2, HW, HW), BF), sd((2, 2, HW, D), BF), sd((2, D, 768), BF)]
    hbm += [sd((2, 3, 4 * f[0], f[1]), BF) for f in SLAB]
    hbm += [sd((2, 3) + f, BF) for f in SLAB]
    out = pl.pallas_call(
        core_kernel,
        out_shape=[sd((2, T, D), BF), sd((2, T, D), BF), sd((4, 8, D), F32),
                   sd((4, 32, QW), BF), sd((4, 32, HW), BF), sd((4, 32, D), BF), sd((2, 96, 768), BF)] + hbm,
        in_specs=[VM] * 2 + [pl.BlockSpec(memory_space=pltpu.SMEM)] * 2 + [VM] * 14,
        out_specs=[VM] * 7 + [ANY] * 16,
        scratch_shapes=[
            V((D, QW), BF), V((HW, D), BF), V((D, D), BF), V((D, D), BF),
            V((D, QW), BF), V((HW, D), BF), V((D, D), BF), V((D, D), BF),
            V((2, TG, D), BF), V((2, TG, D), BF), V((TG, D), BF), V((TG, D), BF),
            V((2, TG, QW), BF), V((2, 3, TG, TG), F32), V((2, TG, HW), BF),
            V((2, TG, D), F32), V((2, TG, D), BF),
            V((2, T, D), F32), V((2, T, D), F32), V((2, T, 128), F32), V((2, T, 128), F32),
            V((TG, D), F32), V((3, T, D), BF), V((2, 3, T, D), BF),
            V((TG, D), BF), V((TG, QW), BF), V((TG, HW), BF), V((TG, TG), F32), V((4, 8, 128), F32),
            V((T, D), F32), V((2, T, D), BF),
            V((4, 32, QW), BF), V((4, 32, HW), BF), V((4, 32, D), BF),
            V((2, 2, 32, QW), BF), V((2, 2, 32, HW), BF), V((2, 2, 32, D), BF), V((2, 96, 768), BF),
            V((2, 48, QW), BF), V((2, 48, HW), BF), V((2, 48, D), BF),
            V((2, 96, 768), BF),
            V((768, D), BF), V((576, D), BF), V((2, 64, 8, 128), F32), V((2, 8, D), F32), V((5, 8, D), F32), V((3, 3, 8, D), F32),
            DMA((16, 2)), DMA((16, 4)), DMA((4,)), DMA((4,)), DMA((4,)), DMA((3,)), DMA((3,)),
            DMA((3, 4)), DMA((2,)), DMA((3, 2, 2)), DMA((2,)), DMA((4, 3)), DMA((4, 3)),
            DMA((2, 7)), DMA((2, 7)), DMA((2, 7)), DMA((2, 2, 7)), DMA((2, 7)), DMA((2, 7)), DMA((2, 7)),
            DMA((2, 4)), DMA((2, 4)), DMA((2, 4)), DMA((2, 4)), DMA((2, 4)), DMA((2, 4)), DMA((9,)),
            DMA((2, 4, 2)), DMA((4, 4)), DMA((4, 3)), DMA((4, 3)), DMA((6,)), DMA((6,)), pltpu.SemaphoreType.REGULAR, DMA((2, 7)), DMA((2, 4)), DMA((4,)),
        ],
        compiler_params=pltpu.CompilerParams(collective_id=1, has_side_effects=True,
                                             vmem_limit_bytes=64 * 2**20 - 2**16),
    )(*args)
    return out[:7]


def finish_call(*args):
    def sd(*shape):
        return jax.ShapeDtypeStruct(shape, F32)
    rows = jax.ShapeDtypeStruct((1, 2, 1, T, D), BF)
    row = sd(1, 24)
    return pl.pallas_call(
        finish_kernel,
        out_shape=[rows, rows, row, row, sd(1, 24, 3 * D), sd(1, 72), sd(1, 24, D), row, row, row,
                   sd(1, 24, 4 * D), sd(1, 96), sd(1, 96, D), row],
        in_specs=[VM] * 7,
        out_specs=[VM] * 14,
        compiler_params=pltpu.CompilerParams(vmem_limit_bytes=64 * 2**20 - 2**16),
    )(*args)


def rotary():
    half = 64
    rates = (np.float32(10000.0) ** (-np.arange(half, dtype=np.float32) / np.float32(half))).astype(np.float32)
    ang = np.arange(T, dtype=np.float32)[:, None] * rates[None, :]
    cos, sin = np.cos(ang), np.sin(ang)
    cos2 = np.concatenate([cos, cos], axis=1)
    sin2 = np.concatenate([-sin, sin], axis=1)
    return np.tile(cos2, (4, 1)).astype(np.float32), np.tile(sin2, (4, 1)).astype(np.float32)


def per_device(window_input, cotangent, lengths, widths, gain_first, shift_first, project_weight, project_bias,
               output_weight, output_bias, gain_second, shift_second, expand_weight, expand_bias,
               shrink_weight, shrink_bias):
    cos2, sin2 = rotary()
    parts = core_call(
        window_input[:, 0], cotangent[:, 0], lengths.reshape(2), widths, gain_first, shift_first, output_bias, gain_second,
        shift_second, shrink_bias, expand_bias, project_bias, jnp.asarray(cos2), jnp.asarray(sin2),
        project_weight, output_weight, expand_weight, shrink_weight)
    return tuple(finish_call(*parts))


def solution(mesh):
    row = P("section", "dp")
    mat = P("section", "dp", None)
    params = (row, row, mat, row, mat, row, row, row, mat, row, mat, row)
    seq = P(None, "dp", None, None)
    out = P("section", None, "dp", None, None)
    return jax.shard_map(
        per_device, mesh=mesh,
        in_specs=(seq, seq, P(None, "dp"), P()) + params,
        out_specs=(out, out) + params,
        check_vma=False,
    )
```

```python
import jax
import jax.numpy as jnp
import numpy as np
from jax import lax
from jax.experimental import pallas as pl
from jax.experimental.pallas import tpu as pltpu
from jax.sharding import PartitionSpec as P

MESH = pl.DeviceIdType.MESH
ANY = pl.BlockSpec(memory_space=pl.ANY)
VM = pl.BlockSpec(memory_space=pltpu.VMEM)
EPS = 1e-05
MASKED = -1e9
BF = jnp.bfloat16
F32 = jnp.float32
D = 1536
T = 64
TG = 256
HW = 384
QW = 1152
SCALE = 128 ** -0.5
GC = (2 / np.pi) ** 0.5
PR, OU, EX, SH = range(4)
PARTS = (4, 5, 6)
FULL = ((D, QW), (HW, D), (D, D), (D, D))
SLAB = ((48, QW), (48, HW), (48, D), (96, 768))


def nn(a, b):
    return jnp.dot(a, b, preferred_element_type=F32)


def nt(a, b):
    return lax.dot_general(a, b, (((1,), (1,)), ((), ())), preferred_element_type=F32)


def tn(a, b):
    return lax.dot_general(a, b, (((0,), (0,)), ((), ())), preferred_element_type=F32)


def tiles(count, body):
    def step(i, carry):
        body(i)
        return carry
    with jax.named_scope(body.__name__):
        lax.fori_loop(0, count, step, 0)


def span(i, size):
    return pl.ds(pl.multiple_of(i * size, size), size)


def at(start, size, unit):
    return pl.ds(pl.multiple_of(start, unit), size)


def stats(x):
    mean = jnp.mean(x, axis=-1, keepdims=True)
    c = x - mean
    var = jnp.mean(c * c, axis=-1, keepdims=True)
    rs = lax.rsqrt(var + EPS)
    return c * rs, rs


def named(name):
    def deco(fn):
        def inner(*args):
            with jax.named_scope(name):
                return fn(*args)
        return inner
    return deco


def colsum(v):
    return jnp.sum(v, axis=0, keepdims=True)


def to32(v):
    v = v.astype(F32)
    return jnp.concatenate([v, jnp.zeros((8, v.shape[1]), F32)], axis=0).astype(BF)


def core_kernel(win_ref, cot_ref, len_ref, wid_ref, v0, v1, v2, v3, v4, v5, v6, v7, cos_ref, sin_ref, pw, ow, ew, sw,
                act_out, ig_out, sm_out, fp, fo, fe, fs,
                wp, wo, we, ws, r0p, r0o, r0e, r0s, r1p, r1o, r1e, r1s, r2p, r2o, r2e, r2s,
                vp, vo, ve, vs, up, uo, ue, us_,
                normed, ns, gall, dball, qkv, probs, mixed, gder, active, xh1, xh2, rd1, rd2,
                pf, sb, rb, dup, dj, dmix, vis, lens, keep, ostage,
                sp, so, se, cp, co, ce, cs, bp, bo, be, fss,
                tmp, tmp1, allp, small, smt, sme,
                y_s, y_r, w_sem, x_s, x_r, l_s, l_r, z_s, zo_s, z_r, zs_r, p_s, p_r,
                a_s, a_r, b_s, b_r, c_s, c_r, o_sem, q0_s, q0_r, q1_s, q1_r, q2_s, q2_r, t_sem,
                f_s, f_r, e_s, e_r, m_s, m_r, token, f2_r, qf_r, v_sem):
    s = lax.axis_index("section")
    chip = lax.axis_index("dp")
    y, x, z = chip // 16, (chip // 4) % 4, chip % 4
    t = y
    zp = z % 2
    zh = z // 2
    first = s == 0

    def dev(core, cy, cx, cz):
        return (core, cy * 16 + cx * 4 + cz)

    def ypeer(d):
        return dev(s, (y + d) % 4, x, z)

    class Axes:
        def __init__(self, straight):
            self.straight = straight
            self.a, self.b = self.grid(x, z)

        def grid(self, a, b):
            return jnp.where(self.straight, a, b), jnp.where(self.straight, b, a)

        def apeer(self, d):
            cx, cz = self.grid((self.a + d) % 4, self.b)
            return dev(s, y, cx, cz)

        def bpeer(self, d):
            cx, cz = self.grid(self.a, (self.b + d) % 4)
            return dev(s, y, cx, cz)

    crossed, same = Axes(first), Axes(False)
    gather_axes = (crossed, same, crossed, crossed, crossed, crossed, crossed)
    sum_axes = (crossed, crossed, crossed, crossed)

    sib = dev(1 - s, y, x, z)
    own = at(t * T, T, T)

    bar = pltpu.get_barrier_semaphore()

    def greet(who):
        pl.semaphore_signal(bar, inc=1, device_id=who, device_id_type=MESH)

    with jax.named_scope("greet"):
        for d in (1, 2, 3):
            for core in (s, 1 - s):
                greet(dev(core, (y + d) % 4, x, z))
        for d in (0, 1, 2, 3):
            for core in (s, 1 - s):
                greet(dev(core, (y + d) % 4, x, 2 * zh + 1 - zp))
        greet(sib)
        for d in (1, 2, 3):
            greet(dev(s, y, (x + d) % 4, z))
        for d in (0, 1):
            greet(dev(s, y, x, 2 * (1 - zh) + d))

    def remote(src, dst, ssem, rsem, who):
        return pltpu.make_async_remote_copy(src_ref=src, dst_ref=dst, send_sem=ssem, recv_sem=rsem,
                                            device_id=who, device_id_type=MESH)

    def wait_for(ref, sem):
        pltpu.make_async_copy(ref, ref, sem).wait()

    w_hbm = (wp, wo, we, ws)
    w_v = (vp, vo, ve, vs)
    g_v = (up, uo, ue, us_)
    r0 = (r0p, r0o, r0e, r0s)
    r1 = (r1p, r1o, r1e, r1s)
    r2 = (r2p, r2o, r2e, r2s)

    def slab_at(k, j, cx, cz):
        if k not in (OU, SH):
            half = 1 - cz % 2 if k == EX else cz % 2
            return at(48 * (8 * (2 * half + j) + 2 * cx + cz // 2), 48, 48), slice(None)
        if k == OU:
            return at(48 * (2 * cx + cz // 2), 48, 48), at(HW * (2 * (cz % 2) + j), HW, HW)
        return at(96 * (4 * cx + cz), 96, 96), at(768 * j, 768, 768)

    def slab_of(ref, k, axes, a, b):
        cx, cz = axes.grid(a, b)
        return ref.at[slab_at(k, s, cx, cz)]

    def parts_of(ref, k, j):
        if k not in (OU, SH):
            return [ref.at[at(HW * (2 * p + j), HW, HW)] for p in (0, 1)]
        if k == OU:
            return [ref.at[:, at(HW * (2 * p + j), HW, HW)] for p in (0, 1)]
        return [ref.at[:, at(768 * j, 768, 768)]]

    def bulk(ref, k, slabs):
        if k == OU:
            return ref.at[pl.ds(0, 12 * slabs)] if slabs > 3 else ref.at[pl.ds(0, 144), pl.ds(0, HW)]
        return ref.at[pl.ds(0, 48 * slabs)]

    def piece_target(yt, half):
        return dev(y % 2, yt, x, 2 * zh + half), (yt == y) & (s == y % 2) & (zp == half)

    def out_target(q):
        return dev(q % 2, y, x, 2 * zh + q // 2), (zp == q // 2) & (s == q % 2)

    def send_or_keep(src, dst, ssem, rsem, who, is_me):
        @pl.when(is_me)
        def _():
            pltpu.make_async_copy(src, dst, rsem).start()

        @pl.when(jnp.logical_not(is_me))
        def _():
            remote(src, dst, ssem, rsem, who).start()

    def sent(src, dst, ssem, rsem, who, is_me):
        @pl.when(jnp.logical_not(is_me))
        def _():
            remote(src, dst, ssem, rsem, who).wait_send()

    def shard_moves():
        out = []
        for yt in range(4):
            who, me = piece_target(yt, y // 2)
            out.append((sp.at[yt], cp.at[s, zp], z_s.at[0, yt], z_r.at[0, s, zp], who, me))
        for q in range(4):
            who, me = out_target(q)
            out.append((so.at[q], co.at[s, zp], z_s.at[1, q], z_r.at[1, s, zp], who, me))
        for yt in range(4):
            who, me = piece_target(yt, 1 - y // 2)
            out.append((se.at[yt], ce.at[s, zp], z_s.at[2, yt], z_r.at[2, s, zp], who, me))
        for j in range(2):
            out.append((sw.at[0, :, pl.ds(768 * j, 768)], cs.at[s], zo_s.at[j], zs_r.at[s],
                        dev(j, y, x, z), s == j))
        return out

    moves = shard_moves()
    with jax.named_scope("shards"):
        for yt in range(4):
            sp[yt] = to32(jnp.concatenate([pw[0, :, p * D + HW * yt:p * D + HW * (yt + 1)] for p in range(3)], axis=1))
        for q in range(4):
            so[q] = to32(ow[0, :, HW * q:HW * (q + 1)])
        for yt in range(4):
            se[yt] = to32(ew[0, :, D * yt:D * (yt + 1)])

    spot = (chip % 16) * 4 + y
    allp[s, pl.ds(spot, 1)] = jnp.zeros((1, 8, 128), F32)
    for r, v in enumerate((v0, v1, v2, v3, v4, v5, v6, v7)):
        allp[s, pl.ds(spot, 1), r:r + 1, 0:v.shape[1]] = v[...].astype(F32)[None]

    def pack_copies(stage):
        out = []
        for d in (1, 2, 3):
            if stage == 0:
                blk, who = allp.at[s, pl.ds(spot, 1)], ypeer(d)
            elif stage == 1:
                blk, who = allp.at[s, at(spot - y, 4, 4)], dev(s, y, x, (z + d) % 4)
            else:
                blk, who = allp.at[s, at(16 * x, 16, 16)], dev(s, y, (x + d) % 4, z)
            out.append(remote(blk, blk, p_s.at[stage, d - 1], p_r.at[stage, d - 1], who))
        return out

    @named("pack go")
    def pack_go(stage):
        for c in pack_copies(stage):
            c.start()

    @named("pack wait")
    def pack_end(stage):
        for c in pack_copies(stage):
            c.wait()

    length = len_ref[s].astype(F32)
    width = wid_ref[s]
    lens[pl.ds(t, 1)] = jnp.full((1, 8, 128), length, F32)
    lcs = [remote(lens.at[pl.ds(t, 1)], lens.at[pl.ds(t, 1)], l_s.at[d - 1], l_r.at[d - 1], ypeer(d)) for d in (1, 2, 3)]

    got = (cp, co, ce, cs)
    bld = (bp, bo, be, cs)

    def home(l, k):
        if k in PARTS:
            return w_v[PR].at[:, pl.ds(HW * (k - 4), HW)]
        return w_hbm[k].at[1] if l else w_v[k]

    def slab_in(l, k):
        return bld[PR].at[l, :, pl.ds(HW * (k - 4), HW)] if k in PARTS else bld[k].at[l]

    def a_copies(l, k):
        src = slab_in(l, k)
        ax = gather_axes[k]
        return [remote(src, slab_of(home(l, k), k, ax, ax.a, ax.b), a_s.at[l, k], a_r.at[l, k], ax.apeer(d))
                for d in (1, 2, 3)]

    def own_copy(l, k):
        ax = gather_axes[k]
        return pltpu.make_async_copy(slab_in(l, k), slab_of(home(l, k), k, ax, ax.a, ax.b), o_sem.at[l, k])

    @named("gather a")
    def gather_a(l, k):
        if k == SH:
            wait_for(cs.at[l], zs_r.at[l])
        else:
            zk = (0, 1, 2)[k]
            for p in (0, 1):
                wait_for(got[k].at[l, p], z_r.at[zk, l, p])
            halves = [got[k][l, p].astype(F32)[:24] for p in (0, 1)]
            bld[k][l] = jnp.concatenate(halves, axis=0).astype(BF)
        for item in PARTS if (l, k) == (0, PR) else (k,):
            go(a_copies(l, item))
            own_copy(l, item).start()

    @named("gather b")
    def gather_b(l, k):
        w, ax = home(l, k), gather_axes[k]
        wait_for(bulk(w, k, 3), a_r.at[l, k])
        own_copy(l, k).wait()
        for a in range(4):
            src = slab_of(w, k, ax, a, ax.b)
            for side, d in ((0, 1), (1, 3)):
                remote(src, src, b_s.at[l, k], b_r.at[side, l, k], ax.bpeer(d)).start()

    @named("gather f")
    def gather_f(l, k):
        w, ax = home(l, k), gather_axes[k]
        for side, d in ((0, 1), (1, 3)):
            wait_for(bulk(w, k, 4), b_r.at[side, l, k])
            for a in (2 * side, 2 * side + 1):
                src = slab_of(w, k, ax, a, (ax.b + 4 - d) % 4)
                remote(src, src, b_s.at[l, k], f2_r.at[l, k], ax.bpeer(d)).start()

    @named("gather c")
    def gather_c(l, k):
        w = home(l, k)
        wait_for(bulk(w, k, 4), f2_r.at[l, k])
        for blk in parts_of(w, k, s):
            remote(blk, blk, c_s.at[l, k], c_r.at[l, k], sib).start()

    @named("gather d")
    def gather_d(l, k):
        wait_for(bulk(home(l, k), k, 16), c_r.at[l, k])
        if l == 0 and k not in (4, 5):
            save(PR if k == 6 else k).start()

    def save(k):
        return pltpu.make_async_copy(w_v[k], w_hbm[k].at[0], v_sem.at[k])

    @named("gather drain")
    def gather_drain(l, k):
        for item in PARTS if (l, k) == (0, PR) else (k,):
            w = home(l, item)
            wait_for(bulk(w, item, 3), a_s.at[l, item])
            wait_for(bulk(w, item, 12), b_s.at[l, item])
            wait_for(bulk(w, item, 16), c_s.at[l, item])

    def gbuf(l, k):
        if l == 0 and k == PR:
            return us_.at[:, pl.ds(0, QW)]
        if l == 0 and k == SH:
            return ue
        return g_v[k] if l else w_v[k]

    @named("sum0 go")
    def sum0_go(l, k):
        for i, blk in enumerate(parts_of(gbuf(l, k), k, 1 - s)):
            dst = r0[k].at[l, i] if k != SH else r0[k].at[l]
            remote(blk, dst, q0_s.at[l, k], q0_r.at[l, k], sib).start()

    def halves_tmp(k):
        if k in (PR, EX):
            return [tmp.at[pl.ds(HW * p, HW), pl.ds(0, FULL[k][1])] for p in (0, 1)]
        if k == OU:
            return [tmp.at[pl.ds(HW * p, HW), pl.ds(0, HW)] for p in (0, 1)]
        return [tmp.at[:, pl.ds(768 * p, 768)] for p in (0, 1)]

    def sum0_copies(l, k):
        srcs = [r0[k].at[l, i] for i in (0, 1)] if k != SH else [r0[k].at[l, pl.ds(768 * i, 768)] for i in (0, 1)]
        return [pltpu.make_async_copy(a, b, t_sem.at[i]) for i, (a, b) in enumerate(zip(srcs, halves_tmp(k)))]

    @named("sum0 load")
    def sum0_load(l, k):
        wait_for(r0[k].at[l], q0_r.at[l, k])
        for c in sum0_copies(l, k):
            c.start()

    @named("sum0")
    def sum0_fin(l, k):
        g, ax = gbuf(l, k), sum_axes[k]
        cps = sum0_copies(l, k)
        for p in (0, 1):
            cps[p].wait()

            def add(i):
                if k in (PR, EX):
                    rows, cols, n = at(HW * (2 * p + s) + 96 * i, 96, 96), slice(None), FULL[k][1]
                    other = tmp[pl.ds(pl.multiple_of(HW * p + 96 * i, 96), 96), 0:n]
                elif k == OU:
                    rows, cols = span(i, 96), at(HW * (2 * p + s), HW, HW)
                    other = tmp[pl.ds(pl.multiple_of(HW * p + 96 * i, 96), 96), 0:HW]
                else:
                    rows, cols = at(768 * p + 96 * i, 96, 96), at(768 * s, 768, 768)
                    other = tmp[span(i, 96), 768 * p:768 * p + 768]
                g[rows, cols] = (g[rows, cols].astype(F32) + other.astype(F32)).astype(BF)
            tiles(8 if k == SH else 4, add)
        for a in (0, 2, 1, 3):
            far = 1 if a < 2 else 3
            remote(slab_of(g, k, ax, a, (ax.b + 2) % 4), r1_slab(l, k, 0, a), q1_s.at[l, k], qf_r.at[l, k],
                   ax.bpeer(far)).start()
        for a in (0, 2, 1, 3):
            near = 3 if a < 2 else 1
            remote(slab_of(g, k, ax, a, (ax.b + near) % 4), r1_slab(l, k, near, a), q1_s.at[l, k], q1_r.at[l, k],
                   ax.bpeer(near)).start()

    def r1_slab(l, k, d, a):
        rows = SLAB[k][0]
        return r1[k].at[l, (0, 1, None, 2)[d], pl.ds(rows * a, rows)]

    def tmp_set(k, side):
        rows, cols = SLAB[k]
        if k == SH:
            return tmp1.at[pl.ds(0, 4 * rows), pl.ds(cols * side, cols)]
        return tmp1.at[pl.ds(4 * rows * side, 4 * rows), pl.ds(0, cols)]

    def tmp_slab(k, side, a):
        rows, cols = SLAB[k]
        if k == SH:
            return tmp1[at(rows * a, rows, rows), cols * side:cols * (side + 1)].astype(F32)
        return tmp1[at(4 * rows * side + rows * a, rows, rows), 0:cols].astype(F32)

    def mid_copies(l, k):
        rows, cols = SLAB[k]
        if k != SH:
            return [pltpu.make_async_copy(r1[k].at[l, 0], tmp1.at[pl.ds(384, 192), pl.ds(0, cols)], t_sem.at[2])]
        return [pltpu.make_async_copy(r1[k].at[l, 0, pl.ds(192 * i, 192)], tmp1.at[pl.ds(384, 192), pl.ds(768 * i, 768)],
                                      t_sem.at[(2, 8)[i]]) for i in (0, 1)]

    def mid_slab(k, a):
        rows, cols = SLAB[k]
        if k != SH:
            return tmp1[384 + 48 * a:432 + 48 * a, 0:cols].astype(F32)
        return tmp1[384 + 96 * (a % 2):480 + 96 * (a % 2), 768 * (a // 2):768 * (a // 2) + 768].astype(F32)

    @named("sum1 pass load")
    def mid_load(l, k):
        wait_for(r1[k].at[l, 0], qf_r.at[l, k])
        go(mid_copies(l, k))

    @named("sum1 pass on")
    def mid_fin(l, k):
        g, ax = gbuf(l, k), sum_axes[k]
        end(mid_copies(l, k))
        for a in range(4):
            d = 1 if a < 2 else 3
            cx, cz = ax.grid(a, (ax.b + d) % 4)
            where = slab_at(k, s, cx, cz)
            g[where] = (g[where].astype(F32) + mid_slab(k, a)).astype(BF)
            remote(g.at[where], r1_slab(l, k, d, a), q1_s.at[l, k], q1_r.at[l, k], ax.bpeer(d)).start()

    def last_copies(l, k):
        return [pltpu.make_async_copy(r1[k].at[l, 1 + i], tmp_set(k, i), t_sem.at[3 + i]) for i in (0, 1)]

    @named("sum1 load")
    def last_load(l, k):
        wait_for(r1[k].at[l, pl.ds(1, 2)], q1_r.at[l, k])
        go(last_copies(l, k))

    @named("sum1")
    def last_fin(l, k):
        g, ax = gbuf(l, k), sum_axes[k]
        end(last_copies(l, k))
        for da in (2, 1, 3, 0):
            a = (ax.a + da) % 4
            cx, cz = ax.grid(a, ax.b)
            where = slab_at(k, s, cx, cz)
            total = g[where].astype(F32) + tmp_slab(k, 0, a) + tmp_slab(k, 1, a)
            if da == 0:
                bld[k][l] = total.astype(BF)
            else:
                g[where] = total.astype(BF)
                remote(g.at[where], r2[k].at[l, da - 1], q2_s.at[l, k], q2_r.at[l, k], ax.apeer(da)).start()

    fsend = (sp, so, se, fss)
    frecv = (fp, fo, fe, fs)

    def last_moves(l, k):
        out = []
        if k == SH:
            out.append((fss.at[l], fs.at[s], f_s.at[l, k, 0], f_r.at[k, s], dev(l, y, x, z), s == l))
            return out
        for p in (0, 1):
            if k == OU:
                q = 2 * zp + s
                who, me, slot = dev(l, y, x, 2 * zh + p), (s == l) & (zp == p), q
            else:
                yo = 2 * (zp if k == PR else 1 - zp) + s
                who, me, slot = dev(l, yo, x, 2 * zh + p), (s == l) & (yo == y) & (zp == p), y
            out.append((fsend[k].at[2 * l + p], frecv[k].at[slot], f_s.at[l, k, p], f_r.at[k, slot], who, me))
        return out

    @named("sum2")
    def sum2_end(l, k):
        wait_for(r2[k].at[l], q2_r.at[l, k])
        rows, cols = SLAB[k]
        spots = [tmp1.at[pl.ds(rows * d, rows), pl.ds(0, cols)] for d in range(3)]
        cps = [pltpu.make_async_copy(r2[k].at[l, d], spots[d], t_sem.at[5 + d]) for d in range(3)]
        go(cps)
        end(cps)
        total = bld[k][l].astype(F32)
        for d in range(3):
            total = total + tmp1[rows * d:rows * (d + 1), 0:cols].astype(F32)
        if k == SH:
            fss[l] = total.astype(BF)
        else:
            for p in (0, 1):
                fsend[k][2 * l + p] = to32(total[24 * p:24 * (p + 1)])
        for m in last_moves(l, k):
            send_or_keep(*m)

    @named("sum drain")
    def sum_drain(l, k):
        wait_for(r0[k].at[l], q0_s.at[l, k])
        wait_for(r1[k].at[l], q1_s.at[l, k])
        wait_for(r2[k].at[l], q2_s.at[l, k])

    @named("last weights")
    def finish_weights():
        for l in (0, 1):
            for k in range(4):
                for m in last_moves(l, k):
                    sent(*m)
        for k in range(4):
            for i in range(2 if k == SH else 4):
                wait_for(frecv[k].at[i], f_r.at[k, i])

    def vec_copies(stage):
        out = []
        if stage == 0:
            out.append(remote(smt.at[1 - s], sme.at[0, 0], e_s.at[0, 0], e_r.at[0, 0], sib))
            return out
        for d in (1, 2, 3):
            if stage == 1:
                who = crossed.apeer(d)
            elif stage == 2:
                who = crossed.bpeer(d)
            else:
                out.append(remote(sm_out.at[t], sm_out.at[t], e_s.at[3, d - 1], e_r.at[3, d - 1], ypeer(d)))
                continue
            out.append(remote(smt.at[2 + stage], sme.at[stage, d - 1], e_s.at[stage, d - 1], e_r.at[stage, d - 1], who))
        return out

    @named("vectors go")
    def vec_go(stage):
        for c in vec_copies(stage):
            c.start()

    @named("vectors wait")
    def vec_end(stage):
        for c in vec_copies(stage):
            c.wait()
        if stage == 0:
            smt[3] = smt[pl.ds(s, 1)][0] + sme[0, 0]
        elif stage == 1:
            smt[4] = smt[3] + sme[1, 0] + sme[1, 1] + sme[1, 2]
        elif stage == 2:
            sm_out[pl.ds(t, 1)] = (smt[4] + sme[2, 0] + sme[2, 1] + sme[2, 2])[None]

    def wcopy(k, l):
        return pltpu.make_async_copy(w_hbm[k].at[l], w_v[k], w_sem.at[k])

    LEFT, RIGHT = slice(0, 768), slice(768, D)
    COLS = (pl.ds(0, 768), pl.ds(768, 768))
    right, left = ypeer(1), ypeer(3)

    def rows_of(d):
        return at((t + d) % 4 * T, T, T)

    def ysent(buf, i):
        for side in (0, 1):
            wait_for(buf.at[pl.ds(0, 96)], y_s.at[i, side])

    def ag_go(buf, idx):
        for c, side, slot in ((0, 0, 0), (1, 1, 1), (1, 0, 2), (0, 1, 3)):
            blk = buf.at[own, COLS[c]]
            remote(blk, blk, y_s.at[idx, side], y_r.at[idx, slot], (right, left)[side]).start()

    @named("y pass on")
    def ag_pass(buf, idx):
        for side, d in ((0, 3), (1, 1)):
            wait_for(buf.at[pl.ds(0, T), COLS[side]], y_r.at[idx, side])
            blk = buf.at[rows_of(d), COLS[side]]
            remote(blk, blk, y_s.at[idx, side], y_r.at[idx, 2 + side], (right, left)[side]).start()

    @named("y wait")
    def ag_end(buf, idx):
        for slot in (2, 3):
            wait_for(buf.at[pl.ds(0, T)], y_r.at[idx, slot])
        ysent(buf, idx)

    def go(cps):
        for c in cps:
            c.start()

    @named("y wait")
    def end(cps):
        for c in cps:
            c.wait()

    def reduce_go(idx, name, product):
        def tile(i):
            c = span(i, 768)
            pf[:, c] = product(c)
            sb[0, :, c] = pf[rows_of(2), c].astype(BF)
            remote(sb.at[0, :, c], rb.at[idx % 2, 2, :, c], y_s.at[8 + idx, i], y_r.at[8 + idx, i], ypeer(1 + 2 * i)).start()
            sb[1, :, c] = pf[rows_of(3 - 2 * i), c].astype(BF)
            remote(sb.at[1, :, c], rb.at[idx % 2, 1 - i, :, c], y_s.at[8 + idx, 1 - i], y_r.at[8 + idx, 3 - i],
                   ypeer(3 - 2 * i)).start()
        tile.__name__ = name
        tiles(2, tile)

    @named("y pass on")
    def reduce_pass(idx):
        for side, d in ((0, 1), (1, 3)):
            c = (LEFT, RIGHT)[side]
            wait_for(rb.at[idx % 2, 2, :, COLS[side]], y_r.at[8 + idx, side])
            sb[2, :, c] = (pf[rows_of(d), c] + rb[idx % 2, 2, :, c].astype(F32)).astype(BF)
            remote(sb.at[2, :, COLS[side]], rb.at[idx % 2, side, :, COLS[side]], y_s.at[8 + idx, side],
                   y_r.at[8 + idx, 2 + side], (right, left)[side]).start()

    @named("y wait")
    def reduce_end(idx):
        for side in (0, 1):
            wait_for(rb.at[idx % 2, side], y_r.at[8 + idx, 2 + side])
        ysent(gall, 8 + idx)
        return pf[own, :] + rb[idx % 2, 0].astype(F32) + rb[idx % 2, 1].astype(F32)

    livef = jnp.where(lax.broadcasted_iota(jnp.int32, (T, D), 0).astype(F32) < length, 1.0, 0.0)

    def put_result(l, ref, value, way):
        @pl.when(s == l)
        def _():
            ref[pl.ds(s, 1)] = value[None]

        @pl.when(s != l)
        def _():
            ostage[way] = value
            remote(ostage.at[way], ref.at[s], x_s.at[way], x_r.at[way], sib).start()

    @named("last results")
    def finish_results():
        for way, ref in enumerate((act_out, ig_out)):
            remote(ostage.at[way], ref.at[s], x_s.at[way], x_r.at[way], sib).wait()

    def nothing():
        pass

    def forward(l, hidden, hooks):
        hook = lambda name: hooks.get(name, nothing)()
        if l:
            with jax.named_scope("norm first"):
                xh, rsd = stats(hidden)
                xh1[l] = xh
                rd1[l] = jnp.broadcast_to(rsd, (T, 128))
                normed[l, own, :] = (xh * small[l, 0:1, :] + small[l, 1:2, :]).astype(BF)
            ag_go(normed.at[l], l * 2)
            hook("normed")
            ag_pass(normed.at[l], l * 2)
            hook("normed2")
            ag_end(normed.at[l], l * 2)
        if l:
            wcopy(PR, 1).wait()
        with jax.named_scope("queries keys values"):
            for part in range(3):
                if l == 0:
                    gather_d(0, PARTS[part])
                joined = nn(normed[l], vp[:, part * HW:(part + 1) * HW]) + small[l, 7:8, part * HW:(part + 1) * HW]
                for h in range(3):
                    v = joined[:, h * 128:(h + 1) * 128]
                    if part < 2:
                        v = v * cos_ref[...] + pltpu.roll(v, 64, 1) * sin_ref[...]
                    qkv[l, :, part * HW + h * 128:part * HW + (h + 1) * 128] = v.astype(BF)
        hook("joined")
        with jax.named_scope("attention"):
            for h in range(3):
                q = qkv[l, :, h * 128:(h + 1) * 128]
                k = qkv[l, :, HW + h * 128:HW + (h + 1) * 128]
                v = qkv[l, :, 2 * HW + h * 128:2 * HW + (h + 1) * 128]
                sc = jnp.where(vis[...] > 0.5, nt(q, k) * SCALE, MASKED)
                top = jnp.max(sc, axis=-1, keepdims=True)
                ex = jnp.exp(sc - top)
                p = ex * (1.0 / jnp.sum(ex, axis=-1, keepdims=True))
                probs[l, h] = p
                mixed[l, :, h * 128:(h + 1) * 128] = nn(p.astype(BF), v).astype(BF)
        hook("attended")
        if l:
            wcopy(OU, 1).wait()
        reduce_go(l * 2, "out_tile", lambda c: nn(mixed[l], vo[:, c]))
        hook("mixed")
        reduce_pass(l * 2)
        hook("mixed2")
        middle = hidden + reduce_end(l * 2) + small[l, 2:3, :]
        with jax.named_scope("norm second"):
            xh, rsd = stats(middle)
            xh2[l] = xh
            rd2[l] = jnp.broadcast_to(rsd, (T, 128))
            ns[l, own, :] = (xh * small[l, 3:4, :] + small[l, 4:5, :]).astype(BF)
            keep[...] = middle
        ag_go(ns.at[l], l * 2 + 1)
        hook("second")
        ag_pass(ns.at[l], l * 2 + 1)
        hook("second2")
        ag_end(ns.at[l], l * 2 + 1)
        if l:
            wcopy(EX, 1).wait()

        def up_tile(i):
            c = span(i, 256)
            u = nn(ns[l], ve[:, c]) + small[l, 6:7, c]
            unit = lax.broadcasted_iota(jnp.int32, (1, 256), 1) + (i * 256 + D * t)
            m = jnp.where(unit < width, 1.0, 0.0)
            u2 = u * u
            th = jnp.tanh(GC * u * (1.0 + 0.044715 * u2))
            half = 0.5 * (1.0 + th)
            active[l, :, c] = (u * half * m).astype(BF)
            gder[l, :, c] = m * (half + 0.5 * u * (1.0 - th * th) * (GC * (1.0 + 3 * 0.044715 * u2)))
        tiles(6, up_tile)
        hook("upper")
        if l:
            wcopy(SH, 1).wait()
        reduce_go(l * 2 + 1, "down_tile", lambda c: nn(active[l], vs[:, c]))
        if l == 0:
            hook("down")
            reduce_pass(1)
            hook("down2")
            return out_rows(0)

    def out_rows(l):
        result = (keep[...] + reduce_end(l * 2 + 1) + small[l, 5:6, :]) * livef
        result = result.astype(BF)
        put_result(l, act_out, result, 0)
        return result

    def norm_back(dn, xh, rsd, gain):
        e = dn * gain
        return rsd[:, 0:1] * (e - jnp.mean(e, axis=-1, keepdims=True)
                              - xh * jnp.mean(e * xh, axis=-1, keepdims=True))

    def backward(l, g, hooks):
        hook = lambda name: hooks.get(name, nothing)()
        g32 = g.astype(F32)
        smt[l, 5:6, :] = colsum(g32)
        if l == 0:
            gall[own, :] = g
        if l == 0:
            ag_go(gall, 4)
            hook("grad")
            ag_pass(gall, 4)
            hook("grad2")
            ag_end(gall, 4)

        def gs_tile(i):
            c = span(i, 256)
            gbuf(l, SH)[c, :] = tn(active[l, :, c], gall[...]).astype(BF)

        def dact_tile(i):
            c = span(i, 256)
            da = nt(gall[...], vs[c, :]) * gder[l, :, c]
            da = da.astype(BF)
            dup[:, c] = da
            smt[l, 6:7, c] = colsum(da.astype(F32))

        def ge_tile(i):
            c = span(i, 256)
            gbuf(l, EX)[c, :] = tn(ns[l, :, c], dup[...]).astype(BF)

        if l == 0:
            tiles(6, gs_tile)
            sum0_go(0, SH)
            wcopy(SH, 0).wait()
            tiles(6, dact_tile)
            wcopy(EX, 0).wait()
        else:
            end(g_cps)
            tiles(6, gs_tile)
            sum0_go(1, SH)
            tiles(6, dact_tile)
            wcopy(SH, 0).start()
            hook("result")
            reduce_pass(3)
            hook("result2")
            out_rows(1)
        reduce_go(4 + l * 2, "e_tile", lambda c: nt(dup[...], ve[c, :]))
        if l == 1:
            wcopy(EX, 0).start()
        hook("partial")
        tiles(6, ge_tile)
        sum0_go(l, EX)
        hook("upper")
        reduce_pass(4 + l * 2)
        hook("upper2")
        dn = reduce_end(4 + l * 2)
        with jax.named_scope("norm second back"):
            smt[l, 3:4, :] = colsum(dn * xh2[l])
            smt[l, 4:5, :] = colsum(dn)
            dmid = g32 + norm_back(dn, xh2[l], rd2[l], small[l, 3:4, :])
            db = dmid.astype(BF)
            smt[l, 2:3, :] = colsum(db.astype(F32))
            keep[...] = dmid
            dball[own, :] = db
        ag_go(dball, 4 + l * 2 + 1)
        hook("middle")
        ag_pass(dball, 4 + l * 2 + 1)
        hook("middle2")
        ag_end(dball, 4 + l * 2 + 1)
        if l == 0:
            wcopy(OU, 0).wait()
        dmix[...] = nt(dball[...], vo[...]).astype(BF)
        if l == 1:
            wcopy(OU, 0).start()
        with jax.named_scope("attention back"):
            for h in range(3):
                c = slice(h * 128, (h + 1) * 128)
                q = qkv[l, :, h * 128:(h + 1) * 128]
                k = qkv[l, :, HW + h * 128:HW + (h + 1) * 128]
                v = qkv[l, :, 2 * HW + h * 128:2 * HW + (h + 1) * 128]
                p = probs[l, h]
                dm = dmix[:, c]
                dj[:, 2 * HW + h * 128:2 * HW + (h + 1) * 128] = tn(p.astype(BF), dm).astype(BF)
                dp = nt(dm, v)
                dsc = (p * (dp - jnp.sum(dp * p, axis=-1, keepdims=True))).astype(BF)
                for part, v in ((0, nn(dsc, k)), (1, tn(dsc, q))):
                    v = v * SCALE
                    v = v * cos_ref[...] - pltpu.roll(v, 64, 1) * sin_ref[...]
                    dj[:, part * HW + h * 128:part * HW + (h + 1) * 128] = v.astype(BF)
        smt[l, 7:8, :] = jnp.zeros((1, D), F32)
        smt[l, 7:8, 0:QW] = colsum(dj[...].astype(F32))
        if l == 0:
            wcopy(PR, 0).wait()

        hook("scores")

        def gp_tile(i):
            c = span(i, 256)
            gbuf(l, PR)[c, :] = tn(normed[l, :, c], dj[...]).astype(BF)
        tiles(6, gp_tile)
        sum0_go(l, PR)
        hook("project")
        reduce_go(4 + l * 2 + 1, "d_tile", lambda c: nt(dj[...], vp[c, :]))
        if l == 1:
            wcopy(PR, 0).start()
        with jax.named_scope("output term"):
            gbuf(l, OU)[...] = tn(mixed[l], dball[...]).astype(BF)
        sum0_go(l, OU)
        hook("joined")
        reduce_pass(4 + l * 2 + 1)
        hook("joined2")
        dn = reduce_end(4 + l * 2 + 1)
        with jax.named_scope("norm first back"):
            smt[l, 0:1, :] = colsum(dn * xh1[l])
            smt[l, 1:2, :] = colsum(dn)
            dh = keep[...] + norm_back(dn, xh1[l], rd1[l], small[l, 0:1, :])
            res = dh.astype(BF)
        put_result(l, ig_out, res, 1)
        return res

    hall = dball
    hall[own, :] = win_ref[s]
    gall[own, :] = (cot_ref[s].astype(F32) * livef).astype(BF)
    h_cps = [remote(hall.at[own], hall.at[own], m_s.at[d - 1], m_r.at[d - 1], ypeer(d)) for d in (1, 2, 3)]
    g_cps = [remote(gall.at[own], gall.at[own], m_s.at[2 + d], m_r.at[2 + d], ypeer(d)) for d in (1, 2, 3)]
    pack_last = remote(allp.at[s], allp.at[s], p_s.at[3, 0], p_r.at[3, 0], sib)
    with jax.named_scope("greet wait"):
        pl.semaphore_wait(bar, 20)
    pack_go(0)
    go(lcs)

    @pl.when(first)
    def _():
        for m in moves[:4]:
            send_or_keep(*m)
    gather_a(0, PR)
    pack_end(0)
    pack_go(1)
    go(h_cps)

    @pl.when(first)
    def _():
        for m in moves[4:8]:
            send_or_keep(*m)
    for m in moves[12:]:
        send_or_keep(*m)
    for k in PARTS:
        gather_b(0, k)

    @pl.when(first)
    def _():
        for m in moves[8:12]:
            send_or_keep(*m)
    pack_end(1)
    pack_go(2)
    gather_a(0, OU)
    for k in PARTS:
        gather_f(0, k)
    gather_b(0, OU)

    @pl.when(jnp.logical_not(first))
    def _():
        for m in moves[:8]:
            send_or_keep(*m)
    go(g_cps)
    end(lcs)
    row = lax.broadcasted_iota(jnp.int32, (TG, TG), 0)
    col = lax.broadcasted_iota(jnp.int32, (TG, TG), 1)
    limit = jnp.zeros((1, TG), F32)
    blk = lax.broadcasted_iota(jnp.int32, (1, TG), 1) // T
    for r in range(4):
        one = lens[r][0:1, :]
        limit = jnp.where(blk == r, jnp.concatenate([one, one], axis=1), limit)
    ok = (row // T == col // T) & (col <= row) & ((col % T).astype(F32) < limit)
    vis[...] = jnp.where(ok, 1.0, 0.0)
    hidden0 = win_ref[s].astype(F32)
    xh, rsd = stats(hidden0)
    xh1[0] = xh
    rd1[0] = jnp.broadcast_to(rsd, (T, 128))
    pack_end(2)
    pack_last.start()
    gather_a(0, EX)
    for k in PARTS:
        gather_c(0, k)
    gather_f(0, OU)
    end(h_cps)
    pack_last.wait()

    def spread(l, r, width, total, feature):
        n = feature(lax.broadcasted_iota(jnp.int32, (128, total), 1))
        i = lax.broadcasted_iota(jnp.int32, (128, total), 0)
        pick = jnp.where(n - (n // width) * width == i, 1.0, 0.0).astype(BF)
        wide = nn(allp[l, :, r, :].astype(BF), pick)
        n = feature(lax.broadcasted_iota(jnp.int32, (64, total), 1))
        i = lax.broadcasted_iota(jnp.int32, (64, total), 0)
        small[l, r:r + 1, 0:total] = colsum(jnp.where(n // width == (i % 4) * 16 + i // 4, wide, 0.0))

    @named("spread")
    def unpack(l, wanted):
        for r in wanted:
            if r < 6:
                spread(l, r, 24, D, lambda n: n)
            elif r == 6:
                spread(l, r, 96, D, lambda n: n + D * t)
            else:
                spread(l, r, 72, QW, lambda n: n + (n // HW) * (D - HW) + HW * t)

    unpack(0, (0, 1, 7))

    def norm_tile(i):
        rows = span(i, T)
        wide, _ = stats(hall[rows, :].astype(F32))
        normed[0, rows, :] = (wide * small[0, 0:1, :] + small[0, 1:2, :]).astype(BF)
    tiles(4, norm_tile)
    gather_b(0, EX)

    def steps(*todo):
        def run():
            for what, *args in todo:
                what(*args)
        return run

    def second_shards():
        @pl.when(jnp.logical_not(first))
        def _():
            for m in moves[8:12]:
                send_or_keep(*m)

    def reload(k):
        gather_drain(0, k)
        save(k).wait()
        gather_d(1, k)
        wcopy(k, 1).start()

    ga, gb, gf, gc, gd = gather_a, gather_b, gather_f, gather_c, gather_d
    first_hooks = dict(
        joined=steps((gc, 0, OU), (ga, 0, SH)),
        attended=steps((gd, 0, OU)),
        mixed=steps((unpack, 0, (2, 3, 4, 5, 6)), (gf, 0, EX), (gb, 0, SH)),
        mixed2=steps((ga, 1, PR), (ga, 1, OU), (gc, 0, EX)),
        second=steps((unpack, 1, (0, 1, 2, 3, 4, 5, 6, 7))),
        second2=steps((gf, 0, SH), (gb, 1, PR), (gb, 1, OU), (gd, 0, EX)),
        upper=steps((gc, 0, SH), (second_shards,), (gd, 0, SH)),
        down=steps((gf, 1, PR), (gf, 1, OU), (ga, 1, SH)),
        down2=steps((ga, 1, EX), (gc, 1, PR)))
    second_hooks = dict(
        normed2=steps((gc, 1, OU), (gb, 1, EX), (gb, 1, SH), (reload, PR)),
        joined=steps((reload, OU)),
        mixed=steps((gf, 1, EX)),
        mixed2=steps((gc, 1, EX)),
        second=steps((gf, 1, SH)),
        second2=steps((reload, EX), (gc, 1, SH)),
        upper=steps((reload, SH)))
    a1 = forward(0, hidden0, first_hooks)
    forward(1, a1.astype(F32), second_hooks)

    for k in range(4):
        gather_drain(1, k)
    for m in moves:
        sent(*m)

    load, fin, ml, mf, ll, lf = sum0_load, sum0_fin, mid_load, mid_fin, last_load, last_fin

    def mid(l, k):
        mid_load(l, k)
        mid_fin(l, k)

    def last(l, k):
        last_load(l, k)
        last_fin(l, k)

    ig2 = backward(1, gall[own, :], dict(
        result2=steps((load, 1, SH), (fin, 1, SH)),
        upper2=steps((ml, 1, SH), (load, 1, EX), (mf, 1, SH), (fin, 1, EX)),
        middle2=steps((ll, 1, SH), (ml, 1, EX), (mf, 1, EX), (lf, 1, SH)),
        joined=steps((load, 1, PR), (fin, 1, PR)),
        joined2=steps((load, 1, OU), (ll, 1, EX), (fin, 1, OU), (lf, 1, EX))))
    g1 = (ig2.astype(F32) * livef).astype(BF)
    backward(0, g1, dict(
        grad=steps((sum2_end, 1, SH), (sum_drain, 1, SH)),
        grad2=steps((ml, 1, PR), (mf, 1, PR), (mid, 1, OU), (sum_drain, 1, EX)),
        partial=steps((load, 0, SH), (fin, 0, SH)),
        upper2=steps((ll, 1, PR), (ml, 0, SH), (lf, 1, PR), (mf, 0, SH)),
        middle=steps((load, 0, EX), (ll, 1, OU), (fin, 0, EX), (lf, 1, OU)),
        middle2=steps((sum2_end, 1, EX), (sum2_end, 1, PR)),
        project=steps((ml, 0, EX), (mf, 0, EX)),
        joined=steps((load, 0, PR), (ll, 0, SH), (fin, 0, PR), (lf, 0, SH)),
        joined2=steps((load, 0, OU), (fin, 0, OU), (last, 0, EX))))
    vec_go(0)
    mid(0, PR)
    vec_end(0)
    vec_go(1)
    mid(0, OU)
    sum2_end(0, SH)
    last(0, PR)
    vec_end(1)
    vec_go(2)
    last(0, OU)
    sum2_end(1, OU)
    sum2_end(0, EX)
    vec_end(2)
    vec_go(3)
    sum2_end(0, PR)
    sum2_end(0, OU)
    vec_end(3)
    finish_weights()
    finish_results()
    for k in range(4):
        for l in (0, 1):
            if (l, k) not in ((1, SH), (1, EX)):
                sum_drain(l, k)


def finish_kernel(act, ig, sums, fp, fo, fe, fs,
                  act_out, ig_out, o0, o1, d_pw, o7, d_ow, o2, o3, o4, d_ew, o6, d_sw, o5):
    chip = lax.axis_index("dp")
    act_out[0, :, 0] = act[...]
    ig_out[0, :, 0] = ig[...]
    for r in range(4):
        for p in range(3):
            d_pw[0, :, p * D + HW * r:p * D + HW * (r + 1)] = fp[r, :, HW * p:HW * (p + 1)].astype(F32)[:24]
        d_ow[0, :, HW * r:HW * (r + 1)] = fo[r].astype(F32)[:24]
        d_ew[0, :, D * r:D * (r + 1)] = fe[r].astype(F32)[:24]
    for j in range(2):
        d_sw[0, :, 768 * j:768 * (j + 1)] = fs[j].astype(F32)
    total = sums[0] + sums[1] + sums[2] + sums[3]
    mine = pltpu.roll(total, (D - 24 * chip) % D, 1)
    for r, o in enumerate((o0, o1, o2, o3, o4, o5)):
        o[...] = mine[r:r + 1, :24]
    units = sums[chip // 16]
    o6[...] = pltpu.roll(units, (D - 96 * (chip % 16)) % D, 1)[6:7, :96]
    cols = jnp.concatenate([sums[r, :, HW * p:HW * (p + 1)] for p in range(3) for r in range(4)], axis=1)
    o7[...] = pltpu.roll(cols, (3 * D - 72 * chip) % (3 * D), 1)[7:8, :72]


def core_call(*args):
    sd = jax.ShapeDtypeStruct
    V = pltpu.VMEM
    DMA = pltpu.SemaphoreType.DMA
    hbm = [sd((2,) + f, BF) for f in FULL]
    hbm += [sd((2, 2, HW, QW), BF), sd((2, 2, HW, HW), BF), sd((2, 2, HW, D), BF), sd((2, D, 768), BF)]
    hbm += [sd((2, 3, 4 * f[0], f[1]), BF) for f in SLAB]
    hbm += [sd((2, 3) + f, BF) for f in SLAB]
    out = pl.pallas_call(
        core_kernel,
        out_shape=[sd((2, T, D), BF), sd((2, T, D), BF), sd((4, 8, D), F32),
                   sd((4, 32, QW), BF), sd((4, 32, HW), BF), sd((4, 32, D), BF), sd((2, 96, 768), BF)] + hbm,
        in_specs=[VM] * 2 + [pl.BlockSpec(memory_space=pltpu.SMEM)] * 2 + [VM] * 14,
        out_specs=[VM] * 7 + [ANY] * 16,
        scratch_shapes=[
            V((D, QW), BF), V((HW, D), BF), V((D, D), BF), V((D, D), BF),
            V((D, QW), BF), V((HW, D), BF), V((D, D), BF), V((D, D), BF),
            V((2, TG, D), BF), V((2, TG, D), BF), V((TG, D), BF), V((TG, D), BF),
            V((2, TG, QW), BF), V((2, 3, TG, TG), F32), V((2, TG, HW), BF),
            V((2, TG, D), F32), V((2, TG, D), BF),
            V((2, T, D), F32), V((2, T, D), F32), V((2, T, 128), F32), V((2, T, 128), F32),
            V((TG, D), F32), V((3, T, D), BF), V((2, 3, T, D), BF),
            V((TG, D), BF), V((TG, QW), BF), V((TG, HW), BF), V((TG, TG), F32), V((4, 8, 128), F32),
            V((T, D), F32), V((2, T, D), BF),
            V((4, 32, QW), BF), V((4, 32, HW), BF), V((4, 32, D), BF),
            V((2, 2, 32, QW), BF), V((2, 2, 32, HW), BF), V((2, 2, 32, D), BF), V((2, 96, 768), BF),
            V((2, 48, QW), BF), V((2, 48, HW), BF), V((2, 48, D), BF),
            V((2, 96, 768), BF),
            V((768, D), BF), V((576, D), BF), V((2, 64, 8, 128), F32), V((2, 8, D), F32), V((5, 8, D), F32), V((3, 3, 8, D), F32),
            DMA((16, 2)), DMA((16, 4)), DMA((4,)), DMA((4,)), DMA((4,)), DMA((3,)), DMA((3,)),
            DMA((3, 4)), DMA((2,)), DMA((3, 2, 2)), DMA((2,)), DMA((4, 3)), DMA((4, 3)),
            DMA((2, 7)), DMA((2, 7)), DMA((2, 7)), DMA((2, 2, 7)), DMA((2, 7)), DMA((2, 7)), DMA((2, 7)),
            DMA((2, 4)), DMA((2, 4)), DMA((2, 4)), DMA((2, 4)), DMA((2, 4)), DMA((2, 4)), DMA((9,)),
            DMA((2, 4, 2)), DMA((4, 4)), DMA((4, 3)), DMA((4, 3)), DMA((6,)), DMA((6,)), pltpu.SemaphoreType.REGULAR, DMA((2, 7)), DMA((2, 4)), DMA((4,)),
        ],
        compiler_params=pltpu.CompilerParams(collective_id=1, has_side_effects=True,
                                             vmem_limit_bytes=64 * 2**20 - 2**16),
    )(*args)
    return out[:7]


def finish_call(*args):
    def sd(*shape):
        return jax.ShapeDtypeStruct(shape, F32)
    rows = jax.ShapeDtypeStruct((1, 2, 1, T, D), BF)
    row = sd(1, 24)
    return pl.pallas_call(
        finish_kernel,
        out_shape=[rows, rows, row, row, sd(1, 24, 3 * D), sd(1, 72), sd(1, 24, D), row, row, row,
                   sd(1, 24, 4 * D), sd(1, 96), sd(1, 96, D), row],
        in_specs=[VM] * 7,
        out_specs=[VM] * 14,
        compiler_params=pltpu.CompilerParams(vmem_limit_bytes=64 * 2**20 - 2**16),
    )(*args)


def rotary():
    half = 64
    rates = (np.float32(10000.0) ** (-np.arange(half, dtype=np.float32) / np.float32(half))).astype(np.float32)
    ang = np.arange(T, dtype=np.float32)[:, None] * rates[None, :]
    cos, sin = np.cos(ang), np.sin(ang)
    cos2 = np.concatenate([cos, cos], axis=1)
    sin2 = np.concatenate([-sin, sin], axis=1)
    return np.tile(cos2, (4, 1)).astype(np.float32), np.tile(sin2, (4, 1)).astype(np.float32)


def per_device(window_input, cotangent, lengths, widths, gain_first, shift_first, project_weight, project_bias,
               output_weight, output_bias, gain_second, shift_second, expand_weight, expand_bias,
               shrink_weight, shrink_bias):
    cos2, sin2 = rotary()
    parts = core_call(
        window_input[:, 0], cotangent[:, 0], lengths.reshape(2), widths, gain_first, shift_first, output_bias, gain_second,
        shift_second, shrink_bias, expand_bias, project_bias, jnp.asarray(cos2), jnp.asarray(sin2),
        project_weight, output_weight, expand_weight, shrink_weight)
    return tuple(finish_call(*parts))


def solution(mesh):
    row = P("section", "dp")
    mat = P("section", "dp", None)
    params = (row, row, mat, row, mat, row, row, row, mat, row, mat, row)
    seq = P(None, "dp", None, None)
    out = P("section", None, "dp", None, None)
    return jax.shard_map(
        per_device, mesh=mesh,
        in_specs=(seq, seq, P(None, "dp"), P()) + params,
        out_specs=(out, out) + params,
        check_vma=False,
    )
```
